32 devices in a mesh: seq: 4 (over y, x), dp: 8 (over z, core).
Axes of the slice: x: 2, y: 2, z: 4, core: 2. Of those that a mesh axis runs over, the one named last changes fastest.
Arguments:
- inputs: bfloat16 [8, 1024, 1536], P('dp', 'seq'), may hold values from -6 to 6
- block_ids: int32 [8, 1024], P('dp', 'seq'), may hold values from 0 to 7, never falling along the last dimension, each value on 1 to 256 neighbouring positions
- cotangent: bfloat16 [8, 1024, 1536], P('dp', 'seq'), may hold values from -6 to 6
- first_gain: bfloat16 [1536], P(('seq', 'dp')), may hold values from 0.5 to 1.5
- query_weight: bfloat16 [1536, 1536], P(('seq', 'dp')), may hold values from -0.15625 to 0.15625
- query_bias: bfloat16 [1536], P(('seq', 'dp')), may hold values from -3 to 3
- key_weight: bfloat16 [1536, 256], P(('seq', 'dp')), may hold values from -0.15625 to 0.15625
- key_bias: bfloat16 [256], P(('seq', 'dp')), may hold values from -3 to 3
- value_weight: bfloat16 [1536, 256], P(('seq', 'dp')), may hold values from -0.15625 to 0.15625
- value_bias: bfloat16 [256], P(('seq', 'dp')), may hold values from -3 to 3
- output_weight: bfloat16 [1536, 1536], P(('seq', 'dp')), may hold values from -1.25 to 1.25
- second_gain: bfloat16 [1536], P(('seq', 'dp')), may hold values from 0.5 to 1.5
- gate_weight: bfloat16 [1536, 8960], P('dp', 'seq'), may hold values from -0.15625 to 0.15625
- up_weight: bfloat16 [1536, 8960], P('dp', 'seq'), may hold values from -0.15625 to 0.15625
- down_weight: bfloat16 [8960, 1536], P('seq', 'dp'), may hold values from -0.375 to 0.375
Outputs:
- layer_out: bfloat16 [8, 1024, 1536], P('dp', 'seq')
- input_grad: bfloat16 [8, 1024, 1536], P('dp', 'seq')
- first_gain_grad: float32 [1536], P(('seq', 'dp'))
- query_weight_grad: float32 [1536, 1536], P(('seq', 'dp'))
- query_bias_grad: float32 [1536], P(('seq', 'dp'))
- key_weight_grad: float32 [1536, 256], P(('seq', 'dp'))
- key_bias_grad: float32 [256], P(('seq', 'dp'))
- value_weight_grad: float32 [1536, 256], P(('seq', 'dp'))
- value_bias_grad: float32 [256], P(('seq', 'dp'))
- output_weight_grad: float32 [1536, 1536], P(('seq', 'dp'))
- second_gain_grad: float32 [1536], P(('seq', 'dp'))
- gate_weight_grad: float32 [1536, 8960], P('dp', 'seq')
- up_weight_grad: float32 [1536, 8960], P('dp', 'seq')
- down_weight_grad: float32 [8960, 1536], P('seq', 'dp')
The draws below stay inside these ranges and needn't reach their ends.
Inputs may be any that keep to these rules, and one draw needn't show every extreme that they name: `block_ids`: along each sequence the block numbers start at 0, never fall and rise by one at a time; each block holds 1 to 256 tokens, one exactly 256.
All inputs are finite; a program needn't handle non-finite values.
Results may differ from the reference program's by a relative error of at most 0.028.
Values may be sent and summed in bfloat16 or wider, within the bound.
A program may use at most 256 MiB of HBM per device.

```python
import math
import jax
import jax.numpy as jnp
import numpy as np
from jax import lax

D = 1536
H = 12
KEY_VALUE_HEADS = 2
HEAD_SIZE = 128
FF = 8960
BLOCK = 256
SEQS = 8
LEN = 1024
ROWS = 512


def block_levels(own_key, extent, cuts, low, high):
    def one(dim, blocks):
        steps = jax.random.uniform(jax.random.fold_in(jax.random.fold_in(own_key, 6), dim), (blocks,), jnp.float32, low / len(cuts), high / len(cuts))
        return jnp.repeat(jnp.exp(steps), extent[dim] // blocks).reshape((-1,) + (1,) * (len(extent) - dim - 1))

    loudness = one(*cuts[0])
    for cut in cuts[1:]:
        loudness = loudness * one(*cut)
    return loudness


def split_up(number_of, total, bound, lean):
    portions = [(1 << 20) // math.isqrt(standing ** lean) + 1 for standing in range(2, number_of + 1)]
    surplus, counts = total - bound - (number_of - 1), [1] * (number_of - 1)
    while surplus > 0:
        free = [i for i in range(number_of - 1) if counts[i] < bound]
        whole, left = sum([portions[i] for i in free]), surplus
        for i in free:
            extra = min(bound - counts[i], max(1, left * portions[i] // whole), surplus)
            counts[i] = counts[i] + extra
            surplus = surplus - extra
    return np.array([bound] + counts)


def uneven(key, count, total, reach, skew):
    if count == 2:
        one = jax.random.randint(key, (), max(1, total - reach), min(reach, total - 1) + 1)
        return jnp.stack([one, total - one])
    tallies = jnp.asarray(split_up(count, total, reach, skew), jnp.int32)
    couples = (count - 1) // 2
    source_of, sink = tallies[1:1 + 2 * couples:2], tallies[2:2 + 2 * couples:2]
    room = jnp.minimum(source_of - 1, reach - sink)
    shifted = jax.random.randint(jax.random.fold_in(key, 1), (couples,), 0, 1 << 20) % (room + 1)
    tallies = tallies.at[1:1 + 2 * couples:2].set(source_of - shifted).at[2:2 + 2 * couples:2].set(sink + shifted)
    return tallies[jax.random.permutation(jax.random.fold_in(key, 2), count)]


def gaussian(stream_key, shape, scale, reach, cuts=(), kind=jnp.bfloat16):
    values = scale * jax.random.normal(stream_key, shape, jnp.float32)
    if cuts:
        values = values * block_levels(stream_key, shape, cuts, -0.22, 0.18)
    return jnp.clip(values, -reach, reach).astype(kind)


def setup_inputs(seed: int = 0) -> dict:
    keys = jax.random.split(jax.random.key(seed), 16)
    inputs = gaussian(keys[0], (SEQS, LEN, D), 1.0, 6.0, ((0, 8), (1, 4)))
    block_ids = jax.vmap(lambda own: jnp.searchsorted(jnp.cumsum(uneven(own, LEN // (BLOCK // 2), LEN, BLOCK, 1)), jnp.arange(LEN), side="right"))(jax.random.split(keys[1], SEQS)).reshape((SEQS, LEN)).astype(jnp.int32)
    cotangent = gaussian(keys[2], (SEQS, LEN, D), 1.0, 6.0, ((0, 8), (1, 4)))
    first_gain = jnp.clip(1.0 + 0.1 * jax.random.normal(keys[3], (D,), jnp.float32), 0.5, 1.5).astype(jnp.bfloat16)
    query_weight = gaussian(keys[4], (D, H * HEAD_SIZE), D ** -0.5, 0.15625, ((0, 32),))
    query_bias = gaussian(keys[5], (H * HEAD_SIZE,), 0.5, 3.0, ((0, 32),))
    key_weight = gaussian(keys[6], (D, KEY_VALUE_HEADS * HEAD_SIZE), D ** -0.5, 0.15625, ((0, 32),))
    key_bias = gaussian(keys[7], (KEY_VALUE_HEADS * HEAD_SIZE,), 0.5, 3.0, ((0, 32),))
    value_weight = gaussian(keys[8], (D, KEY_VALUE_HEADS * HEAD_SIZE), D ** -0.5, 0.15625, ((0, 32),))
    value_bias = gaussian(keys[9], (KEY_VALUE_HEADS * HEAD_SIZE,), 0.5, 3.0, ((0, 32),))
    output_weight = gaussian(keys[10], (H * HEAD_SIZE, D), (D // 64) ** -0.5, 1.25, ((0, 32),))
    second_gain = jnp.clip(1.0 + 0.1 * jax.random.normal(keys[11], (D,), jnp.float32), 0.5, 1.5).astype(jnp.bfloat16)
    gate_weight = gaussian(keys[12], (D, FF), D ** -0.5, 0.15625, ((0, 8), (1, 4)))
    up_weight = gaussian(keys[13], (D, FF), D ** -0.5, 0.15625, ((0, 8), (1, 4)))
    down_weight = gaussian(keys[14], (FF, D), (FF // 32) ** -0.5, 0.375, ((0, 4), (1, 8)))
    return dict(inputs=inputs, block_ids=block_ids, cotangent=cotangent, first_gain=first_gain, query_weight=query_weight, query_bias=query_bias, key_weight=key_weight, key_bias=key_bias, value_weight=value_weight, value_bias=value_bias, output_weight=output_weight, second_gain=second_gain, gate_weight=gate_weight, up_weight=up_weight, down_weight=down_weight)


EPS = 1e-06
THETA = 1000000.0
HIGH = lax.Precision.HIGHEST

@jax.custom_vjp
def low(v):
    return lax.optimization_barrier(v.astype(jnp.bfloat16)).astype(jnp.float32)

@jax.custom_vjp
def low_back(v):
    return v

def low_keep(v):
    return (low(v), None)

def low_pass(kept, grad):
    return (grad,)

def back_keep(v):
    return (v, None)

def back_low(kept, grad):
    return (low(grad),)
low.defvjp(low_keep, low_pass)
low_back.defvjp(back_keep, back_low)

def rope_tables(positions):
    exponent = jnp.arange(0, HEAD_SIZE, 2).astype(jnp.float32) / HEAD_SIZE
    freqs = THETA ** (-exponent)
    angles = positions.astype(jnp.float32)[:, None] * freqs[None, :]
    angles = jnp.concatenate([angles, angles], axis=-1)
    return (jnp.cos(angles), jnp.sin(angles))

def rotate(field_in, cosine, sine):
    half_width = field_in.shape[-1] // 2
    turned = jnp.concatenate([-field_in[..., half_width:], field_in[..., :half_width]], axis=-1)
    return field_in * cosine[:, None, :] + turned * sine[:, None, :]

def rms_norm(vector, norm_gain):
    factor = lax.rsqrt(lax.optimization_barrier(jnp.mean(vector * vector, axis=-1, keepdims=True)) + EPS)
    return vector * factor * norm_gain

def attend(queries, keys_all, values_all, blocks):
    group_size = H // KEY_VALUE_HEADS
    grouped = queries.reshape(LEN, KEY_VALUE_HEADS, group_size, HEAD_SIZE)
    score_scale = HEAD_SIZE ** (-0.5)

    def one_block(row_start):
        block_query = lax.dynamic_slice_in_dim(grouped, row_start, ROWS, 0)
        block_rows = lax.dynamic_slice_in_dim(blocks, row_start, ROWS, 0)
        scores = jnp.einsum('qkgd,tkd->kgqt', block_query, keys_all, precision=HIGH) * score_scale
        allowed = blocks[None, :] <= block_rows[:, None]
        scores = jnp.where(allowed[None, None], scores, -1000000000.0)
        scores = low_back(scores)
        row_peak = lax.optimization_barrier(jnp.max(scores, axis=-1, keepdims=True))
        row_exp = jnp.exp(scores - row_peak)
        probs = row_exp / lax.optimization_barrier(jnp.sum(row_exp, axis=-1, keepdims=True))
        return jnp.einsum('kgqt,tkd->qkgd', low(probs), values_all, precision=HIGH)
    starts = jnp.arange(LEN // ROWS).astype(jnp.int32) * ROWS
    pieces = lax.map(jax.checkpoint(one_block), starts)
    return pieces.reshape(LEN, H * HEAD_SIZE)

def layer(tokens, blocks, weights, cosine, sine):
    gain_one, weight_query, bias_query, key_matrix, bias_key, weight_value, bias_value, weight_out, gain_two, weight_gate, weight_up, weight_down = weights
    normed = low(rms_norm(tokens, gain_one))
    query_pre = low_back(jnp.dot(normed, weight_query, precision=HIGH) + bias_query)
    key_pre = low_back(jnp.dot(normed, key_matrix, precision=HIGH) + bias_key)
    value_pre = low_back(jnp.dot(normed, weight_value, precision=HIGH) + bias_value)
    queries = low(rotate(query_pre.reshape(LEN, H, HEAD_SIZE), cosine, sine))
    keys_all = low(rotate(key_pre.reshape(LEN, KEY_VALUE_HEADS, HEAD_SIZE), cosine, sine))
    values_all = low(value_pre.reshape(LEN, KEY_VALUE_HEADS, HEAD_SIZE))
    mixed = low(low_back(attend(queries, keys_all, values_all, blocks)))
    hidden = tokens + low_back(jnp.dot(mixed, weight_out, precision=HIGH))
    second = low(rms_norm(hidden, gain_two))
    gate_pre = low_back(jnp.dot(second, weight_gate, precision=HIGH))
    up_pre = low_back(jnp.dot(second, weight_up, precision=HIGH))
    active = low(jax.nn.silu(gate_pre) * up_pre)
    return hidden + jnp.dot(active, weight_down, precision=HIGH)

def reference(inputs, block_ids, cotangent, first_gain, query_weight, query_bias, key_weight, key_bias, value_weight, value_bias, output_weight, second_gain, gate_weight, up_weight, down_weight):
    cosine, sine = rope_tables(jnp.arange(LEN).astype(jnp.int32))
    floats = tuple((item.astype(jnp.float32) for item in (inputs, first_gain, query_weight, query_bias, key_weight, key_bias, value_weight, value_bias, output_weight, second_gain, gate_weight, up_weight, down_weight)))

    def forward(tokens, *weights):

        def one_sequence(scan_item):
            return layer(scan_item[0], scan_item[1], weights, cosine, sine)
        return lax.map(jax.checkpoint(one_sequence), (tokens, block_ids))
    result, pull = jax.vjp(forward, *floats)
    grads = pull(cotangent.astype(jnp.float32))
    return (result.astype(jnp.bfloat16), grads[0].astype(jnp.bfloat16), grads[1], grads[2], grads[3], grads[4], grads[5], grads[6], grads[7], grads[8], grads[9], grads[10], grads[11], grads[12])
```

```python
import jax
import jax.numpy as jnp
from jax import lax
from jax.sharding import PartitionSpec as P

H = 12
KEY_VALUE_HEADS = 2
HEAD_SIZE = 128
EPS = 1e-06
THETA = 1000000.0
SCALE = HEAD_SIZE ** (-0.5)
BF = jnp.bfloat16
F32 = jnp.float32


def dot(a, b, dims, out=F32):
    return lax.dot_general(a, b, (dims, ((), ())), preferred_element_type=F32).astype(out)


def nn(a, b, out=F32):
    return dot(a, b, ((1,), (0,)), out)


def nt(a, b, out=F32):
    return dot(a, b, ((1,), (1,)), out)


def tn(a, b, out=F32):
    return dot(a, b, ((0,), (0,)), out)


def rope_tables(positions):
    exponent = jnp.arange(0, HEAD_SIZE, 2).astype(F32) / HEAD_SIZE
    freqs = THETA ** (-exponent)
    angles = positions.astype(F32)[:, None] * freqs[None, :]
    angles = jnp.concatenate([angles, angles], axis=-1)
    return jnp.cos(angles), jnp.sin(angles)


def turn(u):
    half = u.shape[-1] // 2
    return jnp.concatenate([-u[..., half:], u[..., :half]], axis=-1)


def turn_back(w):
    half = w.shape[-1] // 2
    return jnp.concatenate([w[..., half:], -w[..., :half]], axis=-1)


def swap_seq(value, k):
    size = lax.axis_size("seq")
    return lax.ppermute(value, "seq", [(i, i ^ k) for i in range(size)])


def gather_seq(value):
    half = value.shape[0] // 2
    one = swap_seq(value, 1)
    two = swap_seq(value, 2)
    far = jnp.concatenate([swap_seq(two[:half], 1), swap_seq(one[half:], 2)], axis=0)
    return [value, one, two, far]


def scatter_seq(parts):
    low = [part.astype(BF) for part in parts[1:]]
    half = low[0].shape[0] // 2
    from_one = swap_seq(low[2][:half], 1)
    from_two = swap_seq(low[2][half:], 2)
    wide = [part.astype(F32) for part in parts]
    to_one = jnp.concatenate([wide[1][:half], wide[1][half:] + from_two.astype(F32)], axis=0).astype(BF)
    to_two = jnp.concatenate([wide[2][:half] + from_one.astype(F32), wide[2][half:]], axis=0).astype(BF)
    return wide[0] + swap_seq(to_one, 1).astype(F32) + swap_seq(to_two, 2).astype(F32)


def by_index(slots, index):
    stacked = jnp.stack(slots)
    return [
        lax.dynamic_index_in_dim(stacked, index ^ i, 0, keepdims=False) for i in range(len(slots))
    ]


def swap_core(value):
    size = lax.axis_size("dp")
    return lax.ppermute(value, "dp", [(i, i ^ 1) for i in range(size)])


def ring_gather(value):
    size = lax.axis_size("dp")
    chips = size // 2
    index = lax.axis_index("dp")
    chip, core = index // 2, index % 2
    blocks = [value]
    for _ in range(chips - 1):
        blocks.append(
            lax.ppermute(blocks[-1], "dp", [(i, (i - 2) % size) for i in range(size)])
        )
    own = jnp.stack(blocks)
    other = swap_core(own)
    both = jnp.where(core == 0, jnp.stack([own, other], 1), jnp.stack([other, own], 1))
    return lax.dynamic_slice_in_dim(jnp.concatenate([both, both], 0), chips - chip, chips, 0)


def ring_scatter(terms):
    size = lax.axis_size("dp")
    chips = size // 2
    index = lax.axis_index("dp")
    chip, core = index // 2, index % 2
    give = lax.dynamic_index_in_dim(terms, 1 - core, 1, keepdims=False)
    keep = lax.dynamic_index_in_dim(terms, core, 1, keepdims=False)
    got = swap_core(give)

    def term(which):
        pick = lambda field: lax.dynamic_index_in_dim(field, which, 0, keepdims=False).astype(F32)
        return pick(keep) + pick(got)

    came = None
    for step in range(chips - 1):
        send = term((chip + chips - 1 - step) % chips)
        if came is not None:
            send = send + came.astype(F32)
        came = lax.ppermute(send.astype(BF), "dp", [(i, (i + 2) % size) for i in range(size)])
    total = term(chip)
    return total if came is None else total + came.astype(F32)


def shards(
    inputs,
    block_ids,
    cotangent,
    first_gain,
    query_weight,
    query_bias,
    key_weight,
    key_bias,
    value_weight,
    value_bias,
    output_weight,
    second_gain,
    gate_weight,
    up_weight,
    down_weight,
):
    seqs = lax.axis_size("seq")
    seq = lax.axis_index("seq")
    dps = lax.axis_size("dp")
    dpi = lax.axis_index("dp")
    chips, chip, core = dps // 2, dpi // 2, dpi % 2
    heads = H // seqs
    copies = seqs // KEY_VALUE_HEADS
    wq = heads * HEAD_SIZE
    wide = wq + 2 * HEAD_SIZE
    tokens_here, model = inputs.shape[1:]
    share = first_gain.shape[0]
    kv_share = key_bias.shape[0]
    hidden_units = gate_weight.shape[1]

    small = jnp.concatenate([first_gain, second_gain, query_bias, key_bias, value_bias])
    small = jnp.concatenate(by_index([v[0] for v in gather_seq_small(small[None])], seq))
    packed = jnp.concatenate(
        [
            query_weight.reshape(share, seqs, wq),
            jnp.repeat(key_weight.reshape(share, KEY_VALUE_HEADS, HEAD_SIZE), copies, axis=1),
            jnp.repeat(value_weight.reshape(share, KEY_VALUE_HEADS, HEAD_SIZE), copies, axis=1),
        ],
        axis=-1,
    )
    rows = [
        lax.dynamic_index_in_dim(packed, seq ^ k, 1, keepdims=False) for k in range(seqs)
    ]
    rows = by_index([rows[0]] + [swap_seq(rows[k], k) for k in range(1, seqs)], seq)
    small_row = jnp.zeros((1, -(-small.shape[0] // wide) * wide), BF).at[0, : small.shape[0]].set(small)
    small_rows = small_row.reshape(-1, wide)
    extra = jnp.zeros((16, wide), BF).at[: small_rows.shape[0]].set(small_rows)
    qkv_pack = ring_gather(jnp.concatenate(rows + [extra], axis=0))
    out_head = ring_gather(output_weight).reshape(dps * share, model)
    weight_qkv = (
        qkv_pack[:, :, : seqs * share]
        .reshape(chips, 2, seqs, share, wide)
        .transpose(2, 0, 1, 3, 4)
        .reshape(model, wide)
    )
    smalls = qkv_pack[:, :, seqs * share : seqs * share + small_rows.shape[0]]
    smalls = smalls.reshape(dps, -1)[:, : small.shape[0]].reshape(dps, seqs, -1)
    smalls = smalls.transpose(1, 0, 2).astype(F32)
    gain_first = smalls[:, :, :share].reshape(model)
    gain_second = smalls[:, :, share : 2 * share].reshape(model)
    bias_q = lax.dynamic_index_in_dim(smalls, seq, 0, keepdims=False)[:, 2 * share : 3 * share].reshape(wq)
    group = seq // copies
    bias_k = smalls[:, :, 3 * share : 3 * share + kv_share].reshape(KEY_VALUE_HEADS, HEAD_SIZE)
    bias_v = smalls[:, :, 3 * share + kv_share :].reshape(KEY_VALUE_HEADS, HEAD_SIZE)
    bias = jnp.concatenate(
        [
            bias_q,
            lax.dynamic_index_in_dim(bias_k, group, 0, keepdims=False),
            lax.dynamic_index_in_dim(bias_v, group, 0, keepdims=False),
        ]
    )

    tokens = jnp.concatenate(gather_seq(inputs[0]), axis=0).astype(F32)
    blocks = jnp.concatenate(
        [block_ids[0]] + [swap_seq(block_ids[0], k) for k in range(1, seqs)], axis=0
    )
    positions = jnp.concatenate(
        [(seq ^ k) * tokens_here + jnp.arange(tokens_here, dtype=jnp.int32) for k in range(seqs)]
    )
    length = tokens.shape[0]
    cosine, sine = rope_tables(positions)

    half_rows = out_head.shape[0] // 2
    mine = jnp.stack(gather_seq(lax.dynamic_slice_in_dim(out_head, core * half_rows, half_rows, 0)))
    theirs = swap_core(mine)
    weight_out = jnp.where(
        core == 0, jnp.stack([mine, theirs], 1), jnp.stack([theirs, mine], 1)
    ).reshape(model, model)

    down_turned = down_weight.T
    whole_gate, whole_up, whole_down = (
        lax.all_gather(field, "dp", axis=0, tiled=True)
        for field in (gate_weight, up_weight, down_turned)
    )

    first_factor = lax.rsqrt(jnp.mean(tokens * tokens, axis=-1, keepdims=True) + EPS)
    normed = (tokens * first_factor * gain_first).astype(BF)
    pre = nn(normed, weight_qkv) + bias
    rotating = pre[:, : wq + HEAD_SIZE].reshape(length, heads + 1, HEAD_SIZE)
    rotated = (rotating * cosine[:, None] + turn(rotating) * sine[:, None]).astype(BF)
    queries, keys = rotated[:, :heads], rotated[:, heads]
    values = pre[:, wq + HEAD_SIZE :].astype(BF)
    allowed = blocks[None, :] <= blocks[:, None]

    scores = jnp.einsum("rhd,td->hrt", queries, keys, preferred_element_type=F32) * SCALE
    scores = jnp.where(allowed[None], scores, -1000000000.0)
    peak = jnp.max(scores, axis=-1, keepdims=True)
    raised = jnp.exp(scores - peak)
    total = jnp.sum(raised, axis=-1, keepdims=True)
    probs_low = (raised / total).astype(BF)
    logsum = peak + jnp.log(total)
    mixed = jnp.einsum("hrt,td->rhd", probs_low, values, preferred_element_type=F32).astype(BF)
    mixed = mixed.reshape(length, wq)
    all_mixed = []
    for k, field in enumerate(gather_seq(mixed)):
        split = field.reshape(seqs, tokens_here, wq)
        all_mixed.append(jnp.stack([split[i ^ k] for i in range(seqs)]).reshape(length, wq))
    hidden = tokens + nn(jnp.concatenate(all_mixed, axis=1), weight_out)

    incoming = jnp.concatenate(gather_seq(cotangent[0]), axis=0)
    second_factor = lax.rsqrt(jnp.mean(hidden * hidden, axis=-1, keepdims=True) + EPS)
    second = (hidden * second_factor * gain_second).astype(BF)
    gate = nn(second, whole_gate)
    up = nn(second, whole_up)
    back = nn(incoming, whole_down)
    sigma = jax.nn.sigmoid(gate)
    silu = gate * sigma
    active = (silu * up).astype(BF)
    grad_gate = (back * up * sigma * (1.0 + gate * (1.0 - sigma))).astype(BF)
    grad_up = (back * silu).astype(BF)
    second_sum = nt(grad_gate, whole_gate) + nt(grad_up, whole_up)
    out_sum = nt(active, whole_down)
    down_grad, gate_grad, up_grad = (
        lax.psum_scatter(tn(left, right, BF), "dp", scatter_dimension=0, tiled=True).astype(F32)
        for left, right in ((incoming, active), (second, grad_gate), (second, grad_up))
    )
    split = lambda field: [field[k * tokens_here : (k + 1) * tokens_here] for k in range(seqs)]
    grad_second = scatter_seq(split(second_sum))
    layer_out = (hidden[:tokens_here] + scatter_seq(split(out_sum))).astype(BF)

    gain_two_grad = jnp.sum(second_sum * (hidden * second_factor), axis=0)
    unit = hidden[:tokens_here] * second_factor[:tokens_here]
    scaled = grad_second * gain_second
    grad_hidden = cotangent[0].astype(F32) + second_factor[:tokens_here] * (
        scaled - unit * jnp.mean(scaled * unit, axis=-1, keepdims=True)
    )
    branch = jnp.concatenate(gather_seq(grad_hidden.astype(BF)), axis=0)
    out_weight_grad = tn(mixed, branch, BF)
    grad_mixed = nt(branch, out_head, BF).reshape(length, heads, HEAD_SIZE)

    probs = jnp.exp(scores - logsum)
    grad_probs = jnp.einsum("rhd,td->hrt", grad_mixed, values, preferred_element_type=F32)
    delta = jnp.sum(probs * grad_probs, axis=-1, keepdims=True)
    grad_scores = (probs * (grad_probs - delta)).astype(BF)
    grad_queries = jnp.einsum("hrt,td->rhd", grad_scores, keys, preferred_element_type=F32) * SCALE
    grad_keys = jnp.einsum("hrt,rhd->td", grad_scores, queries, preferred_element_type=F32) * SCALE
    grad_values = jnp.einsum(
        "hrt,rhd->td", probs.astype(BF), grad_mixed, preferred_element_type=F32
    )
    grad_rotated = jnp.concatenate([grad_queries, grad_keys[:, None]], axis=1)
    grad_rotating = grad_rotated * cosine[:, None] + turn_back(grad_rotated * sine[:, None])
    grad_pre = jnp.concatenate(
        [grad_rotating.reshape(length, wq + HEAD_SIZE), grad_values], axis=1
    ).astype(BF)
    grad_normed = nt(grad_pre, weight_qkv)
    unit = tokens * first_factor
    gain_one_grad = jnp.sum(grad_normed * unit, axis=0)
    grad_normed = scatter_seq(split(grad_normed))
    unit = unit[:tokens_here]
    scaled = grad_normed * gain_first
    input_grad = grad_hidden + first_factor[:tokens_here] * (
        scaled - unit * jnp.mean(scaled * unit, axis=-1, keepdims=True)
    )
    input_grad = input_grad.astype(BF)

    bias_grad = jnp.sum(grad_pre.astype(F32), axis=0)
    place = lambda field, count, at: jnp.where(
        (jnp.arange(count) == at)[:, None], field[None], 0.0
    ).reshape(seqs, dps, -1)
    small_grad = jnp.concatenate(
        [
            gain_one_grad.reshape(seqs, dps, share),
            gain_two_grad.reshape(seqs, dps, share),
            place(bias_grad[:wq], seqs, seq),
            place(bias_grad[wq : wq + HEAD_SIZE], KEY_VALUE_HEADS, group),
            place(bias_grad[wq + HEAD_SIZE :], KEY_VALUE_HEADS, group),
        ],
        axis=-1,
    )
    one = small_grad.shape[-1]
    small_grad = small_grad.transpose(1, 0, 2).reshape(dps, seqs * one).astype(BF)
    small_grad = jnp.pad(small_grad, ((0, 0), (0, small_rows.size - seqs * one)))
    small_grad = jnp.pad(
        small_grad.reshape(dps, -1, wide), ((0, 0), (0, 16 - small_rows.shape[0]), (0, 0))
    )
    qkv_grad = tn(normed, grad_pre, BF).reshape(seqs, dps, share, wide)
    qkv_grad = qkv_grad.transpose(1, 0, 2, 3).reshape(dps, seqs * share, wide)
    qkv_grad = ring_scatter(
        jnp.concatenate([qkv_grad, small_grad], axis=1).reshape(chips, 2, -1, wide)
    ).astype(BF)
    out_weight_grad = ring_scatter(out_weight_grad.reshape(chips, 2, share, model))
    smalls = qkv_grad[seqs * share : seqs * share + small_rows.shape[0]]
    smalls = smalls.reshape(-1)[: seqs * one].reshape(seqs, 1, one)
    smalls = jnp.pad(smalls, ((0, 0), (0, 15), (0, wide - one)))
    qkv_grad = qkv_grad[: seqs * share].reshape(seqs, share, wide)
    qkv_grad = jnp.concatenate([qkv_grad, smalls], axis=1)
    parts = [lax.dynamic_index_in_dim(qkv_grad, seq ^ k, 0, keepdims=False) for k in range(seqs)]
    parts = by_index([parts[0]] + [swap_seq(parts[k], k) for k in range(1, seqs)], seq)
    query_weight_grad = jnp.concatenate([part[:share, :wq] for part in parts], axis=1).astype(F32)
    pairs = [
        sum(part[:share, wq:].astype(F32) for part in parts[g * copies : (g + 1) * copies])
        for g in range(KEY_VALUE_HEADS)
    ]
    key_weight_grad = jnp.concatenate([pair[:, :HEAD_SIZE] for pair in pairs], axis=1)
    value_weight_grad = jnp.concatenate([pair[:, HEAD_SIZE:] for pair in pairs], axis=1)
    small_sum = sum(part[share, :one].astype(F32) for part in parts)
    gain_one_grad, gain_two_grad, query_bias_grad, key_bias_grad, value_bias_grad = jnp.split(
        small_sum, [share, 2 * share, 3 * share, 3 * share + kv_share]
    )

    return (
        layer_out[None],
        input_grad[None],
        gain_one_grad,
        query_weight_grad,
        query_bias_grad,
        key_weight_grad,
        key_bias_grad,
        value_weight_grad,
        value_bias_grad,
        out_weight_grad,
        gain_two_grad,
        gate_grad,
        up_grad,
        down_grad.T,
    )


def gather_seq_small(value):
    size = lax.axis_size("seq")
    return [value] + [swap_seq(value, k) for k in range(1, size)]


def solution(mesh):
    tokens = P("dp", "seq", None)
    whole = P(("seq", "dp"))
    matrix = P(("seq", "dp"), None)
    feed = P("dp", "seq")
    in_specs = (
        tokens,
        P("dp", "seq"),
        tokens,
        whole,
        matrix,
        whole,
        matrix,
        whole,
        matrix,
        whole,
        matrix,
        whole,
        feed,
        feed,
        P("seq", "dp"),
    )
    out_specs = (
        tokens,
        tokens,
        whole,
        matrix,
        whole,
        matrix,
        whole,
        matrix,
        whole,
        matrix,
        whole,
        feed,
        feed,
        P("seq", "dp"),
    )
    return jax.shard_map(shards, mesh=mesh, in_specs=in_specs, out_specs=out_specs, check_vma=False)
```

```python
import jax
import jax.numpy as jnp
from jax import lax
from jax.experimental import pallas as pl
from jax.experimental.pallas import tpu as pltpu
from jax.sharding import PartitionSpec as P

H = 12
KEY_VALUE_HEADS = 2
HEAD_SIZE = 128
EPS = 1e-06
THETA = 1000000.0
SCALE = HEAD_SIZE ** (-0.5)
BF = jnp.bfloat16
F32 = jnp.float32


def dot(a, b, dims, out=F32):
    return lax.dot_general(a, b, (dims, ((), ())), preferred_element_type=F32).astype(out)


def nn(a, b, out=F32):
    return dot(a, b, ((1,), (0,)), out)


def nt(a, b, out=F32):
    return dot(a, b, ((1,), (1,)), out)


def tn(a, b, out=F32):
    return dot(a, b, ((0,), (0,)), out)


def rope_tables(positions):
    exponent = jnp.arange(0, HEAD_SIZE, 2).astype(F32) / HEAD_SIZE
    freqs = THETA ** (-exponent)
    angles = positions.astype(F32)[:, None] * freqs[None, :]
    angles = jnp.concatenate([angles, angles], axis=-1)
    return jnp.cos(angles), jnp.sin(angles)


def turn(u):
    half = u.shape[-1] // 2
    return jnp.concatenate([-u[..., half:], u[..., :half]], axis=-1)


def turn_back(w):
    half = w.shape[-1] // 2
    return jnp.concatenate([w[..., half:], -w[..., :half]], axis=-1)


def swap_seq(value, k):
    size = lax.axis_size("seq")
    return lax.ppermute(value, "seq", [(i, i ^ k) for i in range(size)])


def gather_seq(value):
    half = value.shape[0] // 2
    one = swap_seq(value, 1)
    two = swap_seq(value, 2)
    far = jnp.concatenate([swap_seq(two[:half], 1), swap_seq(one[half:], 2)], axis=0)
    return [value, one, two, far]


def scatter_seq(parts):
    low = [part.astype(BF) for part in parts[1:]]
    half = low[0].shape[0] // 2
    from_one = swap_seq(low[2][:half], 1)
    from_two = swap_seq(low[2][half:], 2)
    wide = [part.astype(F32) for part in parts]
    to_one = jnp.concatenate([wide[1][:half], wide[1][half:] + from_two.astype(F32)], axis=0).astype(BF)
    to_two = jnp.concatenate([wide[2][:half] + from_one.astype(F32), wide[2][half:]], axis=0).astype(BF)
    return wide[0] + swap_seq(to_one, 1).astype(F32) + swap_seq(to_two, 2).astype(F32)


def by_index(slots, index):
    stacked = jnp.stack(slots)
    return [
        lax.dynamic_index_in_dim(stacked, index ^ i, 0, keepdims=False) for i in range(len(slots))
    ]


def swap_core(value):
    size = lax.axis_size("dp")
    return lax.ppermute(value, "dp", [(i, i ^ 1) for i in range(size)])


def start_kernel(
    x_in, ids_in, small_in, pack_in, out_in,
    x_out, ids_out, small_out, pack_out, out_out,
    local_sem, seq_send, seq_recv, far_send, far_recv, ring_send, ring_recv, core_send, core_recv,
):
    seqs, dps = lax.axis_size("seq"), lax.axis_size("dp")
    chips = dps // 2
    seq, dpi = lax.axis_index("seq"), lax.axis_index("dp")
    chip, core = dpi // 2, dpi % 2
    ahead = ((chip + chips - 1) % chips) * 2 + core
    behind = ((chip + 1) % chips) * 2 + core
    sibling = chip * 2 + 1 - core

    barrier = pltpu.get_barrier_semaphore()
    for k in range(1, seqs):
        pl.semaphore_signal(barrier, inc=1, device_id=(seq ^ k, dpi), device_id_type=pl.DeviceIdType.MESH)
    for other in (ahead, behind, sibling):
        pl.semaphore_signal(barrier, inc=1, device_id=(seq, other), device_id_type=pl.DeviceIdType.MESH)
    pl.semaphore_wait(barrier, seqs + 2)

    rows = x_in.shape[0]
    half = rows // 2

    def remote(src, dst, send, recv, where):
        return pltpu.make_async_remote_copy(
            src_ref=src, dst_ref=dst, send_sem=send, recv_sem=recv,
            device_id=where, device_id_type=pl.DeviceIdType.MESH,
        )

    small_sends = [
        remote(small_in, small_out.at[dpi, seq], seq_send.at[0, k], seq_recv.at[0, k], (seq ^ k, dpi))
        for k in range(1, seqs)
    ]
    pack_sends = [
        remote(
            pack_in.at[seq ^ k], pack_out.at[seq, dpi], seq_send.at[1, k], seq_recv.at[1, k], (seq ^ k, dpi)
        )
        for k in range(1, seqs)
    ]
    id_sends = [
        remote(ids_in, ids_out.at[k], seq_send.at[2, k], seq_recv.at[2, k], (seq ^ k, dpi))
        for k in range(1, seqs)
    ]
    x_sends = [
        remote(x_in, x_out.at[pl.ds(k * rows, rows)], seq_send.at[3, k], seq_recv.at[3, k], (seq ^ k, dpi))
        for k in (1, 2)
    ]
    locals_ = [
        pltpu.make_async_copy(small_in, small_out.at[dpi, seq], local_sem.at[0]),
        pltpu.make_async_copy(pack_in.at[seq], pack_out.at[seq, dpi], local_sem.at[1]),
        pltpu.make_async_copy(out_in, out_out.at[dpi], local_sem.at[2]),
        pltpu.make_async_copy(ids_in, ids_out.at[0], local_sem.at[3]),
        pltpu.make_async_copy(x_in, x_out.at[pl.ds(0, rows)], local_sem.at[4]),
    ]
    for copy in small_sends + pack_sends + locals_[:3] + id_sends + x_sends + locals_[3:]:
        copy.start()
    for copy in locals_[:3] + small_sends + pack_sends:
        copy.wait()

    far_sends = [
        remote(
            x_out.at[pl.ds(2 * rows, half)], x_out.at[pl.ds(3 * rows, half)],
            far_send.at[0], far_recv.at[0], (seq ^ 1, dpi),
        ),
        remote(
            x_out.at[pl.ds(rows + half, half)], x_out.at[pl.ds(3 * rows + half, half)],
            far_send.at[1], far_recv.at[1], (seq ^ 2, dpi),
        ),
    ]

    def hop_sends(hop, to_core):
        block = ((chip + hop) % chips) * 2 + core
        send, recv = (core_send, core_recv) if to_core else (ring_send, ring_recv)
        where = (seq, sibling) if to_core else (seq, ahead)
        return [
            remote(field, field, send.at[i, hop], recv.at[i, hop], where)
            for i, field in enumerate((small_out.at[block], pack_out.at[:, block], out_out.at[block]))
        ]

    flying = []
    for hop in range(chips):
        if hop > 0:
            for copy in rings:
                copy.wait_recv()
            flying += rings
        rings = hop_sends(hop, False) if hop < chips - 1 else []
        cores = hop_sends(hop, True)
        for copy in rings + cores:
            copy.start()
        flying += cores
        if hop == 0:
            for copy in x_sends:
                copy.wait()
            for copy in far_sends:
                copy.start()
    for copy in flying:
        copy.wait_send()
    for hop in range(chips):
        for copy in hop_sends(hop, True):
            copy.wait_recv()
    for copy in far_sends + id_sends + locals_[3:]:
        copy.wait()


def start_call(x, ids, small, pack, out):
    seqs, dps = lax.axis_size("seq"), lax.axis_size("dp")
    chips = dps // 2
    share, wide = pack.shape[1:]
    any_space = pl.BlockSpec(memory_space=pl.ANY)
    shapes = (
        jax.ShapeDtypeStruct((seqs * x.shape[0], x.shape[1]), x.dtype),
        jax.ShapeDtypeStruct((seqs,) + ids.shape, ids.dtype),
        jax.ShapeDtypeStruct((dps, seqs) + small.shape, small.dtype),
        jax.ShapeDtypeStruct((seqs, dps, share, wide), pack.dtype),
        jax.ShapeDtypeStruct((dps,) + out.shape, out.dtype),
    )
    dma = pltpu.SemaphoreType.DMA
    return pl.pallas_call(
        start_kernel,
        out_shape=shapes,
        in_specs=[any_space] * 5,
        out_specs=(any_space,) * 5,
        scratch_shapes=[
            dma((5,)), dma((4, seqs)), dma((4, seqs)), dma((2,)), dma((2,)),
            dma((3, chips)), dma((3, chips)), dma((3, chips)), dma((3, chips)),
        ],
        compiler_params=pltpu.CompilerParams(collective_id=0, has_side_effects=True),
        name="start_gather",
    )(x, ids, small, pack, out)


def ring_scatter(terms):
    size = lax.axis_size("dp")
    chips = size // 2
    index = lax.axis_index("dp")
    chip, core = index // 2, index % 2
    give = lax.dynamic_index_in_dim(terms, 1 - core, 1, keepdims=False)
    keep = lax.dynamic_index_in_dim(terms, core, 1, keepdims=False)
    got = swap_core(give)

    def term(which):
        pick = lambda field: lax.dynamic_index_in_dim(field, which, 0, keepdims=False).astype(F32)
        return pick(keep) + pick(got)

    came = None
    for step in range(chips - 1):
        send = term((chip + chips - 1 - step) % chips)
        if came is not None:
            send = send + came.astype(F32)
        came = lax.ppermute(send.astype(BF), "dp", [(i, (i + 2) % size) for i in range(size)])
    total = term(chip)
    return total if came is None else total + came.astype(F32)


def shards(
    inputs,
    block_ids,
    cotangent,
    first_gain,
    query_weight,
    query_bias,
    key_weight,
    key_bias,
    value_weight,
    value_bias,
    output_weight,
    second_gain,
    gate_weight,
    up_weight,
    down_weight,
):
    seqs = lax.axis_size("seq")
    seq = lax.axis_index("seq")
    dps = lax.axis_size("dp")
    dpi = lax.axis_index("dp")
    chips, chip, core = dps // 2, dpi // 2, dpi % 2
    heads = H // seqs
    copies = seqs // KEY_VALUE_HEADS
    wq = heads * HEAD_SIZE
    wide = wq + 2 * HEAD_SIZE
    tokens_here, model = inputs.shape[1:]
    share = first_gain.shape[0]
    kv_share = key_bias.shape[0]
    hidden_units = gate_weight.shape[1]

    small = jnp.concatenate([first_gain, second_gain, query_bias, key_bias, value_bias])
    packed = jnp.concatenate(
        [
            query_weight.reshape(share, seqs, wq),
            jnp.repeat(key_weight.reshape(share, KEY_VALUE_HEADS, HEAD_SIZE), copies, axis=1),
            jnp.repeat(value_weight.reshape(share, KEY_VALUE_HEADS, HEAD_SIZE), copies, axis=1),
        ],
        axis=-1,
    ).transpose(1, 0, 2)
    one = small.shape[0]
    small = jnp.pad(small[None], ((0, 15), (0, -one % 128)))
    tokens, blocks, smalls, weight_qkv, out_head = start_call(
        inputs[0], block_ids.reshape(-1, 128), small, packed, output_weight
    )
    tokens = tokens.astype(F32)
    blocks = blocks.reshape(-1)
    weight_qkv = weight_qkv.reshape(model, wide)
    out_head = out_head.reshape(dps * share, model)
    smalls = smalls[:, :, 0, :one].transpose(1, 0, 2).astype(F32)
    gain_first = smalls[:, :, :share].reshape(model)
    gain_second = smalls[:, :, share : 2 * share].reshape(model)
    bias_q = lax.dynamic_index_in_dim(smalls, seq, 0, keepdims=False)[:, 2 * share : 3 * share].reshape(wq)
    group = seq // copies
    bias_k = smalls[:, :, 3 * share : 3 * share + kv_share].reshape(KEY_VALUE_HEADS, HEAD_SIZE)
    bias_v = smalls[:, :, 3 * share + kv_share :].reshape(KEY_VALUE_HEADS, HEAD_SIZE)
    bias = jnp.concatenate(
        [
            bias_q,
            lax.dynamic_index_in_dim(bias_k, group, 0, keepdims=False),
            lax.dynamic_index_in_dim(bias_v, group, 0, keepdims=False),
        ]
    )
    positions = jnp.concatenate(
        [(seq ^ k) * tokens_here + jnp.arange(tokens_here, dtype=jnp.int32) for k in range(seqs)]
    )
    length = tokens.shape[0]
    cosine, sine = rope_tables(positions)

    half_rows = out_head.shape[0] // 2
    mine = jnp.stack(gather_seq(lax.dynamic_slice_in_dim(out_head, core * half_rows, half_rows, 0)))
    theirs = swap_core(mine)
    weight_out = jnp.where(
        core == 0, jnp.stack([mine, theirs], 1), jnp.stack([theirs, mine], 1)
    ).reshape(model, model)

    down_turned = down_weight.T
    whole_gate, whole_up, whole_down = (
        lax.all_gather(field, "dp", axis=0, tiled=True)
        for field in (gate_weight, up_weight, down_turned)
    )

    first_factor = lax.rsqrt(jnp.mean(tokens * tokens, axis=-1, keepdims=True) + EPS)
    normed = (tokens * first_factor * gain_first).astype(BF)
    pre = nn(normed, weight_qkv) + bias
    rotating = pre[:, : wq + HEAD_SIZE].reshape(length, heads + 1, HEAD_SIZE)
    rotated = (rotating * cosine[:, None] + turn(rotating) * sine[:, None]).astype(BF)
    queries, keys = rotated[:, :heads], rotated[:, heads]
    values = pre[:, wq + HEAD_SIZE :].astype(BF)
    allowed = blocks[None, :] <= blocks[:, None]

    scores = jnp.einsum("rhd,td->hrt", queries, keys, preferred_element_type=F32) * SCALE
    scores = jnp.where(allowed[None], scores, -1000000000.0)
    peak = jnp.max(scores, axis=-1, keepdims=True)
    raised = jnp.exp(scores - peak)
    total = jnp.sum(raised, axis=-1, keepdims=True)
    probs_low = (raised / total).astype(BF)
    logsum = peak + jnp.log(total)
    mixed = jnp.einsum("hrt,td->rhd", probs_low, values, preferred_element_type=F32).astype(BF)
    mixed = mixed.reshape(length, wq)
    all_mixed = []
    for k, field in enumerate(gather_seq(mixed)):
        split = field.reshape(seqs, tokens_here, wq)
        all_mixed.append(jnp.stack([split[i ^ k] for i in range(seqs)]).reshape(length, wq))
    hidden = tokens + nn(jnp.concatenate(all_mixed, axis=1), weight_out)

    incoming = jnp.concatenate(gather_seq(lax.optimization_barrier((cotangent, tokens))[0][0]), axis=0)
    second_factor = lax.rsqrt(jnp.mean(hidden * hidden, axis=-1, keepdims=True) + EPS)
    second = (hidden * second_factor * gain_second).astype(BF)
    gate = nn(second, whole_gate)
    up = nn(second, whole_up)
    sigma = jax.nn.sigmoid(gate)
    silu = gate * sigma
    active = (silu * up).astype(BF)
    scatter = lambda field: lax.psum_scatter(field, "dp", scatter_dimension=0, tiled=True)
    down_grad = scatter(tn(incoming, active, BF)).astype(F32)
    back = nn(incoming, whole_down)
    grad_gate = (back * up * sigma * (1.0 + gate * (1.0 - sigma))).astype(BF)
    grad_up = (back * silu).astype(BF)
    second_sum = nt(grad_gate, whole_gate) + nt(grad_up, whole_up)
    out_sum = nt(active, whole_down)
    gate_grad = scatter(tn(second, grad_gate, BF)).astype(F32)
    up_grad = scatter(tn(second, grad_up, BF)).astype(F32)
    split = lambda field: [field[k * tokens_here : (k + 1) * tokens_here] for k in range(seqs)]
    grad_second = scatter_seq(split(second_sum))
    layer_out = (hidden[:tokens_here] + scatter_seq(split(out_sum))).astype(BF)

    gain_two_grad = jnp.sum(second_sum * (hidden * second_factor), axis=0)
    unit = hidden[:tokens_here] * second_factor[:tokens_here]
    scaled = grad_second * gain_second
    grad_hidden = cotangent[0].astype(F32) + second_factor[:tokens_here] * (
        scaled - unit * jnp.mean(scaled * unit, axis=-1, keepdims=True)
    )
    branch = jnp.concatenate(gather_seq(grad_hidden.astype(BF)), axis=0)
    out_weight_grad = tn(mixed, branch, BF)
    grad_mixed = nt(branch, out_head, BF).reshape(length, heads, HEAD_SIZE)

    probs = jnp.exp(scores - logsum)
    grad_probs = jnp.einsum("rhd,td->hrt", grad_mixed, values, preferred_element_type=F32)
    delta = jnp.sum(probs * grad_probs, axis=-1, keepdims=True)
    grad_scores = (probs * (grad_probs - delta)).astype(BF)
    grad_queries = jnp.einsum("hrt,td->rhd", grad_scores, keys, preferred_element_type=F32) * SCALE
    grad_keys = jnp.einsum("hrt,rhd->td", grad_scores, queries, preferred_element_type=F32) * SCALE
    grad_values = jnp.einsum(
        "hrt,rhd->td", probs.astype(BF), grad_mixed, preferred_element_type=F32
    )
    grad_rotated = jnp.concatenate([grad_queries, grad_keys[:, None]], axis=1)
    grad_rotating = grad_rotated * cosine[:, None] + turn_back(grad_rotated * sine[:, None])
    grad_pre = jnp.concatenate(
        [grad_rotating.reshape(length, wq + HEAD_SIZE), grad_values], axis=1
    ).astype(BF)
    grad_normed = nt(grad_pre, weight_qkv)
    unit = tokens * first_factor
    gain_one_grad = jnp.sum(grad_normed * unit, axis=0)
    grad_normed = scatter_seq(split(grad_normed))
    unit = unit[:tokens_here]
    scaled = grad_normed * gain_first
    input_grad = grad_hidden + first_factor[:tokens_here] * (
        scaled - unit * jnp.mean(scaled * unit, axis=-1, keepdims=True)
    )
    input_grad = input_grad.astype(BF)

    bias_grad = jnp.sum(grad_pre.astype(F32), axis=0)
    place = lambda field, count, at: jnp.where(
        (jnp.arange(count) == at)[:, None], field[None], 0.0
    ).reshape(seqs, dps, -1)
    small_grad = jnp.concatenate(
        [
            gain_one_grad.reshape(seqs, dps, share),
            gain_two_grad.reshape(seqs, dps, share),
            place(bias_grad[:wq], seqs, seq),
            place(bias_grad[wq : wq + HEAD_SIZE], KEY_VALUE_HEADS, group),
            place(bias_grad[wq + HEAD_SIZE :], KEY_VALUE_HEADS, group),
        ],
        axis=-1,
    )
    small_rows = -(-seqs * one // wide)
    small_grad = small_grad.transpose(1, 0, 2).reshape(dps, seqs * one).astype(BF)
    small_grad = jnp.pad(small_grad, ((0, 0), (0, small_rows * wide - seqs * one)))
    small_grad = jnp.pad(small_grad.reshape(dps, -1, wide), ((0, 0), (0, 16 - small_rows), (0, 0)))
    qkv_grad = tn(normed, grad_pre, BF).reshape(seqs, dps, share, wide)
    qkv_grad = qkv_grad.transpose(1, 0, 2, 3).reshape(dps, seqs * share, wide)
    qkv_grad = ring_scatter(
        jnp.concatenate([qkv_grad, small_grad], axis=1).reshape(chips, 2, -1, wide)
    ).astype(BF)
    out_weight_grad = ring_scatter(out_weight_grad.reshape(chips, 2, share, model))
    smalls = qkv_grad[seqs * share : seqs * share + small_rows]
    smalls = smalls.reshape(-1)[: seqs * one].reshape(seqs, 1, one)
    smalls = jnp.pad(smalls, ((0, 0), (0, 15), (0, wide - one)))
    qkv_grad = qkv_grad[: seqs * share].reshape(seqs, share, wide)
    qkv_grad = jnp.concatenate([qkv_grad, smalls], axis=1)
    parts = [lax.dynamic_index_in_dim(qkv_grad, seq ^ k, 0, keepdims=False) for k in range(seqs)]
    parts = by_index([parts[0]] + [swap_seq(parts[k], k) for k in range(1, seqs)], seq)
    query_weight_grad = jnp.concatenate([part[:share, :wq] for part in parts], axis=1).astype(F32)
    pairs = [
        sum(part[:share, wq:].astype(F32) for part in parts[g * copies : (g + 1) * copies])
        for g in range(KEY_VALUE_HEADS)
    ]
    key_weight_grad = jnp.concatenate([pair[:, :HEAD_SIZE] for pair in pairs], axis=1)
    value_weight_grad = jnp.concatenate([pair[:, HEAD_SIZE:] for pair in pairs], axis=1)
    small_sum = sum(part[share, :one].astype(F32) for part in parts)
    gain_one_grad, gain_two_grad, query_bias_grad, key_bias_grad, value_bias_grad = jnp.split(
        small_sum, [share, 2 * share, 3 * share, 3 * share + kv_share]
    )

    return (
        layer_out[None],
        input_grad[None],
        gain_one_grad,
        query_weight_grad,
        query_bias_grad,
        key_weight_grad,
        key_bias_grad,
        value_weight_grad,
        value_bias_grad,
        out_weight_grad,
        gain_two_grad,
        gate_grad,
        up_grad,
        down_grad.T,
    )


def solution(mesh):
    tokens = P("dp", "seq", None)
    whole = P(("seq", "dp"))
    matrix = P(("seq", "dp"), None)
    feed = P("dp", "seq")
    in_specs = (
        tokens,
        P("dp", "seq"),
        tokens,
        whole,
        matrix,
        whole,
        matrix,
        whole,
        matrix,
        whole,
        matrix,
        whole,
        feed,
        feed,
        P("seq", "dp"),
    )
    out_specs = (
        tokens,
        tokens,
        whole,
        matrix,
        whole,
        matrix,
        whole,
        matrix,
        whole,
        matrix,
        whole,
        feed,
        feed,
        P("seq", "dp"),
    )
    return jax.shard_map(shards, mesh=mesh, in_specs=in_specs, out_specs=out_specs, check_vma=False)
```

```python
import functools

import jax
import jax.numpy as jnp
from jax import lax
from jax.experimental import pallas as pl
from jax.experimental.pallas import tpu as pltpu
from jax.sharding import PartitionSpec as P

H = 12
KEY_VALUE_HEADS = 2
HEAD_SIZE = 128
EPS = 1e-06
THETA = 1000000.0
SCALE = HEAD_SIZE ** (-0.5)
BF = jnp.bfloat16
F32 = jnp.float32


def dot(a, b, dims, out=F32):
    return lax.dot_general(a, b, (dims, ((), ())), preferred_element_type=F32).astype(out)


def nn(a, b, out=F32):
    return dot(a, b, ((1,), (0,)), out)


def nt(a, b, out=F32):
    return dot(a, b, ((1,), (1,)), out)


def tn(a, b, out=F32):
    return dot(a, b, ((0,), (0,)), out)


def rope_tables(length):
    exponent = jnp.arange(0, HEAD_SIZE, 2).astype(F32) / HEAD_SIZE
    freqs = THETA ** (-exponent)
    angles = jnp.arange(length, dtype=jnp.int32).astype(F32)[:, None] * freqs[None, :]
    cosine, sine = jnp.cos(angles), jnp.sin(angles)
    return jnp.concatenate([cosine, cosine], axis=-1), jnp.concatenate([-sine, sine], axis=-1)


def swap_halves(w):
    half = w.shape[-1] // 2
    return jnp.concatenate([w[..., half:], w[..., :half]], axis=-1)


def swap_seq(value, k):
    size = lax.axis_size("seq")
    return lax.ppermute(value, "seq", [(i, i ^ k) for i in range(size)])


def gather_seq(value):
    half = value.shape[0] // 2
    one = swap_seq(value, 1)
    two = swap_seq(value, 2)
    far = jnp.concatenate([swap_seq(two[:half], 1), swap_seq(one[half:], 2)], axis=0)
    return [value, one, two, far]


def scatter_seq(parts):
    low = [part.astype(BF) for part in parts[1:]]
    half = low[0].shape[0] // 2
    from_one = swap_seq(low[2][:half], 1)
    from_two = swap_seq(low[2][half:], 2)
    wide = [part.astype(F32) for part in parts]
    to_one = jnp.concatenate([wide[1][:half], wide[1][half:] + from_two.astype(F32)], axis=0).astype(BF)
    to_two = jnp.concatenate([wide[2][:half] + from_one.astype(F32), wide[2][half:]], axis=0).astype(BF)
    return wide[0] + swap_seq(to_one, 1).astype(F32) + swap_seq(to_two, 2).astype(F32)


def by_index(slots, index):
    stacked = jnp.stack(slots)
    return [
        lax.dynamic_index_in_dim(stacked, index ^ i, 0, keepdims=False) for i in range(len(slots))
    ]


def swap_core(value):
    size = lax.axis_size("dp")
    return lax.ppermute(value, "dp", [(i, i ^ 1) for i in range(size)])


def remote(src, dst, send, recv, where):
    return pltpu.make_async_remote_copy(
        src_ref=src, dst_ref=dst, send_sem=send, recv_sem=recv,
        device_id=where, device_id_type=pl.DeviceIdType.MESH,
    )


def greet(partners):
    barrier = pltpu.get_barrier_semaphore()
    for partner in partners:
        pl.semaphore_signal(barrier, inc=1, device_id=partner, device_id_type=pl.DeviceIdType.MESH)
    pl.semaphore_wait(barrier, len(partners))


def start_kernel(
    x_in, c_in, ids_in, small_in, pack_in, out_in,
    x_out, c_out, ids_out, small_out, pack_out, out_out,
    local_sem, seq_send, seq_recv, far_send, far_recv, ring_send, ring_recv, core_send, core_recv,
    out_send, out_recv, slot_send, slot_recv,
):
    seqs, dps = lax.axis_size("seq"), lax.axis_size("dp")
    chips = dps // 2
    seq, dpi = lax.axis_index("seq"), lax.axis_index("dp")
    chip, core = dpi // 2, dpi % 2
    ahead = ((chip + chips - 1) % chips) * 2 + core
    behind = ((chip + 1) % chips) * 2 + core
    sibling = chip * 2 + 1 - core
    greet([(seq ^ k, dpi) for k in range(1, seqs)] + [(seq, other) for other in (ahead, behind, sibling)])

    rows = x_in.shape[0]
    half = rows // 2

    def to_slots(i, src, dst, slots):
        return [remote(src, dst, seq_send.at[i, k], seq_recv.at[i, k], (seq ^ k, dpi)) for k in slots]

    def block(index, low=0, count=rows):
        return pl.ds(pl.multiple_of(index * rows + low, half), count)

    small_sends = to_slots(0, small_in, small_out.at[dpi, seq], range(1, seqs))
    pack_sends = [
        remote(
            pack_in.at[seq ^ k], pack_out.at[seq, dpi], seq_send.at[1, k], seq_recv.at[1, k], (seq ^ k, dpi)
        )
        for k in range(1, seqs)
    ]
    id_sends = to_slots(2, ids_in, ids_out.at[seq], range(1, seqs))
    x_sends = to_slots(3, x_in, x_out.at[block(seq)], (1, 2))
    c_sends = to_slots(4, c_in, c_out.at[block(seq)], (1, 2))
    locals_ = [
        pltpu.make_async_copy(small_in, small_out.at[dpi, seq], local_sem.at[0]),
        pltpu.make_async_copy(pack_in.at[seq], pack_out.at[seq, dpi], local_sem.at[1]),
        pltpu.make_async_copy(out_in, out_out.at[0, dpi], local_sem.at[2]),
        pltpu.make_async_copy(ids_in, ids_out.at[seq], local_sem.at[3]),
        pltpu.make_async_copy(x_in, x_out.at[block(seq)], local_sem.at[4]),
        pltpu.make_async_copy(c_in, c_out.at[block(seq)], local_sem.at[5]),
    ]
    for copy in small_sends + pack_sends + locals_[:3] + id_sends + x_sends + locals_[3:]:
        copy.start()
    for copy in locals_[:3] + small_sends + pack_sends:
        copy.wait()

    def far_sends(i, field):
        return [
            remote(
                field.at[block(seq ^ 2, 0, half)], field.at[block(seq ^ 2, 0, half)],
                far_send.at[i, 0], far_recv.at[i, 0], (seq ^ 1, dpi),
            ),
            remote(
                field.at[block(seq ^ 1, half, half)], field.at[block(seq ^ 1, half, half)],
                far_send.at[i, 1], far_recv.at[i, 1], (seq ^ 2, dpi),
            ),
        ]

    def hop_sends(hop, to_core):
        at = ((chip + hop) % chips) * 2 + core
        send, recv = (core_send, core_recv) if to_core else (ring_send, ring_recv)
        where = (seq, sibling) if to_core else (seq, ahead)
        return [
            remote(field, field, send.at[i, hop], recv.at[i, hop], where)
            for i, field in enumerate((small_out.at[at], pack_out.at[:, at], out_out.at[0, at]))
        ]

    def out_sends(hop):
        at = ((chip + hop) % chips) * 2 + core
        return [
            remote(
                out_out.at[0, at], out_out.at[k, at], out_send.at[k, hop], out_recv.at[k, hop], (seq ^ k, dpi)
            )
            for k in range(1, seqs)
        ]

    flying, outs = [], []
    for hop in range(chips):
        if hop > 0:
            for copy in rings:
                copy.wait_recv()
            flying += rings
        rings = hop_sends(hop, False) if hop < chips - 1 else []
        cores = hop_sends(hop, True)
        for copy in rings + cores:
            copy.start()
        flying += cores
        if hop == 0:
            for copy in x_sends:
                copy.wait()
            far_x = far_sends(0, x_out)
            for copy in far_x:
                copy.start()
        more = out_sends(hop)
        outs += more
        for copy in more:
            copy.start()
        if hop == 0:
            for copy in c_sends:
                copy.start()
    for copy in c_sends:
        copy.wait()
    far_c = far_sends(1, c_out)
    for copy in far_c:
        copy.start()
    for copy in outs:
        copy.wait_recv()
    slots = [
        remote(
            out_out.at[k, ((chip + hop) % chips) * 2 + core], out_out.at[k, ((chip + hop) % chips) * 2 + core],
            slot_send.at[k, hop], slot_recv.at[k, hop], (seq, sibling),
        )
        for k in range(1, seqs)
        for hop in range(chips)
    ]
    for copy in slots:
        copy.start()
    for copy in flying + outs:
        copy.wait_send()
    for hop in range(chips):
        for copy in hop_sends(hop, True):
            copy.wait_recv()
    for copy in slots + far_x + far_c + id_sends + locals_[3:]:
        copy.wait()


def start_call(x, c, ids, small, pack, out):
    seqs, dps = lax.axis_size("seq"), lax.axis_size("dp")
    chips = dps // 2
    share, wide = pack.shape[1:]
    any_space = pl.BlockSpec(memory_space=pl.ANY)
    shapes = (
        jax.ShapeDtypeStruct((seqs * x.shape[0], x.shape[1]), x.dtype),
        jax.ShapeDtypeStruct((seqs * c.shape[0], c.shape[1]), c.dtype),
        jax.ShapeDtypeStruct((seqs,) + ids.shape, ids.dtype),
        jax.ShapeDtypeStruct((dps, seqs) + small.shape, small.dtype),
        jax.ShapeDtypeStruct((seqs, dps, share, wide), pack.dtype),
        jax.ShapeDtypeStruct((seqs, dps) + out.shape, out.dtype),
    )
    dma = pltpu.SemaphoreType.DMA
    return pl.pallas_call(
        start_kernel,
        out_shape=shapes,
        in_specs=[any_space] * 6,
        out_specs=(any_space,) * 6,
        scratch_shapes=[
            dma((6,)), dma((5, seqs)), dma((5, seqs)), dma((2, 2)), dma((2, 2)),
            dma((3, chips)), dma((3, chips)), dma((3, chips)), dma((3, chips)),
            dma((seqs, chips)), dma((seqs, chips)), dma((seqs, chips)), dma((seqs, chips)),
        ],
        compiler_params=pltpu.CompilerParams(collective_id=0, has_side_effects=True),
        name="start_gather",
    )(x, c, ids, small, pack, out)


def attend_kernel(
    x_ref, w_ref, bias_ref, cos_ref, sin_ref, ids_row_ref, ids_col_ref, gain_one_ref, gain_two_ref, out_ref,
    normed_ref, qkv_ref, mixed_ref, lse_ref, hidden_ref, second_ref,
    all_ref, send_sem, recv_sem,
):
    seqs = lax.axis_size("seq")
    seq, dpi = lax.axis_index("seq"), lax.axis_index("dp")
    greet([(seq ^ k, dpi) for k in range(1, seqs)])
    length, model = x_ref.shape
    wq = mixed_ref.shape[1]
    heads = wq // HEAD_SIZE
    rows = length // seqs

    @pl.loop(0, seqs)
    def _(i):
        at = pl.ds(pl.multiple_of(i * rows, rows), rows)
        x = x_ref[at, :].astype(F32)
        factor = lax.rsqrt(jnp.mean(x * x, axis=-1, keepdims=True) + EPS)
        normed_ref[at, :] = (x * factor * gain_one_ref[...]).astype(BF)

    @pl.loop(0, 2)
    def _(i):
        at = pl.ds(pl.multiple_of(i * 2 * rows, 2 * rows), 2 * rows)
        pre = jnp.dot(normed_ref[at, :], w_ref[...], preferred_element_type=F32) + bias_ref[...]
        cosine, sine = cos_ref[at, :], sin_ref[at, :]
        for h in range(heads + 1):
            u = pre[:, h * HEAD_SIZE : (h + 1) * HEAD_SIZE]
            turned = pltpu.roll(u, HEAD_SIZE // 2, 1)
            qkv_ref[at, h * HEAD_SIZE : (h + 1) * HEAD_SIZE] = (u * cosine + turned * sine).astype(BF)
        qkv_ref[at, wq + HEAD_SIZE :] = pre[:, wq + HEAD_SIZE :].astype(BF)

    copies = []
    for t in range(seqs):
        at = slice(t * rows, (t + 1) * rows)
        reach = min(t + 2, seqs) * rows
        keys = qkv_ref[:reach, wq : wq + HEAD_SIZE]
        values = qkv_ref[:reach, wq + HEAD_SIZE :]
        allowed = ids_row_ref[:, :reach] <= ids_col_ref[at, :]
        sums = []
        for h in range(heads):
            lanes = slice(h * HEAD_SIZE, (h + 1) * HEAD_SIZE)
            scores = nt(qkv_ref[at, lanes], keys) * SCALE
            scores = jnp.where(allowed, scores, -1000000000.0)
            peak = jnp.max(scores, axis=-1, keepdims=True)
            raised = jnp.exp(scores - peak)
            total = jnp.sum(raised, axis=-1, keepdims=True)
            low = (raised * (1.0 / total)).astype(BF)
            mixed_ref[at, lanes] = nn(low, values).astype(BF)
            sums.append(peak + jnp.log(total))
        lse_ref[at, :heads] = jnp.concatenate(sums, axis=1)
        more = [
            remote(
                mixed_ref.at[pl.ds(t * rows, rows)], all_ref.at[pl.ds(t * rows, rows), pl.ds(k * wq, wq)],
                send_sem.at[k, t], recv_sem.at[k, t], (seq ^ k, dpi),
            )
            for k in range(1, seqs)
        ]
        for copy in more:
            copy.start()
        copies.append(more)
        all_ref[at, :wq] = mixed_ref[at, :]

    for t in range(seqs):
        at = slice(t * rows, (t + 1) * rows)
        for copy in copies[t]:
            copy.wait_recv()
        hidden = x_ref[at, :].astype(F32) + nn(all_ref[at, :], out_ref[...])
        hidden_ref[at, :] = hidden
        factor = lax.rsqrt(jnp.mean(hidden * hidden, axis=-1, keepdims=True) + EPS)
        second_ref[at, :] = (hidden * factor * gain_two_ref[...]).astype(BF)
    for t in range(seqs):
        for copy in copies[t]:
            copy.wait_send()


def attend_call(x, w, bias, cosine, sine, ids, gain_one, gain_two, out):
    seqs = lax.axis_size("seq")
    length, model = x.shape
    wide = w.shape[1]
    wq = wide - 2 * HEAD_SIZE
    vmem = pl.BlockSpec(memory_space=pltpu.VMEM)
    shape = jax.ShapeDtypeStruct
    return pl.pallas_call(
        attend_kernel,
        out_shape=(
            shape((length, model), BF),
            shape((length, wide), BF),
            shape((length, wq), BF),
            shape((length, 128), F32),
            shape((length, model), F32),
            shape((length, model), BF),
        ),
        in_specs=[vmem] * 10,
        out_specs=(vmem,) * 6,
        scratch_shapes=[
            pltpu.VMEM((length, seqs * wq), BF),
            pltpu.SemaphoreType.DMA((seqs, seqs)),
            pltpu.SemaphoreType.DMA((seqs, seqs)),
        ],
        cost_estimate=pl.CostEstimate(flops=9 * 10**9, bytes_accessed=30 * 10**6, transcendentals=3 * 10**6),
        compiler_params=pltpu.CompilerParams(
            collective_id=1, has_side_effects=True, vmem_limit_bytes=60 * 2**20
        ),
        name="attend",
    )(x, w, bias, cosine, sine, ids[None], ids[:, None], gain_one[None], gain_two[None], out)


TILE = 256


def act_kernel(x_ref, w_ref, active_ref, by_gate_ref, by_up_ref, *, tail):
    last = pl.program_id(0) == pl.num_programs(0) - 1

    def body(shift):
        both = jnp.dot(x_ref[...], w_ref[...], preferred_element_type=F32)
        gate, up = both[:, :TILE], both[:, shift : shift + TILE]
        sigma = jax.nn.sigmoid(gate)
        silu = gate * sigma
        active_ref[...] = (silu * up).astype(BF)
        by_gate_ref[...] = (up * sigma * (1.0 + gate * (1.0 - sigma))).astype(BF)
        by_up_ref[...] = silu.astype(BF)

    if tail == TILE:
        body(TILE)
    else:
        pl.when(jnp.logical_not(last))(lambda: body(TILE))
        pl.when(last)(lambda: body(tail))


def act_call(x, both):
    rows, model = x.shape
    units = both.shape[1] // 2
    tiles = -(-units // TILE)
    tail = units - (tiles - 1) * TILE
    tile = pl.BlockSpec((rows, TILE), lambda j: (0, j))
    return pl.pallas_call(
        functools.partial(act_kernel, tail=tail),
        grid=(tiles,),
        out_shape=[jax.ShapeDtypeStruct((rows, units), BF)] * 3,
        in_specs=[
            pl.BlockSpec((rows, model), lambda j: (0, 0)),
            pl.BlockSpec((model, 2 * TILE), lambda j: (0, j)),
        ],
        out_specs=[tile] * 3,
        cost_estimate=pl.CostEstimate(
            flops=4 * rows * model * units,
            bytes_accessed=2 * (both.size + x.size + 3 * rows * units),
            transcendentals=rows * units,
        ),
        compiler_params=pltpu.CompilerParams(vmem_limit_bytes=56 * 2**20),
        name="gate_up",
    )(x, both)


def back_kernel(order_ref, x_ref, w_ref, by_gate_ref, by_up_ref, out_ref, *, tail):
    last = pl.program_id(0) == pl.num_programs(0) - 1

    def body(widths):
        back = jnp.dot(x_ref[...], w_ref[...], preferred_element_type=F32)
        to_gate = (back * by_gate_ref[...].astype(F32)).astype(BF)
        to_up = (back * by_up_ref[...].astype(F32)).astype(BF)
        for i, width in enumerate(widths):
            low = i * TILE
            pair = jnp.concatenate([to_gate[:, low : low + width], to_up[:, low : low + width]], axis=1)
            out_ref[:, 2 * low : 2 * low + 2 * width] = pair

    if tail == (TILE, TILE):
        body(tail)
    else:
        pl.when(jnp.logical_not(last))(lambda: body((TILE, TILE)))
        pl.when(last)(lambda: body(tail))


def back_call(order, x, down, by_gate, by_up):
    rows, model = x.shape
    units = down.shape[1]
    step = 2 * TILE
    tiles = -(-units // step)
    rest = units - (tiles - 1) * step
    tail = (rest,) if rest <= TILE else (TILE, rest - TILE)
    tile = pl.BlockSpec((rows, step), lambda j: (0, j))
    return pl.pallas_call(
        functools.partial(back_kernel, tail=tail),
        grid=(tiles,),
        out_shape=jax.ShapeDtypeStruct((rows, 2 * units), BF),
        in_specs=[
            pl.BlockSpec(memory_space=pl.ANY),
            pl.BlockSpec((rows, model), lambda j: (0, 0)),
            pl.BlockSpec((model, step), lambda j: (0, j)),
            tile,
            tile,
        ],
        out_specs=pl.BlockSpec((rows, 2 * step), lambda j: (0, j)),
        cost_estimate=pl.CostEstimate(
            flops=2 * rows * model * units,
            bytes_accessed=2 * (down.size + x.size + 4 * rows * units),
            transcendentals=0,
        ),
        compiler_params=pltpu.CompilerParams(vmem_limit_bytes=56 * 2**20),
        name="back_down",
    )(order, x, down, by_gate, by_up)


def pair_tiles(left, right):
    units = left.shape[1]
    cuts = list(range(0, units, TILE)) + [units]
    return jnp.concatenate(
        [field[:, low:high] for low, high in zip(cuts[:-1], cuts[1:]) for field in (left, right)], axis=1
    )


def split_tiles(both):
    units = both.shape[1] // 2
    cuts = list(range(0, units, TILE)) + [units]
    spans = list(zip(cuts[:-1], cuts[1:]))
    return (
        jnp.concatenate([both[:, 2 * low : low + high] for low, high in spans], axis=1),
        jnp.concatenate([both[:, low + high : 2 * high] for low, high in spans], axis=1),
    )


def ring_scatter(terms):
    size = lax.axis_size("dp")
    chips = size // 2
    index = lax.axis_index("dp")
    chip, core = index // 2, index % 2
    give = lax.dynamic_index_in_dim(terms, 1 - core, 1, keepdims=False)
    keep = lax.dynamic_index_in_dim(terms, core, 1, keepdims=False)
    got = swap_core(give)

    def term(which):
        pick = lambda field: lax.dynamic_index_in_dim(field, which, 0, keepdims=False).astype(F32)
        return pick(keep) + pick(got)

    came = None
    for step in range(chips - 1):
        send = term((chip + chips - 1 - step) % chips)
        if came is not None:
            send = send + came.astype(F32)
        came = lax.ppermute(send.astype(BF), "dp", [(i, (i + 2) % size) for i in range(size)])
    total = term(chip)
    return total if came is None else total + came.astype(F32)


def shards(
    inputs,
    block_ids,
    cotangent,
    first_gain,
    query_weight,
    query_bias,
    key_weight,
    key_bias,
    value_weight,
    value_bias,
    output_weight,
    second_gain,
    gate_weight,
    up_weight,
    down_weight,
):
    seqs = lax.axis_size("seq")
    seq = lax.axis_index("seq")
    dps = lax.axis_size("dp")
    dpi = lax.axis_index("dp")
    chips, chip, core = dps // 2, dpi // 2, dpi % 2
    heads = H // seqs
    copies = seqs // KEY_VALUE_HEADS
    wq = heads * HEAD_SIZE
    wide = wq + 2 * HEAD_SIZE
    tokens_here, model = inputs.shape[1:]
    share = first_gain.shape[0]
    kv_share = key_bias.shape[0]
    hidden_units = gate_weight.shape[1]

    small = jnp.concatenate([first_gain, second_gain, query_bias, key_bias, value_bias])
    packed = jnp.concatenate(
        [
            query_weight.reshape(share, seqs, wq),
            jnp.repeat(key_weight.reshape(share, KEY_VALUE_HEADS, HEAD_SIZE), copies, axis=1),
            jnp.repeat(value_weight.reshape(share, KEY_VALUE_HEADS, HEAD_SIZE), copies, axis=1),
        ],
        axis=-1,
    ).transpose(1, 0, 2)
    one = small.shape[0]
    small = jnp.pad(small[None], ((0, 15), (0, -one % 128)))
    tokens, incoming, blocks, smalls, weight_qkv, weight_out = start_call(
        inputs[0], cotangent[0], block_ids.reshape(-1, 128), small, packed, output_weight
    )
    blocks = blocks.reshape(-1)
    weight_qkv = weight_qkv.reshape(model, wide)
    out_head = weight_out[0].reshape(dps * share, model)
    weight_out = weight_out.reshape(model, model)
    smalls = smalls[:, :, 0, :one].transpose(1, 0, 2).astype(F32)
    gain_first = smalls[:, :, :share].reshape(model)
    gain_second = smalls[:, :, share : 2 * share].reshape(model)
    bias_q = lax.dynamic_index_in_dim(smalls, seq, 0, keepdims=False)[:, 2 * share : 3 * share].reshape(wq)
    group = seq // copies
    bias_k = smalls[:, :, 3 * share : 3 * share + kv_share].reshape(KEY_VALUE_HEADS, HEAD_SIZE)
    bias_v = smalls[:, :, 3 * share + kv_share :].reshape(KEY_VALUE_HEADS, HEAD_SIZE)
    bias = jnp.concatenate(
        [
            bias_q,
            lax.dynamic_index_in_dim(bias_k, group, 0, keepdims=False),
            lax.dynamic_index_in_dim(bias_v, group, 0, keepdims=False),
        ]
    )
    length = tokens.shape[0]
    cosine, sine = rope_tables(length)

    gather = lambda field: lax.all_gather(field, "dp", axis=0, tiled=True)
    whole_both = gather(pair_tiles(gate_weight, up_weight))
    tokens, down_turned = lax.optimization_barrier((tokens, down_weight.T))
    whole_down = gather(down_turned)

    normed, qkv, mixed, logsum, hidden, second = attend_call(
        tokens, weight_qkv, bias[None], cosine, sine, blocks, gain_first, gain_second, weight_out
    )
    tokens = tokens.astype(F32)
    first_factor = lax.rsqrt(jnp.mean(tokens * tokens, axis=-1, keepdims=True) + EPS)
    second_factor = lax.rsqrt(jnp.mean(hidden * hidden, axis=-1, keepdims=True) + EPS)
    own = lambda field: lax.dynamic_slice_in_dim(field, seq * tokens_here, tokens_here, 0)
    split = lambda field: [
        lax.dynamic_slice_in_dim(field, (seq ^ k) * tokens_here, tokens_here, 0) for k in range(seqs)
    ]
    by_place = lambda field: jnp.concatenate(by_index(gather_seq(field), seq), axis=0)

    active, by_gate, by_up = act_call(second, whole_both)
    scatter = lambda field: lax.psum_scatter(field, "dp", scatter_dimension=0, tiled=True)
    down_grad = tn(incoming, active, BF)
    grad_both = back_call(down_grad, incoming, whole_down, by_gate, by_up)
    down_grad = scatter(down_grad).astype(F32)
    second_sum = nt(grad_both, whole_both)
    out_sum = nt(active, whole_down)
    gate_grad, up_grad = split_tiles(scatter(tn(second, grad_both, BF)).astype(F32))
    grad_second = scatter_seq(split(second_sum))
    layer_out = (own(hidden) + scatter_seq(split(out_sum))).astype(BF)

    gain_two_grad = jnp.sum(second_sum * (hidden * second_factor), axis=0)
    factor = own(second_factor)
    unit = own(hidden) * factor
    scaled = grad_second * gain_second
    grad_hidden = cotangent[0].astype(F32) + factor * (
        scaled - unit * jnp.mean(scaled * unit, axis=-1, keepdims=True)
    )
    branch = by_place(grad_hidden.astype(BF))
    out_weight_grad = tn(mixed, branch, BF)
    grad_mixed = nt(branch, out_head, BF).reshape(length, heads, HEAD_SIZE)

    queries, keys = qkv[:, :wq].reshape(length, heads, HEAD_SIZE), qkv[:, wq : wq + HEAD_SIZE]
    values = qkv[:, wq + HEAD_SIZE :]
    allowed = blocks[None, :] <= blocks[:, None]
    scores = jnp.einsum("rhd,td->hrt", queries, keys, preferred_element_type=F32) * SCALE
    scores = jnp.where(allowed[None], scores, -1000000000.0)
    probs = jnp.exp(scores - logsum[:, :heads].T[:, :, None])
    grad_probs = jnp.einsum("rhd,td->hrt", grad_mixed, values, preferred_element_type=F32)
    delta = jnp.sum(probs * grad_probs, axis=-1, keepdims=True)
    grad_scores = (probs * (grad_probs - delta)).astype(BF)
    grad_queries = jnp.einsum("hrt,td->rhd", grad_scores, keys, preferred_element_type=F32) * SCALE
    grad_keys = jnp.einsum("hrt,rhd->td", grad_scores, queries, preferred_element_type=F32) * SCALE
    grad_values = jnp.einsum(
        "hrt,rhd->td", probs.astype(BF), grad_mixed, preferred_element_type=F32
    )
    grad_rotated = jnp.concatenate([grad_queries, grad_keys[:, None]], axis=1)
    grad_rotating = grad_rotated * cosine[:, None] + swap_halves(grad_rotated * sine[:, None])
    grad_pre = jnp.concatenate(
        [grad_rotating.reshape(length, wq + HEAD_SIZE), grad_values], axis=1
    ).astype(BF)
    grad_normed = nt(grad_pre, weight_qkv)
    gain_one_grad = jnp.sum(grad_normed * (tokens * first_factor), axis=0)
    grad_normed = scatter_seq(split(grad_normed))
    factor = own(first_factor)
    unit = own(tokens) * factor
    scaled = grad_normed * gain_first
    input_grad = grad_hidden + factor * (
        scaled - unit * jnp.mean(scaled * unit, axis=-1, keepdims=True)
    )
    input_grad = input_grad.astype(BF)

    bias_grad = jnp.sum(grad_pre.astype(F32), axis=0)
    place = lambda field, count, at: jnp.where(
        (jnp.arange(count) == at)[:, None], field[None], 0.0
    ).reshape(seqs, dps, -1)
    small_grad = jnp.concatenate(
        [
            gain_one_grad.reshape(seqs, dps, share),
            gain_two_grad.reshape(seqs, dps, share),
            place(bias_grad[:wq], seqs, seq),
            place(bias_grad[wq : wq + HEAD_SIZE], KEY_VALUE_HEADS, group),
            place(bias_grad[wq + HEAD_SIZE :], KEY_VALUE_HEADS, group),
        ],
        axis=-1,
    )
    small_rows = -(-seqs * one // wide)
    small_grad = small_grad.transpose(1, 0, 2).reshape(dps, seqs * one).astype(BF)
    small_grad = jnp.pad(small_grad, ((0, 0), (0, small_rows * wide - seqs * one)))
    small_grad = jnp.pad(small_grad.reshape(dps, -1, wide), ((0, 0), (0, 16 - small_rows), (0, 0)))
    qkv_grad = tn(normed, grad_pre, BF).reshape(seqs, dps, share, wide)
    qkv_grad = qkv_grad.transpose(1, 0, 2, 3).reshape(dps, seqs * share, wide)
    qkv_grad = ring_scatter(
        jnp.concatenate([qkv_grad, small_grad], axis=1).reshape(chips, 2, -1, wide)
    ).astype(BF)
    out_weight_grad = ring_scatter(out_weight_grad.reshape(chips, 2, share, model))
    smalls = qkv_grad[seqs * share : seqs * share + small_rows]
    smalls = smalls.reshape(-1)[: seqs * one].reshape(seqs, 1, one)
    smalls = jnp.pad(smalls, ((0, 0), (0, 15), (0, wide - one)))
    qkv_grad = qkv_grad[: seqs * share].reshape(seqs, share, wide)
    qkv_grad = jnp.concatenate([qkv_grad, smalls], axis=1)
    parts = [lax.dynamic_index_in_dim(qkv_grad, seq ^ k, 0, keepdims=False) for k in range(seqs)]
    parts = by_index([parts[0]] + [swap_seq(parts[k], k) for k in range(1, seqs)], seq)
    query_weight_grad = jnp.concatenate([part[:share, :wq] for part in parts], axis=1).astype(F32)
    pairs = [
        sum(part[:share, wq:].astype(F32) for part in parts[g * copies : (g + 1) * copies])
        for g in range(KEY_VALUE_HEADS)
    ]
    key_weight_grad = jnp.concatenate([pair[:, :HEAD_SIZE] for pair in pairs], axis=1)
    value_weight_grad = jnp.concatenate([pair[:, HEAD_SIZE:] for pair in pairs], axis=1)
    small_sum = sum(part[share, :one].astype(F32) for part in parts)
    gain_one_grad, gain_two_grad, query_bias_grad, key_bias_grad, value_bias_grad = jnp.split(
        small_sum, [share, 2 * share, 3 * share, 3 * share + kv_share]
    )

    return (
        layer_out[None],
        input_grad[None],
        gain_one_grad,
        query_weight_grad,
        query_bias_grad,
        key_weight_grad,
        key_bias_grad,
        value_weight_grad,
        value_bias_grad,
        out_weight_grad,
        gain_two_grad,
        gate_grad,
        up_grad,
        down_grad.T,
    )


def solution(mesh):
    tokens = P("dp", "seq", None)
    whole = P(("seq", "dp"))
    matrix = P(("seq", "dp"), None)
    feed = P("dp", "seq")
    in_specs = (
        tokens,
        P("dp", "seq"),
        tokens,
        whole,
        matrix,
        whole,
        matrix,
        whole,
        matrix,
        whole,
        matrix,
        whole,
        feed,
        feed,
        P("seq", "dp"),
    )
    out_specs = (
        tokens,
        tokens,
        whole,
        matrix,
        whole,
        matrix,
        whole,
        matrix,
        whole,
        matrix,
        whole,
        feed,
        feed,
        P("seq", "dp"),
    )
    return jax.shard_map(shards, mesh=mesh, in_specs=in_specs, out_specs=out_specs, check_vma=False)
```

```python
import functools

import jax
import jax.numpy as jnp
from jax import lax
from jax.experimental import pallas as pl
from jax.experimental.pallas import tpu as pltpu
from jax.sharding import PartitionSpec as P

H = 12
KEY_VALUE_HEADS = 2
HEAD_SIZE = 128
EPS = 1e-06
THETA = 1000000.0
SCALE = HEAD_SIZE ** (-0.5)
BF = jnp.bfloat16
F32 = jnp.float32


def dot(a, b, dims, out=F32):
    return lax.dot_general(a, b, (dims, ((), ())), preferred_element_type=F32).astype(out)


def nn(a, b, out=F32):
    return dot(a, b, ((1,), (0,)), out)


def nt(a, b, out=F32):
    return dot(a, b, ((1,), (1,)), out)


def tn(a, b, out=F32):
    return dot(a, b, ((0,), (0,)), out)


def rope_tables(length):
    exponent = jnp.arange(0, HEAD_SIZE, 2).astype(F32) / HEAD_SIZE
    freqs = THETA ** (-exponent)
    angles = jnp.arange(length, dtype=jnp.int32).astype(F32)[:, None] * freqs[None, :]
    cosine, sine = jnp.cos(angles), jnp.sin(angles)
    return jnp.concatenate([cosine, cosine], axis=-1), jnp.concatenate([-sine, sine], axis=-1)


def swap_halves(w):
    half = w.shape[-1] // 2
    return jnp.concatenate([w[..., half:], w[..., :half]], axis=-1)


def swap_seq(value, k):
    size = lax.axis_size("seq")
    return lax.ppermute(value, "seq", [(i, i ^ k) for i in range(size)])


def swap_core(value):
    size = lax.axis_size("dp")
    return lax.ppermute(value, "dp", [(i, i ^ 1) for i in range(size)])


def remote(src, dst, send, recv, where):
    return pltpu.make_async_remote_copy(
        src_ref=src, dst_ref=dst, send_sem=send, recv_sem=recv,
        device_id=where, device_id_type=pl.DeviceIdType.MESH,
    )


def greet(partners):
    barrier = pltpu.get_barrier_semaphore()
    for partner in partners:
        pl.semaphore_signal(barrier, inc=1, device_id=partner, device_id_type=pl.DeviceIdType.MESH)
    pl.semaphore_wait(barrier, len(partners))


def start_kernel(
    x_in, c_in, ids_in, small_in, pack_in, out_in,
    x_out, c_out, ids_out, small_out, pack_out, out_out,
    local_sem, seq_send, seq_recv, far_send, far_recv, ring_send, ring_recv, core_send, core_recv,
    out_send, out_recv, slot_send, slot_recv,
):
    seqs, dps = lax.axis_size("seq"), lax.axis_size("dp")
    chips = dps // 2
    seq, dpi = lax.axis_index("seq"), lax.axis_index("dp")
    chip, core = dpi // 2, dpi % 2
    ahead = ((chip + chips - 1) % chips) * 2 + core
    behind = ((chip + 1) % chips) * 2 + core
    sibling = chip * 2 + 1 - core
    greet([(seq ^ k, dpi) for k in range(1, seqs)] + [(seq, other) for other in (ahead, behind, sibling)])

    rows = x_in.shape[0]
    half = rows // 2

    def to_slots(i, src, dst, slots):
        return [remote(src, dst, seq_send.at[i, k], seq_recv.at[i, k], (seq ^ k, dpi)) for k in slots]

    def block(index, low=0, count=rows):
        return pl.ds(pl.multiple_of(index * rows + low, half), count)

    small_sends = to_slots(0, small_in, small_out.at[dpi, seq], range(1, seqs))
    pack_sends = [
        remote(
            pack_in.at[seq ^ k], pack_out.at[seq, dpi], seq_send.at[1, k], seq_recv.at[1, k], (seq ^ k, dpi)
        )
        for k in range(1, seqs)
    ]
    id_sends = to_slots(2, ids_in, ids_out.at[seq], range(1, seqs))
    x_sends = to_slots(3, x_in, x_out.at[block(seq)], (1, 2))
    c_sends = to_slots(4, c_in, c_out.at[block(seq)], (1, 2))
    locals_ = [
        pltpu.make_async_copy(small_in, small_out.at[dpi, seq], local_sem.at[0]),
        pltpu.make_async_copy(pack_in.at[seq], pack_out.at[seq, dpi], local_sem.at[1]),
        pltpu.make_async_copy(out_in, out_out.at[0, dpi], local_sem.at[2]),
        pltpu.make_async_copy(ids_in, ids_out.at[seq], local_sem.at[3]),
        pltpu.make_async_copy(x_in, x_out.at[block(seq)], local_sem.at[4]),
        pltpu.make_async_copy(c_in, c_out.at[block(seq)], local_sem.at[5]),
    ]
    for copy in small_sends + pack_sends + locals_[:3] + id_sends + x_sends + locals_[3:]:
        copy.start()
    for copy in locals_[:3] + small_sends + pack_sends:
        copy.wait()

    def far_sends(i, field):
        return [
            remote(
                field.at[block(seq ^ 2, 0, half)], field.at[block(seq ^ 2, 0, half)],
                far_send.at[i, 0], far_recv.at[i, 0], (seq ^ 1, dpi),
            ),
            remote(
                field.at[block(seq ^ 1, half, half)], field.at[block(seq ^ 1, half, half)],
                far_send.at[i, 1], far_recv.at[i, 1], (seq ^ 2, dpi),
            ),
        ]

    def hop_sends(hop, to_core):
        at = ((chip + hop) % chips) * 2 + core
        send, recv = (core_send, core_recv) if to_core else (ring_send, ring_recv)
        where = (seq, sibling) if to_core else (seq, ahead)
        return [
            remote(field, field, send.at[i, hop], recv.at[i, hop], where)
            for i, field in enumerate((small_out.at[at], pack_out.at[:, at], out_out.at[0, at]))
        ]

    def out_sends(hop):
        at = ((chip + hop) % chips) * 2 + core
        return [
            remote(
                out_out.at[0, at], out_out.at[k, at], out_send.at[k, hop], out_recv.at[k, hop], (seq ^ k, dpi)
            )
            for k in range(1, seqs)
        ]

    flying, outs = [], []
    for hop in range(chips):
        if hop > 0:
            for copy in rings:
                copy.wait_recv()
            flying += rings
        rings = hop_sends(hop, False) if hop < chips - 1 else []
        cores = hop_sends(hop, True)
        for copy in rings + cores:
            copy.start()
        flying += cores
        if hop == 0:
            for copy in x_sends:
                copy.wait()
            far_x = far_sends(0, x_out)
            for copy in far_x:
                copy.start()
        more = out_sends(hop)
        outs += more
        for copy in more:
            copy.start()
        if hop == 0:
            for copy in c_sends:
                copy.start()
    for copy in c_sends:
        copy.wait()
    far_c = far_sends(1, c_out)
    for copy in far_c:
        copy.start()
    for copy in outs:
        copy.wait_recv()
    slots = [
        remote(
            out_out.at[k, ((chip + hop) % chips) * 2 + core], out_out.at[k, ((chip + hop) % chips) * 2 + core],
            slot_send.at[k, hop], slot_recv.at[k, hop], (seq, sibling),
        )
        for k in range(1, seqs)
        for hop in range(chips)
    ]
    for copy in slots:
        copy.start()
    for copy in flying + outs:
        copy.wait_send()
    for hop in range(chips):
        for copy in hop_sends(hop, True):
            copy.wait_recv()
    for copy in slots + far_x + far_c + id_sends + locals_[3:]:
        copy.wait()


def start_call(x, c, ids, small, pack, out):
    seqs, dps = lax.axis_size("seq"), lax.axis_size("dp")
    chips = dps // 2
    share, wide = pack.shape[1:]
    any_space = pl.BlockSpec(memory_space=pl.ANY)
    shapes = (
        jax.ShapeDtypeStruct((seqs * x.shape[0], x.shape[1]), x.dtype),
        jax.ShapeDtypeStruct((seqs * c.shape[0], c.shape[1]), c.dtype),
        jax.ShapeDtypeStruct((seqs,) + ids.shape, ids.dtype),
        jax.ShapeDtypeStruct((dps, seqs) + small.shape, small.dtype),
        jax.ShapeDtypeStruct((seqs, dps, share, wide), pack.dtype),
        jax.ShapeDtypeStruct((seqs, dps) + out.shape, out.dtype),
    )
    dma = pltpu.SemaphoreType.DMA
    return pl.pallas_call(
        start_kernel,
        out_shape=shapes,
        in_specs=[any_space] * 6,
        out_specs=(any_space,) * 6,
        scratch_shapes=[
            dma((6,)), dma((5, seqs)), dma((5, seqs)), dma((2, 2)), dma((2, 2)),
            dma((3, chips)), dma((3, chips)), dma((3, chips)), dma((3, chips)),
            dma((seqs, chips)), dma((seqs, chips)), dma((seqs, chips)), dma((seqs, chips)),
        ],
        compiler_params=pltpu.CompilerParams(collective_id=0, has_side_effects=True),
        name="start_gather",
    )(x, c, ids, small, pack, out)


def attend_kernel(
    x_ref, w_ref, bias_ref, cos_ref, sin_ref, ids_row_ref, ids_col_ref, gain_one_ref, gain_two_ref, out_ref,
    normed_ref, qkv_ref, mixed_ref, lse_ref, hidden_ref, second_ref,
    all_ref, send_sem, recv_sem,
):
    seqs = lax.axis_size("seq")
    seq, dpi = lax.axis_index("seq"), lax.axis_index("dp")
    greet([(seq ^ k, dpi) for k in range(1, seqs)])
    length, model = x_ref.shape
    wq = mixed_ref.shape[1]
    heads = wq // HEAD_SIZE
    rows = length // seqs

    @pl.loop(0, seqs)
    def _(i):
        at = pl.ds(pl.multiple_of(i * rows, rows), rows)
        x = x_ref[at, :].astype(F32)
        factor = lax.rsqrt(jnp.mean(x * x, axis=-1, keepdims=True) + EPS)
        normed_ref[at, :] = (x * factor * gain_one_ref[...]).astype(BF)

    @pl.loop(0, 2)
    def _(i):
        at = pl.ds(pl.multiple_of(i * 2 * rows, 2 * rows), 2 * rows)
        pre = jnp.dot(normed_ref[at, :], w_ref[...], preferred_element_type=F32) + bias_ref[...]
        cosine, sine = cos_ref[at, :], sin_ref[at, :]
        for h in range(heads + 1):
            u = pre[:, h * HEAD_SIZE : (h + 1) * HEAD_SIZE]
            turned = pltpu.roll(u, HEAD_SIZE // 2, 1)
            qkv_ref[at, h * HEAD_SIZE : (h + 1) * HEAD_SIZE] = (u * cosine + turned * sine).astype(BF)
        qkv_ref[at, wq + HEAD_SIZE :] = pre[:, wq + HEAD_SIZE :].astype(BF)

    copies = []
    for t in range(seqs):
        at = slice(t * rows, (t + 1) * rows)
        reach = min(t + 2, seqs) * rows
        keys = qkv_ref[:reach, wq : wq + HEAD_SIZE]
        values = qkv_ref[:reach, wq + HEAD_SIZE :]
        allowed = ids_row_ref[:, :reach] <= ids_col_ref[at, :]
        sums = []
        for h in range(heads):
            lanes = slice(h * HEAD_SIZE, (h + 1) * HEAD_SIZE)
            scores = nt(qkv_ref[at, lanes], keys) * SCALE
            scores = jnp.where(allowed, scores, -1000000000.0)
            peak = jnp.max(scores, axis=-1, keepdims=True)
            raised = jnp.exp(scores - peak)
            total = jnp.sum(raised, axis=-1, keepdims=True)
            low = (raised * (1.0 / total)).astype(BF)
            mixed_ref[at, lanes] = nn(low, values).astype(BF)
            sums.append(peak + jnp.log(total))
        lse_ref[at, :heads] = jnp.concatenate(sums, axis=1)
        more = [
            remote(
                mixed_ref.at[pl.ds(t * rows, rows)], all_ref.at[pl.ds(t * rows, rows), pl.ds(k * wq, wq)],
                send_sem.at[k, t], recv_sem.at[k, t], (seq ^ k, dpi),
            )
            for k in range(1, seqs)
        ]
        for copy in more:
            copy.start()
        copies.append(more)
        all_ref[at, :wq] = mixed_ref[at, :]

    for t in range(seqs):
        at = slice(t * rows, (t + 1) * rows)
        for copy in copies[t]:
            copy.wait_recv()
        hidden = x_ref[at, :].astype(F32) + nn(all_ref[at, :], out_ref[...])
        hidden_ref[at, :] = hidden
        factor = lax.rsqrt(jnp.mean(hidden * hidden, axis=-1, keepdims=True) + EPS)
        second_ref[at, :] = (hidden * factor * gain_two_ref[...]).astype(BF)
    for t in range(seqs):
        for copy in copies[t]:
            copy.wait_send()


def attend_call(x, w, bias, cosine, sine, ids, gain_one, gain_two, out):
    seqs = lax.axis_size("seq")
    length, model = x.shape
    wide = w.shape[1]
    wq = wide - 2 * HEAD_SIZE
    vmem = pl.BlockSpec(memory_space=pltpu.VMEM)
    shape = jax.ShapeDtypeStruct
    return pl.pallas_call(
        attend_kernel,
        out_shape=(
            shape((length, model), BF),
            shape((length, wide), BF),
            shape((length, wq), BF),
            shape((length, 128), F32),
            shape((length, model), F32),
            shape((length, model), BF),
        ),
        in_specs=[vmem] * 10,
        out_specs=(vmem,) * 6,
        scratch_shapes=[
            pltpu.VMEM((length, seqs * wq), BF),
            pltpu.SemaphoreType.DMA((seqs, seqs)),
            pltpu.SemaphoreType.DMA((seqs, seqs)),
        ],
        cost_estimate=pl.CostEstimate(flops=9 * 10**9, bytes_accessed=30 * 10**6, transcendentals=3 * 10**6),
        compiler_params=pltpu.CompilerParams(
            collective_id=1, has_side_effects=True, vmem_limit_bytes=60 * 2**20
        ),
        name="attend",
    )(x, w, bias, cosine, sine, ids[None], ids[:, None], gain_one[None], gain_two[None], out)


PIECES = 4


def slot_rows(index, rows):
    return pl.ds(pl.multiple_of(index * rows, rows), rows)


class SeqSum:
    def __init__(self, field, rows, came, sums, from_one, from_two, sems, dpi, seq):
        self.field, self.rows, self.piece = field, rows, rows // PIECES
        self.came, self.sums, self.got = came, sums, {1: from_one, 2: from_two}
        self.send, self.recv = sems
        self.dpi, self.seq = dpi, seq
        self.started = []

    def at(self, k, c):
        start = (self.seq ^ k) * self.rows + c * self.piece
        return pl.ds(pl.multiple_of(start, self.piece), self.piece)

    def pass_on(self, c):
        by = 1 + c % 2
        return remote(
            self.field.at[self.at(3, c)], self.came.at[c], self.send.at[0, c], self.recv.at[0, c], (self.seq ^ by, self.dpi)
        )

    def direct(self, k, c):
        late = (k == 2) == (c % 2 == 0)
        src = self.sums.at[c] if late else self.field.at[self.at(k, c)]
        return remote(src, self.got[k].at[c], self.send.at[k, c], self.recv.at[k, c], (self.seq ^ k, self.dpi))

    def begin(self):
        for c in range(PIECES):
            self.pass_on(c).start()
            self.direct(1 + c % 2, c).start()

    def middle(self):
        for c in range(PIECES):
            k = 2 - c % 2
            self.pass_on(c).wait_recv()
            own = self.field[self.at(k, c), :].astype(F32)
            self.sums[c] = (self.came[c].astype(F32) + own).astype(BF)
            self.direct(k, c).start()

    def take(self, c):
        for k in (1, 2):
            self.direct(k, c).wait_recv()
        total = self.field[self.at(0, c), :].astype(F32) + self.got[1][c].astype(F32)
        return total + self.got[2][c].astype(F32)

    def finish(self):
        for c in range(PIECES):
            self.pass_on(c).wait_send()
            for k in (1, 2):
                self.direct(k, c).wait_send()


def backward_kernel(
    second_grad_ref, hidden_ref, cotangent_ref, gain_one_ref, gain_two_ref, lse_ref, cos_ref, sin_ref,
    ids_row_ref, ids_col_ref, tokens_hbm, normed_hbm, w_hbm, out_hbm, qkv_hbm, mixed_hbm, order_hbm,
    normed_grad_ref, hidden_grad_ref, w_grad_ref, out_grad_ref, bias_grad_ref, gain_grad_ref,
    tokens_ref, normed_ref, w_ref, out_ref, qkv_ref, mixed_ref,
    branch_ref, mixed_grad_ref, pre_grad_ref, key_grad_ref, value_grad_ref,
    came_ref, sums_ref, one_ref, two_ref,
    load_sem, sum_send, sum_recv, branch_send, branch_recv,
):
    seqs = lax.axis_size("seq")
    seq, dpi = lax.axis_index("seq"), lax.axis_index("dp")
    length, model = second_grad_ref.shape
    rows = length // seqs
    piece = rows // PIECES
    wq = mixed_ref.shape[1]
    heads = wq // HEAD_SIZE
    loads = [
        pltpu.make_async_copy(src, dst, load_sem.at[i])
        for i, (src, dst) in enumerate(
            (
                (out_hbm, out_ref), (qkv_hbm, qkv_ref), (w_hbm, w_ref),
                (tokens_hbm, tokens_ref), (normed_hbm, normed_ref), (mixed_hbm, mixed_ref),
            )
        )
    ]
    for load in loads:
        load.start()
    greet([(seq ^ k, dpi) for k in range(1, seqs)])

    total = SeqSum(second_grad_ref, rows, came_ref, sums_ref, one_ref, two_ref, (sum_send, sum_recv), dpi, seq)
    total.begin()
    total.middle()

    def branch_at(k, c):
        start = (seq ^ k) * rows + c * piece
        return branch_ref.at[pl.ds(pl.multiple_of(start, piece), piece)]

    def branch_copy(k, c):
        if k < 3:
            return remote(
                branch_at(0, c), branch_at(0, c), branch_send.at[k, c], branch_recv.at[k, c], (seq ^ k, dpi)
            )
        came, to = (2, 1) if c % 2 == 0 else (1, 2)
        return remote(
            branch_at(came, c), branch_at(came, c), branch_send.at[3, c], branch_recv.at[3, c], (seq ^ to, dpi)
        )

    for c in range(PIECES):
        at = pl.ds(c * piece, piece)
        grad = total.take(c)
        hidden = hidden_ref[at, :]
        factor = lax.rsqrt(jnp.mean(hidden * hidden, axis=-1, keepdims=True) + EPS)
        unit = hidden * factor
        scaled = grad * gain_two_ref[...]
        grad = cotangent_ref[at, :].astype(F32) + factor * (
            scaled - unit * jnp.mean(scaled * unit, axis=-1, keepdims=True)
        )
        hidden_grad_ref[at, :] = grad
        start = pl.multiple_of(seq * rows + c * piece, piece)
        branch_ref[pl.ds(start, piece), :] = grad.astype(BF)
        for k in (1, 2):
            branch_copy(k, c).start()
    total.finish()
    for load in loads[:2]:
        load.wait()

    key_grad_ref[...] = jnp.zeros_like(key_grad_ref)
    value_grad_ref[...] = jnp.zeros_like(value_grad_ref)

    def rot_back(w, at):
        return w * cos_ref[at, :] + pltpu.roll(w * sin_ref[at, :], HEAD_SIZE // 2, 1)

    def attend_back(k):
        at = slot_rows(seq ^ k, rows)
        mixed_grad_ref[at, :] = nt(branch_ref[at, :], out_ref[...]).astype(BF)
        allowed = ids_row_ref[...] <= ids_col_ref[at, :]
        keys = qkv_ref[:, wq : wq + HEAD_SIZE]
        values = qkv_ref[:, wq + HEAD_SIZE :]
        for h in range(heads):
            lanes = slice(h * HEAD_SIZE, (h + 1) * HEAD_SIZE)
            queries = qkv_ref[at, lanes]
            grad = mixed_grad_ref[at, lanes]
            scores = jnp.where(allowed, nt(queries, keys) * SCALE, -1000000000.0)
            probs = jnp.exp(scores - lse_ref[at, h : h + 1])
            prob_grad = nt(grad, values)
            delta = jnp.sum(probs * prob_grad, axis=-1, keepdims=True)
            score_grad = (probs * (prob_grad - delta)).astype(BF)
            pre_grad_ref[at, lanes] = rot_back(nn(score_grad, keys) * SCALE, at).astype(BF)
            key_grad_ref[...] += tn(score_grad, queries)
            value_grad_ref[...] += tn(probs.astype(BF), grad)

    attend_back(0)
    for k in (1, 2):
        for c in range(PIECES):
            branch_copy(k, c).wait_recv()
            if (k == 2) == (c % 2 == 0):
                branch_copy(3, c).start()
        attend_back(k)
    for c in range(PIECES):
        branch_copy(3, c).wait_recv()
    attend_back(3)
    for c in range(PIECES):
        for k in (1, 2, 3):
            branch_copy(k, c).wait_send()

    every = pl.ds(0, length)
    pre_grad_ref[:, wq : wq + HEAD_SIZE] = rot_back(key_grad_ref[...] * SCALE, every).astype(BF)
    pre_grad_ref[:, wq + HEAD_SIZE :] = value_grad_ref[...].astype(BF)
    bias_grad_ref[...] = jnp.sum(pre_grad_ref[...].astype(F32), axis=0, keepdims=True)
    for load in loads[2:]:
        load.wait()
    gain_grad_ref[...] = jnp.zeros_like(gain_grad_ref)

    @pl.loop(0, seqs)
    def _(i):
        at = slot_rows(i, rows)
        grad = nt(pre_grad_ref[at, :], w_ref[...])
        x = tokens_ref[at, :].astype(F32)
        factor = lax.rsqrt(jnp.mean(x * x, axis=-1, keepdims=True) + EPS)
        gain_grad_ref[...] += jnp.sum(grad * (x * factor), axis=0, keepdims=True)
        normed_grad_ref[at, :] = grad.astype(BF)

    @pl.loop(0, model // wq)
    def _(i):
        lanes = pl.ds(pl.multiple_of(i * wq, HEAD_SIZE), wq)
        w_grad_ref[pl.ds(pl.multiple_of(i * wq, HEAD_SIZE), wq), :] = tn(normed_ref[:, lanes], pre_grad_ref[...]).astype(BF)
        out_grad_ref[:, lanes] = tn(mixed_ref[...], branch_ref[:, lanes]).astype(BF)


def backward_call(
    second_grad, hidden, cotangent, gain_one, gain_two, logsum, cosine, sine, ids, tokens, normed, w, out, qkv, mixed, order
):
    seqs = lax.axis_size("seq")
    length, model = tokens.shape
    rows = length // seqs
    wide = w.shape[1]
    wq = mixed.shape[1]
    vmem, hbm = pl.BlockSpec(memory_space=pltpu.VMEM), pl.BlockSpec(memory_space=pl.ANY)
    shape, dma = jax.ShapeDtypeStruct, pltpu.SemaphoreType.DMA
    held = pltpu.VMEM((PIECES, rows // PIECES, model), BF)
    return pl.pallas_call(
        backward_kernel,
        out_shape=(
            shape((length, model), BF),
            shape((rows, model), F32),
            shape((model, wide), BF),
            shape((wq, model), BF),
            shape((1, wide), F32),
            shape((1, model), F32),
        ),
        in_specs=[vmem] * 10 + [hbm] * 7,
        out_specs=(vmem,) * 6,
        scratch_shapes=[pltpu.VMEM(field.shape, field.dtype) for field in (tokens, normed, w, out, qkv, mixed)]
        + [
            pltpu.VMEM((length, model), BF),
            pltpu.VMEM((length, wq), BF),
            pltpu.VMEM((length, wide), BF),
            pltpu.VMEM((length, HEAD_SIZE), F32),
            pltpu.VMEM((length, HEAD_SIZE), F32),
            held, held, held, held,
            dma((6,)), dma((3, PIECES)), dma((3, PIECES)), dma((4, PIECES)), dma((4, PIECES)),
        ],
        cost_estimate=pl.CostEstimate(flops=13 * 10**9, bytes_accessed=30 * 10**6, transcendentals=3 * 10**6),
        compiler_params=pltpu.CompilerParams(
            collective_id=2, has_side_effects=True, vmem_limit_bytes=62 * 2**20
        ),
        name="backward",
    )(
        second_grad, hidden, cotangent, gain_one[None], gain_two[None], logsum, cosine, sine,
        ids[None], ids[:, None], tokens, normed, w, out, qkv, mixed, order,
    )


TILE = 256


def act_kernel(x_ref, w_ref, active_ref, by_gate_ref, by_up_ref, *, tail):
    last = pl.program_id(0) == pl.num_programs(0) - 1

    def body(shift):
        both = jnp.dot(x_ref[...], w_ref[...], preferred_element_type=F32)
        gate, up = both[:, :TILE], both[:, shift : shift + TILE]
        sigma = jax.nn.sigmoid(gate)
        silu = gate * sigma
        active_ref[...] = (silu * up).astype(BF)
        by_gate_ref[...] = (up * sigma * (1.0 + gate * (1.0 - sigma))).astype(BF)
        by_up_ref[...] = silu.astype(BF)

    if tail == TILE:
        body(TILE)
    else:
        pl.when(jnp.logical_not(last))(lambda: body(TILE))
        pl.when(last)(lambda: body(tail))


def act_call(x, both):
    rows, model = x.shape
    units = both.shape[1] // 2
    tiles = -(-units // TILE)
    tail = units - (tiles - 1) * TILE
    tile = pl.BlockSpec((rows, TILE), lambda j: (0, j))
    return pl.pallas_call(
        functools.partial(act_kernel, tail=tail),
        grid=(tiles,),
        out_shape=[jax.ShapeDtypeStruct((rows, units), BF)] * 3,
        in_specs=[
            pl.BlockSpec((rows, model), lambda j: (0, 0)),
            pl.BlockSpec((model, 2 * TILE), lambda j: (0, j)),
        ],
        out_specs=[tile] * 3,
        cost_estimate=pl.CostEstimate(
            flops=4 * rows * model * units,
            bytes_accessed=2 * (both.size + x.size + 3 * rows * units),
            transcendentals=rows * units,
        ),
        compiler_params=pltpu.CompilerParams(vmem_limit_bytes=56 * 2**20),
        name="gate_up",
    )(x, both)


def back_kernel(order_ref, x_ref, w_ref, by_gate_ref, by_up_ref, out_ref, *, tail):
    last = pl.program_id(0) == pl.num_programs(0) - 1

    def body(widths):
        back = jnp.dot(x_ref[...], w_ref[...], preferred_element_type=F32)
        to_gate = (back * by_gate_ref[...].astype(F32)).astype(BF)
        to_up = (back * by_up_ref[...].astype(F32)).astype(BF)
        for i, width in enumerate(widths):
            low = i * TILE
            pair = jnp.concatenate([to_gate[:, low : low + width], to_up[:, low : low + width]], axis=1)
            out_ref[:, 2 * low : 2 * low + 2 * width] = pair

    if tail == (TILE, TILE):
        body(tail)
    else:
        pl.when(jnp.logical_not(last))(lambda: body((TILE, TILE)))
        pl.when(last)(lambda: body(tail))


def back_call(order, x, down, by_gate, by_up):
    rows, model = x.shape
    units = down.shape[1]
    step = 2 * TILE
    tiles = -(-units // step)
    rest = units - (tiles - 1) * step
    tail = (rest,) if rest <= TILE else (TILE, rest - TILE)
    tile = pl.BlockSpec((rows, step), lambda j: (0, j))
    return pl.pallas_call(
        functools.partial(back_kernel, tail=tail),
        grid=(tiles,),
        out_shape=jax.ShapeDtypeStruct((rows, 2 * units), BF),
        in_specs=[
            pl.BlockSpec(memory_space=pl.ANY),
            pl.BlockSpec((rows, model), lambda j: (0, 0)),
            pl.BlockSpec((model, step), lambda j: (0, j)),
            tile,
            tile,
        ],
        out_specs=pl.BlockSpec((rows, 2 * step), lambda j: (0, j)),
        cost_estimate=pl.CostEstimate(
            flops=2 * rows * model * units,
            bytes_accessed=2 * (down.size + x.size + 4 * rows * units),
            transcendentals=0,
        ),
        compiler_params=pltpu.CompilerParams(vmem_limit_bytes=56 * 2**20),
        name="back_down",
    )(order, x, down, by_gate, by_up)


def end_kernel(
    normed_grad_ref, hidden_grad_ref, x_ref, gain_ref, qkv_ref, out_ref, small_ref, feed_ref, hidden_ref,
    input_grad_ref, qkv_out_ref, out_out_ref, small_out_ref, layer_out_ref,
    qkv_got_ref, out_got_ref, small_got_ref,
    qkv_move_ref, out_move_ref, small_move_ref, qkv_came_ref, out_came_ref, small_came_ref,
    came_ref, sums_ref, one_ref, two_ref, came2_ref, sums2_ref, one2_ref, two2_ref,
    sum_send, sum_recv, sum2_send, sum2_recv, core_send, core_recv, ring_send, ring_recv, seq_send, seq_recv,
):
    seqs, dps = lax.axis_size("seq"), lax.axis_size("dp")
    chips = dps // 2
    seq, dpi = lax.axis_index("seq"), lax.axis_index("dp")
    chip, core = dpi // 2, dpi % 2
    ahead = ((chip + 1) % chips) * 2 + core
    behind = ((chip + chips - 1) % chips) * 2 + core
    sibling = chip * 2 + 1 - core
    greet([(seq ^ k, dpi) for k in range(1, seqs)] + [(seq, other) for other in (ahead, behind, sibling)])
    rows = x_ref.shape[0]
    piece = rows // PIECES

    cores = [
        remote(src.at[..., 1 - core, :, :], dst, core_send.at[i], core_recv.at[i], (seq, sibling))
        for i, (src, dst) in enumerate(
            ((qkv_ref, qkv_got_ref), (out_ref, out_got_ref), (small_ref, small_got_ref))
        )
    ]
    for copy in cores:
        copy.start()
    total = SeqSum(normed_grad_ref, rows, came_ref, sums_ref, one_ref, two_ref, (sum_send, sum_recv), dpi, seq)
    total.begin()
    feed = SeqSum(feed_ref, rows, came2_ref, sums2_ref, one2_ref, two2_ref, (sum2_send, sum2_recv), dpi, seq)
    for copy in cores:
        copy.wait_recv()

    def term(which, step):
        parts = [
            qkv_ref[:, which, core].astype(F32) + qkv_got_ref[:, which].astype(F32),
            out_ref[which, core].astype(F32) + out_got_ref[which].astype(F32),
            small_ref[which, core].astype(F32) + small_got_ref[which].astype(F32),
        ]
        if step > 0:
            came = (qkv_came_ref, out_came_ref, small_came_ref)
            parts = [part + field[step - 1].astype(F32) for part, field in zip(parts, came)]
        return parts

    def ring(step):
        return [
            remote(src.at[step], dst.at[step], ring_send.at[i, step], ring_recv.at[i, step], (seq, ahead))
            for i, (src, dst) in enumerate(
                ((qkv_move_ref, qkv_came_ref), (out_move_ref, out_came_ref), (small_move_ref, small_came_ref))
            )
        ]

    def input_piece(c):
        at = pl.ds(c * piece, piece)
        x = x_ref[at, :].astype(F32)
        factor = lax.rsqrt(jnp.mean(x * x, axis=-1, keepdims=True) + EPS)
        unit = x * factor
        scaled = total.take(c) * gain_ref[...]
        grad = scaled - unit * jnp.mean(scaled * unit, axis=-1, keepdims=True)
        input_grad_ref[at, :] = (hidden_grad_ref[at, :] + factor * grad).astype(BF)

    for step in range(chips - 1):
        if step > 0:
            for copy in ring(step - 1):
                copy.wait_recv()
        for field, part in zip((qkv_move_ref, out_move_ref, small_move_ref), term((chip + chips - 1 - step) % chips, step)):
            field[step] = part.astype(BF)
        for copy in ring(step):
            copy.start()
        if step == 0:
            total.middle()
            feed.begin()
        if step == 1:
            for c in range(PIECES):
                input_piece(c)
            feed.middle()
    for c in range(PIECES):
        at = pl.ds(c * piece, piece)
        layer_out_ref[at, :] = (hidden_ref[at, :] + feed.take(c)).astype(BF)
    for copy in ring(chips - 2):
        copy.wait_recv()
    qkv, out, small = term(chip, chips - 1)
    out_out_ref[...] = out
    qkv_move_ref[chips - 1] = qkv.astype(BF)
    small_move_ref[chips - 1] = small.astype(BF)
    last = [
        remote(
            src, dst.at[seq], seq_send.at[i, k], seq_recv.at[i, k], (seq ^ k, dpi)
        )
        for k in range(1, seqs)
        for i, (src, dst) in enumerate(
            ((qkv_move_ref.at[chips - 1, seq ^ k], qkv_out_ref), (small_move_ref.at[chips - 1], small_out_ref))
        )
    ]
    for copy in last:
        copy.start()
    qkv_out_ref[seq] = qkv_move_ref[chips - 1, seq]
    small_out_ref[seq] = small_move_ref[chips - 1]
    total.finish()
    feed.finish()
    for copy in cores + [copy for step in range(chips - 1) for copy in ring(step)]:
        copy.wait_send()
    for copy in last:
        copy.wait()


def end_call(normed_grad, hidden_grad, x, gain, qkv, out, small, feed, hidden):
    seqs, chips, _, share, wide = qkv.shape
    rows, model = x.shape
    vmem = pl.BlockSpec(memory_space=pltpu.VMEM)
    shape, dma = jax.ShapeDtypeStruct, pltpu.SemaphoreType.DMA
    held = pltpu.VMEM((PIECES, rows // PIECES, model), BF)
    blocks = ((seqs, share, wide), (share, model), small.shape[2:])
    return pl.pallas_call(
        end_kernel,
        out_shape=(
            shape((rows, model), BF),
            shape(blocks[0], BF),
            shape(blocks[1], F32),
            shape((seqs,) + blocks[2], BF),
            shape((rows, model), BF),
        ),
        in_specs=[vmem] * 9,
        out_specs=(vmem,) * 5,
        scratch_shapes=[
            pltpu.VMEM((seqs, chips, share, wide), BF),
            pltpu.VMEM((chips, share, model), BF),
            pltpu.VMEM((chips,) + blocks[2], BF),
        ]
        + [pltpu.VMEM((chips,) + block, BF) for block in blocks]
        + [pltpu.VMEM((chips - 1,) + block, BF) for block in blocks]
        + [
            held, held, held, held, held, held, held, held,
            dma((3, PIECES)), dma((3, PIECES)), dma((3, PIECES)), dma((3, PIECES)), dma((3,)), dma((3,)),
            dma((3, chips)), dma((3, chips)), dma((2, seqs)), dma((2, seqs)),
        ],
        cost_estimate=pl.CostEstimate(flops=10**8, bytes_accessed=2 * 10**7, transcendentals=0),
        compiler_params=pltpu.CompilerParams(
            collective_id=3, has_side_effects=True, vmem_limit_bytes=48 * 2**20
        ),
        name="end_sums",
    )(normed_grad, hidden_grad, x, gain[None], qkv, out, small, feed, hidden)


def pair_tiles(left, right):
    units = left.shape[1]
    cuts = list(range(0, units, TILE)) + [units]
    return jnp.concatenate(
        [field[:, low:high] for low, high in zip(cuts[:-1], cuts[1:]) for field in (left, right)], axis=1
    )


def split_tiles(both):
    units = both.shape[1] // 2
    cuts = list(range(0, units, TILE)) + [units]
    spans = list(zip(cuts[:-1], cuts[1:]))
    return (
        jnp.concatenate([both[:, 2 * low : low + high] for low, high in spans], axis=1),
        jnp.concatenate([both[:, low + high : 2 * high] for low, high in spans], axis=1),
    )


def shards(
    inputs,
    block_ids,
    cotangent,
    first_gain,
    query_weight,
    query_bias,
    key_weight,
    key_bias,
    value_weight,
    value_bias,
    output_weight,
    second_gain,
    gate_weight,
    up_weight,
    down_weight,
):
    seqs = lax.axis_size("seq")
    seq = lax.axis_index("seq")
    dps = lax.axis_size("dp")
    dpi = lax.axis_index("dp")
    chips, chip, core = dps // 2, dpi // 2, dpi % 2
    heads = H // seqs
    copies = seqs // KEY_VALUE_HEADS
    wq = heads * HEAD_SIZE
    wide = wq + 2 * HEAD_SIZE
    tokens_here, model = inputs.shape[1:]
    share = first_gain.shape[0]
    kv_share = key_bias.shape[0]
    hidden_units = gate_weight.shape[1]

    small = jnp.concatenate([first_gain, second_gain, query_bias, key_bias, value_bias])
    packed = jnp.concatenate(
        [
            query_weight.reshape(share, seqs, wq),
            jnp.repeat(key_weight.reshape(share, KEY_VALUE_HEADS, HEAD_SIZE), copies, axis=1),
            jnp.repeat(value_weight.reshape(share, KEY_VALUE_HEADS, HEAD_SIZE), copies, axis=1),
        ],
        axis=-1,
    ).transpose(1, 0, 2)
    one = small.shape[0]
    small = jnp.pad(small[None], ((0, 15), (0, -one % 128)))
    tokens, incoming, blocks, smalls, weight_qkv, weight_out = start_call(
        inputs[0], cotangent[0], block_ids.reshape(-1, 128), small, packed, output_weight
    )
    blocks = blocks.reshape(-1)
    weight_qkv = weight_qkv.reshape(model, wide)
    out_head = weight_out[0].reshape(dps * share, model)
    weight_out = weight_out.reshape(model, model)
    smalls = smalls[:, :, 0, :one].transpose(1, 0, 2).astype(F32)
    gain_first = smalls[:, :, :share].reshape(model)
    gain_second = smalls[:, :, share : 2 * share].reshape(model)
    bias_q = lax.dynamic_index_in_dim(smalls, seq, 0, keepdims=False)[:, 2 * share : 3 * share].reshape(wq)
    group = seq // copies
    bias_k = smalls[:, :, 3 * share : 3 * share + kv_share].reshape(KEY_VALUE_HEADS, HEAD_SIZE)
    bias_v = smalls[:, :, 3 * share + kv_share :].reshape(KEY_VALUE_HEADS, HEAD_SIZE)
    bias = jnp.concatenate(
        [
            bias_q,
            lax.dynamic_index_in_dim(bias_k, group, 0, keepdims=False),
            lax.dynamic_index_in_dim(bias_v, group, 0, keepdims=False),
        ]
    )
    length = tokens.shape[0]
    cosine, sine = rope_tables(length)

    gather = lambda field: lax.all_gather(field, "dp", axis=0, tiled=True)
    whole_both = gather(pair_tiles(gate_weight, up_weight))
    tokens, down_turned = lax.optimization_barrier((tokens, down_weight.T))
    whole_down = gather(down_turned)

    normed, qkv, mixed, logsum, hidden, second = attend_call(
        tokens, weight_qkv, bias[None], cosine, sine, blocks, gain_first, gain_second, weight_out
    )
    second_factor = lax.rsqrt(jnp.mean(hidden * hidden, axis=-1, keepdims=True) + EPS)
    own = lambda field: lax.dynamic_slice_in_dim(field, seq * tokens_here, tokens_here, 0)
    active, by_gate, by_up = act_call(second, whole_both)
    scatter = lambda field: lax.psum_scatter(field, "dp", scatter_dimension=0, tiled=True)
    down_grad = tn(incoming, active, BF)
    grad_both = back_call(down_grad, incoming, whole_down, by_gate, by_up)
    down_grad = scatter(down_grad).astype(F32)
    second_sum = nt(grad_both, whole_both)
    gain_two_grad = jnp.sum(second_sum * (hidden * second_factor), axis=0)
    second, second_sum = lax.optimization_barrier((second, second_sum.astype(BF)))
    both_grad = tn(second, grad_both, BF)
    gate_grad, up_grad = split_tiles(scatter(both_grad).astype(F32))
    normed_grad, grad_hidden, qkv_grad, out_weight_grad, bias_grad, gain_one_grad = backward_call(
        second_sum, own(hidden), cotangent[0], gain_first, gain_second, logsum, cosine, sine, blocks,
        tokens, normed, weight_qkv, out_head, qkv, mixed, both_grad,
    )
    bias_grad, gain_one_grad = bias_grad[0], gain_one_grad[0]
    normed_grad, whole_down = lax.optimization_barrier((normed_grad, whole_down))
    out_sum = nt(active, whole_down, BF)

    place = lambda field, count, at: jnp.where(
        (jnp.arange(count) == at)[:, None], field[None], 0.0
    ).reshape(seqs, dps, -1)
    small_grad = jnp.concatenate(
        [
            gain_one_grad.reshape(seqs, dps, share),
            gain_two_grad.reshape(seqs, dps, share),
            place(bias_grad[:wq], seqs, seq),
            place(bias_grad[wq : wq + HEAD_SIZE], KEY_VALUE_HEADS, group),
            place(bias_grad[wq + HEAD_SIZE :], KEY_VALUE_HEADS, group),
        ],
        axis=-1,
    )
    small_rows = -(-seqs * one // wide)
    small_grad = small_grad.transpose(1, 0, 2).reshape(dps, seqs * one).astype(BF)
    small_grad = jnp.pad(small_grad, ((0, 0), (0, small_rows * wide - seqs * one)))
    small_grad = jnp.pad(small_grad.reshape(dps, -1, wide), ((0, 0), (0, 16 - small_rows), (0, 0)))
    input_grad, parts, out_weight_grad, smalls, layer_out = end_call(
        normed_grad, grad_hidden, inputs[0], gain_first,
        qkv_grad.reshape(seqs, chips, 2, share, wide),
        out_weight_grad.reshape(chips, 2, share, model),
        small_grad.reshape(chips, 2, 16, wide),
        out_sum, own(hidden),
    )
    smalls = smalls[:, :small_rows].reshape(seqs, -1)[:, : seqs * one].reshape(seqs, seqs, one)
    small_sum = jnp.sum(
        lax.dynamic_index_in_dim(smalls, seq, 1, keepdims=False).astype(F32), axis=0
    )
    query_weight_grad = jnp.concatenate([part[:share, :wq] for part in parts], axis=1).astype(F32)
    pairs = [
        sum(part[:share, wq:].astype(F32) for part in parts[g * copies : (g + 1) * copies])
        for g in range(KEY_VALUE_HEADS)
    ]
    key_weight_grad = jnp.concatenate([pair[:, :HEAD_SIZE] for pair in pairs], axis=1)
    value_weight_grad = jnp.concatenate([pair[:, HEAD_SIZE:] for pair in pairs], axis=1)
    gain_one_grad, gain_two_grad, query_bias_grad, key_bias_grad, value_bias_grad = jnp.split(
        small_sum, [share, 2 * share, 3 * share, 3 * share + kv_share]
    )

    return (
        layer_out[None],
        input_grad[None],
        gain_one_grad,
        query_weight_grad,
        query_bias_grad,
        key_weight_grad,
        key_bias_grad,
        value_weight_grad,
        value_bias_grad,
        out_weight_grad,
        gain_two_grad,
        gate_grad,
        up_grad,
        down_grad.T,
    )


def solution(mesh):
    tokens = P("dp", "seq", None)
    whole = P(("seq", "dp"))
    matrix = P(("seq", "dp"), None)
    feed = P("dp", "seq")
    in_specs = (
        tokens,
        P("dp", "seq"),
        tokens,
        whole,
        matrix,
        whole,
        matrix,
        whole,
        matrix,
        whole,
        matrix,
        whole,
        feed,
        feed,
        P("seq", "dp"),
    )
    out_specs = (
        tokens,
        tokens,
        whole,
        matrix,
        whole,
        matrix,
        whole,
        matrix,
        whole,
        matrix,
        whole,
        feed,
        feed,
        P("seq", "dp"),
    )
    return jax.shard_map(shards, mesh=mesh, in_specs=in_specs, out_specs=out_specs, check_vma=False)
```

```python
import functools

import jax
import jax.numpy as jnp
import numpy as np
from jax import lax
from jax.experimental import pallas as pl
from jax.experimental.pallas import tpu as pltpu
from jax.sharding import PartitionSpec as P

H = 12
KEY_VALUE_HEADS = 2
HEAD_SIZE = 128
EPS = 1e-06
THETA = 1000000.0
SCALE = HEAD_SIZE ** (-0.5)
BF = jnp.bfloat16
F32 = jnp.float32


def dot(a, b, dims, out=F32):
    return lax.dot_general(a, b, (dims, ((), ())), preferred_element_type=F32).astype(out)


def nn(a, b, out=F32):
    return dot(a, b, ((1,), (0,)), out)


def nt(a, b, out=F32):
    return dot(a, b, ((1,), (1,)), out)


def tn(a, b, out=F32):
    return dot(a, b, ((0,), (0,)), out)


def rope_tables(length):
    exponent = np.arange(0, HEAD_SIZE, 2).astype(np.float32) / np.float32(HEAD_SIZE)
    freqs = np.float32(THETA) ** (-exponent)
    angles = np.arange(length).astype(np.float32)[:, None] * freqs[None, :]
    cosine, sine = np.cos(angles), np.sin(angles)
    return (
        jnp.asarray(np.concatenate([cosine, cosine], axis=-1), F32),
        jnp.asarray(np.concatenate([-sine, sine], axis=-1), F32),
    )


def remote(src, dst, send, recv, where):
    return pltpu.make_async_remote_copy(
        src_ref=src, dst_ref=dst, send_sem=send, recv_sem=recv,
        device_id=where, device_id_type=pl.DeviceIdType.MESH,
    )


def greet(partners):
    barrier = pltpu.get_barrier_semaphore()
    for partner in partners:
        pl.semaphore_signal(barrier, inc=1, device_id=partner, device_id_type=pl.DeviceIdType.MESH)
    pl.semaphore_wait(barrier, len(partners))


def far_sends(field, half, seq, dpi, send, recv):
    def rows(k, low):
        return field.at[pl.ds(pl.multiple_of((seq ^ k) * 2 * half + low, half), half)]

    return [
        remote(rows(2, 0), rows(2, 0), send.at[0], recv.at[0], (seq ^ 1, dpi)),
        remote(rows(1, half), rows(1, half), send.at[1], recv.at[1], (seq ^ 2, dpi)),
    ]


def start_kernel(
    x_in, c_in, ids_in, small_in, pack_in, out_in,
    x_out, c_out, ids_out, small_out, pack_out, out_out,
    local_sem, seq_send, seq_recv, far_send, far_recv, ring_send, ring_recv, core_send, core_recv,
    out_send, out_recv, slot_send, slot_recv,
):
    seqs, dps = lax.axis_size("seq"), lax.axis_size("dp")
    chips = dps // 2
    seq, dpi = lax.axis_index("seq"), lax.axis_index("dp")
    chip, core = dpi // 2, dpi % 2
    sibling = chip * 2 + 1 - core
    others = [((chip + h) % chips) * 2 + core for h in range(1, chips)]
    greet([(seq ^ k, dpi) for k in range(1, seqs)] + [(seq, other) for other in others + [sibling]])

    rows = x_in.shape[0]
    half = rows // 2

    def to_slots(i, src, dst, slots):
        return [remote(src, dst, seq_send.at[i, k], seq_recv.at[i, k], (seq ^ k, dpi)) for k in slots]

    def block(index, low=0, count=rows):
        return pl.ds(pl.multiple_of(index * rows + low, half), count)

    small_sends = to_slots(0, small_in, small_out.at[dpi, seq], range(1, seqs))
    pack_sends = [
        remote(
            pack_in.at[seq ^ k], pack_out.at[seq, dpi], seq_send.at[1, k], seq_recv.at[1, k], (seq ^ k, dpi)
        )
        for k in range(1, seqs)
    ]
    id_sends = to_slots(2, ids_in, ids_out.at[seq], range(1, seqs))
    x_sends = to_slots(3, x_in, x_out.at[block(seq)], (1, 2))
    c_sends = to_slots(4, c_in, c_out.at[block(seq)], (1, 2))
    locals_ = [
        pltpu.make_async_copy(small_in, small_out.at[dpi, seq], local_sem.at[0]),
        pltpu.make_async_copy(pack_in.at[seq], pack_out.at[seq, dpi], local_sem.at[1]),
        pltpu.make_async_copy(out_in, out_out.at[0, dpi], local_sem.at[2]),
        pltpu.make_async_copy(ids_in, ids_out.at[seq], local_sem.at[3]),
        pltpu.make_async_copy(x_in, x_out.at[block(seq)], local_sem.at[4]),
        pltpu.make_async_copy(c_in, c_out.at[block(seq)], local_sem.at[5]),
    ]
    def fields(at, which):
        every = (out_out.at[0, at], small_out.at[at], pack_out.at[:, at])
        return [(i, every[i]) for i in which]

    def hop_sends(hop, which):
        to = ((chip + chips - hop) % chips) * 2 + core
        return [
            remote(out_in if i == 0 else field, field, ring_send.at[i, hop], ring_recv.at[i, hop], (seq, to))
            for i, field in fields(dpi, which)
        ]

    def core_sends(hop, which=(0, 1, 2)):
        at = ((chip + hop) % chips) * 2 + core
        return [
            remote(field, field, core_send.at[i, hop], core_recv.at[i, hop], (seq, sibling))
            for i, field in fields(at, which)
        ]

    def out_sends(hop):
        at = ((chip + hop) % chips) * 2 + core
        src = out_out.at[0, at] if hop else out_in
        return [
            remote(src, out_out.at[k, at], out_send.at[k, hop], out_recv.at[k, hop], (seq ^ k, dpi))
            for k in range(1, seqs)
        ]

    order = sorted(range(1, chips), key=lambda hop: min(hop, chips - hop))
    flying, outs = [], []
    for hop in order:
        flying += hop_sends(hop, (0,))
    first = small_sends + pack_sends + locals_[:3] + x_sends + id_sends + locals_[3:]
    for copy in flying + first:
        copy.start()
    for copy in locals_[:3] + small_sends + pack_sends:
        copy.wait()
    more = [copy for hop in order for copy in hop_sends(hop, (1, 2))]
    for copy in more:
        copy.start()
    flying += more
    for hop in [0] + order:
        if hop > 0:
            for copy in hop_sends(hop, (0,)):
                copy.wait_recv()
        cores, more = core_sends(hop, (0,)), out_sends(hop)
        for copy in cores + more:
            copy.start()
        flying += cores
        outs += more
    for copy in x_sends:
        copy.wait()
    far_x = far_sends(x_out, half, seq, dpi, far_send.at[0], far_recv.at[0])
    for copy in far_x + c_sends:
        copy.start()
    for hop in [0] + order:
        if hop > 0:
            for copy in hop_sends(hop, (1, 2)):
                copy.wait_recv()
        cores = core_sends(hop, (1, 2))
        for copy in cores:
            copy.start()
        flying += cores
    for copy in c_sends:
        copy.wait()
    far_c = far_sends(c_out, half, seq, dpi, far_send.at[1], far_recv.at[1])
    for copy in far_c:
        copy.start()
    for copy in outs:
        copy.wait_recv()
    slots = [
        remote(
            out_out.at[k, ((chip + hop) % chips) * 2 + core], out_out.at[k, ((chip + hop) % chips) * 2 + core],
            slot_send.at[k, hop], slot_recv.at[k, hop], (seq, sibling),
        )
        for k in range(1, seqs)
        for hop in range(chips)
    ]
    for copy in slots:
        copy.start()
    for copy in flying + outs:
        copy.wait_send()
    for hop in range(chips):
        for copy in core_sends(hop):
            copy.wait_recv()
    for copy in slots + far_x + far_c + id_sends + locals_[3:]:
        copy.wait()


def start_call(x, c, ids, small, pack, out):
    seqs, dps = lax.axis_size("seq"), lax.axis_size("dp")
    chips = dps // 2
    share, wide = pack.shape[1:]
    any_space = pl.BlockSpec(memory_space=pl.ANY)
    shapes = (
        jax.ShapeDtypeStruct((seqs * x.shape[0], x.shape[1]), x.dtype),
        jax.ShapeDtypeStruct((seqs * c.shape[0], c.shape[1]), c.dtype),
        jax.ShapeDtypeStruct((seqs,) + ids.shape, ids.dtype),
        jax.ShapeDtypeStruct((dps, seqs) + small.shape, small.dtype),
        jax.ShapeDtypeStruct((seqs, dps, share, wide), pack.dtype),
        jax.ShapeDtypeStruct((seqs, dps) + out.shape, out.dtype),
    )
    dma = pltpu.SemaphoreType.DMA
    return pl.pallas_call(
        start_kernel,
        out_shape=shapes,
        in_specs=[pl.BlockSpec(memory_space=pltpu.VMEM)] * 6,
        out_specs=(any_space,) * 6,
        scratch_shapes=[
            dma((6,)), dma((5, seqs)), dma((5, seqs)), dma((2, 2)), dma((2, 2)),
            dma((3, chips)), dma((3, chips)), dma((3, chips)), dma((3, chips)),
            dma((seqs, chips)), dma((seqs, chips)), dma((seqs, chips)), dma((seqs, chips)),
        ],
        compiler_params=pltpu.CompilerParams(collective_id=0, has_side_effects=True),
        name="start_gather",
    )(x, c, ids, small, pack, out)


def attend_kernel(
    x_ref, w_ref, bias_ref, cos_ref, sin_ref, ids_row_ref, ids_col_ref, gain_one_ref, gain_two_ref, out_ref,
    normed_ref, qkv_ref, mixed_ref, lse_ref, hidden_ref, second_ref,
    all_ref, send_sem, recv_sem,
):
    seqs = lax.axis_size("seq")
    seq, dpi = lax.axis_index("seq"), lax.axis_index("dp")
    greet([(seq ^ k, dpi) for k in range(1, seqs)])
    length, model = x_ref.shape
    wq = mixed_ref.shape[1]
    heads = wq // HEAD_SIZE
    rows = length // seqs
    @pl.loop(0, seqs)
    def _(i):
        at = pl.ds(pl.multiple_of(i * rows, rows), rows)
        x = x_ref[at, :].astype(F32)
        factor = lax.rsqrt(jnp.mean(x * x, axis=-1, keepdims=True) + EPS)
        normed_ref[at, :] = (x * factor * gain_one_ref[...]).astype(BF)

    @pl.loop(0, 2)
    def _(i):
        at = pl.ds(pl.multiple_of(i * 2 * rows, 2 * rows), 2 * rows)
        pre = jnp.dot(normed_ref[at, :], w_ref[...], preferred_element_type=F32) + bias_ref[...]
        cosine, sine = cos_ref[at, :], sin_ref[at, :]
        for h in range(heads + 1):
            u = pre[:, h * HEAD_SIZE : (h + 1) * HEAD_SIZE]
            turned = pltpu.roll(u, HEAD_SIZE // 2, 1)
            qkv_ref[at, h * HEAD_SIZE : (h + 1) * HEAD_SIZE] = (u * cosine + turned * sine).astype(BF)
        qkv_ref[at, wq + HEAD_SIZE :] = pre[:, wq + HEAD_SIZE :].astype(BF)

    copies = []
    for t in range(seqs):
        at = slice(t * rows, (t + 1) * rows)
        reach = min(t + 2, seqs) * rows
        keys = qkv_ref[:reach, wq : wq + HEAD_SIZE]
        values = qkv_ref[:reach, wq + HEAD_SIZE :]
        allowed = ids_row_ref[:, :reach] <= ids_col_ref[at, :]
        sums = []
        for h in range(heads):
            lanes = slice(h * HEAD_SIZE, (h + 1) * HEAD_SIZE)
            scores = nt(qkv_ref[at, lanes], keys) * SCALE
            scores = jnp.where(allowed, scores, -1000000000.0)
            peak = jnp.max(scores, axis=-1, keepdims=True)
            raised = jnp.exp(scores - peak)
            total = jnp.sum(raised, axis=-1, keepdims=True)
            low = (raised * (1.0 / total)).astype(BF)
            mixed_ref[at, lanes] = nn(low, values).astype(BF)
            sums.append(peak + jnp.log(total))
        lse_ref[at, :heads] = jnp.concatenate(sums, axis=1)
        more = [
            remote(
                mixed_ref.at[pl.ds(t * rows, rows)], all_ref.at[pl.ds(t * rows, rows), pl.ds(k * wq, wq)],
                send_sem.at[k, t], recv_sem.at[k, t], (seq ^ k, dpi),
            )
            for k in range(1, seqs)
        ]
        for copy in more:
            copy.start()
        copies.append(more)
        all_ref[at, :wq] = mixed_ref[at, :]

    for t in range(seqs):
        at = slice(t * rows, (t + 1) * rows)
        for copy in copies[t]:
            copy.wait_recv()
        hidden = x_ref[at, :].astype(F32) + nn(all_ref[at, :], out_ref[...])
        hidden_ref[at, :] = hidden
        factor = lax.rsqrt(jnp.mean(hidden * hidden, axis=-1, keepdims=True) + EPS)
        second_ref[at, :] = (hidden * factor * gain_two_ref[...]).astype(BF)
    for t in range(seqs):
        for copy in copies[t]:
            copy.wait_send()


def attend_call(x, w, bias, cosine, sine, ids, gain_one, gain_two, out):
    seqs = lax.axis_size("seq")
    length, model = x.shape
    wide = w.shape[1]
    wq = wide - 2 * HEAD_SIZE
    vmem = pl.BlockSpec(memory_space=pltpu.VMEM)
    shape = jax.ShapeDtypeStruct
    return pl.pallas_call(
        attend_kernel,
        out_shape=(
            shape((length, model), BF),
            shape((length, wide), BF),
            shape((length, wq), BF),
            shape((length, 128), F32),
            shape((length, model), F32),
            shape((length, model), BF),
        ),
        in_specs=[vmem] * 10,
        out_specs=(vmem,) * 6,
        scratch_shapes=[
            pltpu.VMEM((length, seqs * wq), BF),
            pltpu.SemaphoreType.DMA((seqs, seqs)),
            pltpu.SemaphoreType.DMA((seqs, seqs)),
        ],
        cost_estimate=pl.CostEstimate(flops=9 * 10**9, bytes_accessed=30 * 10**6, transcendentals=3 * 10**6),
        compiler_params=pltpu.CompilerParams(
            collective_id=1, has_side_effects=True, vmem_limit_bytes=60 * 2**20
        ),
        name="attend",
    )(x, w, bias, cosine, sine, ids[None], ids[:, None], gain_one[None], gain_two[None], out)


PIECES = 4
READY = 6
SUMMED = 4


def slot_rows(index, rows):
    return pl.ds(pl.multiple_of(index * rows, rows), rows)


class SeqSum:
    def __init__(self, field, rows, came, sums, from_one, from_two, sems, dpi, seq):
        self.field, self.rows, self.piece = field, rows, rows // PIECES
        self.came, self.sums, self.got = came, sums, {1: from_one, 2: from_two}
        self.send, self.recv = sems
        self.dpi, self.seq = dpi, seq
        self.started = []

    def at(self, k, c):
        start = (self.seq ^ k) * self.rows + c * self.piece
        return pl.ds(pl.multiple_of(start, self.piece), self.piece)

    def pass_on(self, c):
        by = 1 + c % 2
        return remote(
            self.field.at[self.at(3, c)], self.came.at[c], self.send.at[0, c], self.recv.at[0, c], (self.seq ^ by, self.dpi)
        )

    def direct(self, k, c):
        late = (k == 2) == (c % 2 == 0)
        src = self.sums.at[c] if late else self.field.at[self.at(k, c)]
        return remote(src, self.got[k].at[c], self.send.at[k, c], self.recv.at[k, c], (self.seq ^ k, self.dpi))

    def begin(self):
        for c in range(PIECES):
            self.pass_on(c).start()
            self.direct(1 + c % 2, c).start()

    def middle(self):
        for c in range(PIECES):
            k = 2 - c % 2
            self.pass_on(c).wait_recv()
            own = self.field[self.at(k, c), :].astype(F32)
            self.sums[c] = (self.came[c].astype(F32) + own).astype(BF)
            self.direct(k, c).start()

    def take(self, c):
        for k in (1, 2):
            self.direct(k, c).wait_recv()
        total = self.field[self.at(0, c), :].astype(F32) + self.got[1][c].astype(F32)
        return total + self.got[2][c].astype(F32)

    def finish(self):
        for c in range(PIECES):
            self.pass_on(c).wait_send()
            for k in (1, 2):
                self.direct(k, c).wait_send()


def backward_kernel(
    second_grad_ref, feed_ref, cotangent_ref, gain_one_ref, gain_two_ref, lse_ref, cos_ref, sin_ref,
    ids_row_ref, ids_col_ref, hidden_hbm, tokens_hbm, normed_hbm, w_hbm, out_hbm, qkv_hbm, mixed_hbm,
    normed_grad_ref, hidden_grad_ref, w_grad_ref, out_grad_ref, bias_grad_ref, gain_grad_ref, gain_two_grad_ref, layer_out_ref,
    hidden_ref, tokens_ref, normed_ref, w_ref, out_ref, qkv_ref, mixed_ref,
    branch_ref, mixed_grad_ref, pre_grad_ref, key_grad_ref, value_grad_ref,
    came_ref, sums_ref, one_ref, two_ref, came2_ref, sums2_ref, one2_ref, two2_ref,
    load_sem, sum_send, sum_recv, sum2_send, sum2_recv, branch_send, branch_recv,
):
    seqs = lax.axis_size("seq")
    seq, dpi = lax.axis_index("seq"), lax.axis_index("dp")
    length, model = second_grad_ref.shape
    rows = length // seqs
    piece = rows // PIECES
    wq = mixed_ref.shape[1]
    heads = wq // HEAD_SIZE
    loads = [
        pltpu.make_async_copy(src, dst, load_sem.at[i])
        for i, (src, dst) in enumerate(
            (
                (hidden_hbm.at[slot_rows(seq, rows)], hidden_ref),
                (out_hbm, out_ref), (qkv_hbm, qkv_ref), (w_hbm, w_ref),
                (tokens_hbm, tokens_ref), (normed_hbm, normed_ref), (mixed_hbm, mixed_ref),
            )
        )
    ]
    for load in loads:
        load.start()
    greet([(seq ^ k, dpi) for k in range(1, seqs)])

    total = SeqSum(second_grad_ref, rows, came_ref, sums_ref, one_ref, two_ref, (sum_send, sum_recv), dpi, seq)
    total.begin()
    loads[0].wait()
    total.middle()

    def branch_at(k, c):
        start = (seq ^ k) * rows + c * piece
        return branch_ref.at[pl.ds(pl.multiple_of(start, piece), piece)]

    def branch_copy(k, c):
        if k < 3:
            return remote(
                branch_at(0, c), branch_at(0, c), branch_send.at[k, c], branch_recv.at[k, c], (seq ^ k, dpi)
            )
        came, to = (2, 1) if c % 2 == 0 else (1, 2)
        return remote(
            branch_at(came, c), branch_at(came, c), branch_send.at[3, c], branch_recv.at[3, c], (seq ^ to, dpi)
        )

    gain_two_grad_ref[...] = jnp.zeros_like(gain_two_grad_ref)
    for c in range(PIECES):
        at = pl.ds(c * piece, piece)
        grad = total.take(c)
        hidden = hidden_ref[at, :]
        factor = lax.rsqrt(jnp.mean(hidden * hidden, axis=-1, keepdims=True) + EPS)
        unit = hidden * factor
        gain_two_grad_ref[...] += jnp.sum(grad * unit, axis=0, keepdims=True)
        scaled = grad * gain_two_ref[...]
        grad = cotangent_ref[at, :].astype(F32) + factor * (
            scaled - unit * jnp.mean(scaled * unit, axis=-1, keepdims=True)
        )
        hidden_grad_ref[at, :] = grad
        start = pl.multiple_of(seq * rows + c * piece, piece)
        branch_ref[pl.ds(start, piece), :] = grad.astype(BF)
        for k in (1, 2):
            branch_copy(k, c).start()
    total.finish()
    for load in loads[1:3]:
        load.wait()

    key_grad_ref[...] = jnp.zeros_like(key_grad_ref)
    value_grad_ref[...] = jnp.zeros_like(value_grad_ref)

    def rot_back(w, at):
        return w * cos_ref[at, :] + pltpu.roll(w * sin_ref[at, :], HEAD_SIZE // 2, 1)

    def attend_back(k):
        at = slot_rows(seq ^ k, rows)
        mixed_grad_ref[at, :] = nt(branch_ref[at, :], out_ref[...]).astype(BF)
        allowed = ids_row_ref[...] <= ids_col_ref[at, :]
        keys = qkv_ref[:, wq : wq + HEAD_SIZE]
        values = qkv_ref[:, wq + HEAD_SIZE :]
        for h in range(heads):
            lanes = slice(h * HEAD_SIZE, (h + 1) * HEAD_SIZE)
            queries = qkv_ref[at, lanes]
            grad = mixed_grad_ref[at, lanes]
            scores = jnp.where(allowed, nt(queries, keys) * SCALE, -1000000000.0)
            probs = jnp.exp(scores - lse_ref[at, h : h + 1])
            prob_grad = nt(grad, values)
            delta = jnp.sum(probs * prob_grad, axis=-1, keepdims=True)
            score_grad = (probs * (prob_grad - delta)).astype(BF)
            pre_grad_ref[at, lanes] = rot_back(nn(score_grad, keys) * SCALE, at).astype(BF)
            key_grad_ref[...] += tn(score_grad, queries)
            value_grad_ref[...] += tn(probs.astype(BF), grad)

    attend_back(0)
    for k in (1, 2):
        for c in range(PIECES):
            branch_copy(k, c).wait_recv()
            if (k == 2) == (c % 2 == 0):
                branch_copy(3, c).start()
        attend_back(k)
    for c in range(PIECES):
        branch_copy(3, c).wait_recv()
    feed = SeqSum(feed_ref, rows, came2_ref, sums2_ref, one2_ref, two2_ref, (sum2_send, sum2_recv), dpi, seq)
    feed.begin()
    attend_back(3)
    feed.middle()
    for c in range(PIECES):
        for k in (1, 2, 3):
            branch_copy(k, c).wait_send()

    every = pl.ds(0, length)
    pre_grad_ref[:, wq : wq + HEAD_SIZE] = rot_back(key_grad_ref[...] * SCALE, every).astype(BF)
    pre_grad_ref[:, wq + HEAD_SIZE :] = value_grad_ref[...].astype(BF)
    bias_grad_ref[...] = jnp.sum(pre_grad_ref[...].astype(F32), axis=0, keepdims=True)
    for load in loads[3:]:
        load.wait()
    gain_grad_ref[...] = jnp.zeros_like(gain_grad_ref)

    @pl.loop(0, seqs)
    def _(i):
        at = slot_rows(i, rows)
        grad = nt(pre_grad_ref[at, :], w_ref[...])
        x = tokens_ref[at, :].astype(F32)
        factor = lax.rsqrt(jnp.mean(x * x, axis=-1, keepdims=True) + EPS)
        gain_grad_ref[...] += jnp.sum(grad * (x * factor), axis=0, keepdims=True)
        normed_grad_ref[at, :] = grad.astype(BF)

    @pl.loop(0, model // wq)
    def _(i):
        lanes = pl.ds(pl.multiple_of(i * wq, HEAD_SIZE), wq)
        w_grad_ref[pl.ds(pl.multiple_of(i * wq, HEAD_SIZE), wq), :] = tn(normed_ref[:, lanes], pre_grad_ref[...]).astype(BF)
        out_grad_ref[:, lanes] = tn(mixed_ref[...], branch_ref[:, lanes]).astype(BF)

    for c in range(PIECES):
        at = pl.ds(c * piece, piece)
        layer_out_ref[at, :] = (hidden_ref[at, :] + feed.take(c)).astype(BF)
    feed.finish()


def backward_call(
    second_grad, feed, cotangent, gain_one, gain_two, logsum, cosine, sine, ids, hidden, tokens, normed, w, out, qkv, mixed
):
    seqs = lax.axis_size("seq")
    length, model = tokens.shape
    rows = length // seqs
    wide = w.shape[1]
    wq = mixed.shape[1]
    vmem, hbm = pl.BlockSpec(memory_space=pltpu.VMEM), pl.BlockSpec(memory_space=pl.ANY)
    shape, dma = jax.ShapeDtypeStruct, pltpu.SemaphoreType.DMA
    held = pltpu.VMEM((PIECES, rows // PIECES, model), BF)
    return pl.pallas_call(
        backward_kernel,
        out_shape=(
            shape((length, model), BF),
            shape((rows, model), F32),
            shape((model, wide), BF),
            shape((wq, model), BF),
            shape((1, wide), F32),
            shape((1, model), F32),
            shape((1, model), F32),
            shape((rows, model), BF),
        ),
        in_specs=[vmem] * 10 + [hbm] * 7,
        out_specs=(vmem,) * 8,
        scratch_shapes=[pltpu.VMEM((rows, model), F32)]
        + [pltpu.VMEM(field.shape, field.dtype) for field in (tokens, normed, w, out, qkv, mixed)]
        + [
            pltpu.VMEM((length, model), BF),
            pltpu.VMEM((length, wq), BF),
            pltpu.VMEM((length, wide), BF),
            pltpu.VMEM((length, HEAD_SIZE), F32),
            pltpu.VMEM((length, HEAD_SIZE), F32),
            held, held, held, held, held, held, held, held,
            dma((7,)), dma((3, PIECES)), dma((3, PIECES)), dma((3, PIECES)), dma((3, PIECES)),
            dma((4, PIECES)), dma((4, PIECES)),
        ],
        cost_estimate=pl.CostEstimate(flops=13 * 10**9, bytes_accessed=30 * 10**6, transcendentals=3 * 10**6),
        compiler_params=pltpu.CompilerParams(
            collective_id=2, has_side_effects=True, vmem_limit_bytes=62 * 2**20
        ),
        name="backward",
    )(
        second_grad, feed, cotangent, gain_one[None], gain_two[None], logsum, cosine, sine,
        ids[None], ids[:, None], hidden, tokens, normed, w, out, qkv, mixed,
    )


TILE = 256


class ChipGather:
    def __init__(self, whole, columns, sems, seq, dpi, chips, own=None):
        self.whole, self.columns, self.sems, self.own = whole, columns, sems, own
        self.seq, self.dpi, self.chips = seq, dpi, chips
        self.chip, self.core = dpi // 2, dpi % 2

    def copy(self, kind, s, chip, core, to):
        block = self.whole.at[chip * 2 + core, :, self.columns]
        send, recv = self.sems
        src = block if s or self.own is None else self.own.at[:, self.columns]
        return remote(src, block, send.at[kind, s], recv.at[kind, s], (self.seq, to))

    def copies(self, s):
        z, c = self.chip, self.core
        low, high = z - s, z + s
        sibling = z * 2 + 1 - c
        out = [
            ((low >= 0) & (z < self.chips - 1), self.copy(0, s, low, c, self.dpi + 2)),
            ((high < self.chips) & (z > 0), self.copy(1, s, high, c, self.dpi - 2)),
            (low >= 0, self.copy(2, s, low, c, sibling)),
        ]
        if s > 0:
            out.append((high < self.chips, self.copy(3, s, high, c, sibling)))
        return out

    def send(self, s):
        for condition, copy in self.copies(s):
            pl.when(condition)(copy.start)

    def sent(self, s):
        for condition, copy in self.copies(s):
            pl.when(condition)(copy.wait_send)

    def came(self, s):
        z, c = self.chip, self.core
        pl.when(z - s >= 0)(self.copy(0, s - 1, z - s, c, self.dpi).wait_recv)
        pl.when(z + s < self.chips)(self.copy(1, s - 1, z + s, c, self.dpi).wait_recv)

    def came_across(self, s):
        z, c = self.chip, self.core
        pl.when(z - s >= 0)(self.copy(2, s, z - s, 1 - c, self.dpi).wait_recv)
        if s > 0:
            pl.when(z + s < self.chips)(self.copy(3, s, z + s, 1 - c, self.dpi).wait_recv)


class ChipScatter:
    def __init__(self, terms, got, held, sems, seq, dpi, chips):
        self.terms, self.got, self.held, self.sems = terms, got, held, sems
        self.seq, self.dpi, self.chips = seq, dpi, chips
        self.chip, self.core = dpi // 2, dpi % 2

    def give(self):
        send, recv = self.sems
        return remote(
            self.terms.at[:, 1 - self.core], self.got, send.at[2, 0], recv.at[2, 0], (self.seq, self.chip * 2 + 1 - self.core)
        )

    def up(self, d, to, field=None):
        send, recv = self.sems
        return remote((field or self.held).at[d], self.held.at[d], send.at[0, d], recv.at[0, d], (self.seq, to))

    def down(self, d, to, last, field=None):
        send, recv = self.sems
        slot = self.chips if last else d
        return remote((field or self.held).at[d], self.held.at[slot], send.at[1, d], recv.at[1, d], (self.seq, to))

    def each(self, body):
        size = self.got.shape[1]
        chunk = 16 if size % 16 == 0 else size

        @pl.loop(0, size // chunk)
        def _(i):
            body(pl.ds(pl.multiple_of(i * chunk, chunk), chunk))

    def take(self):
        self.give().wait()

        @pl.loop(0, self.chips)
        def _(d):
            def body(rows):
                own = self.terms[d, self.core, rows, :].astype(F32)
                self.got[d, rows, :] = (own + self.got[d, rows, :].astype(F32)).astype(BF)

            self.each(body)

    def add(self, d):
        def body(rows):
            total = self.got[d, rows, :].astype(F32) + self.held[d, rows, :].astype(F32)
            self.held[d, rows, :] = total.astype(BF)

        self.each(body)

    def step(self, r):
        z, chips = self.chip, self.chips

        @pl.when(z + r < chips)
        def _():
            d = z + r

            @pl.when(z > 0)
            def _():
                self.up(d, self.dpi).wait_recv()
                self.add(d)
                self.up(d, self.dpi + 2).start()

            @pl.when(z == 0)
            def _():
                self.up(d, self.dpi + 2, self.got).start()

        @pl.when(z - r >= 0)
        def _():
            d = z - r

            @pl.when(z < chips - 1)
            def _():
                self.down(d, self.dpi, False).wait_recv()
                self.add(d)
                self.down(d, self.dpi - 2, r == 1).start()

            @pl.when(z == chips - 1)
            def _():
                self.down(d, self.dpi - 2, r == 1, self.got).start()

    def finish(self, result):
        z, chips = self.chip, self.chips
        pl.when(z > 0)(lambda: self.up(z, self.dpi).wait_recv())
        pl.when(z < chips - 1)(lambda: self.down(z, self.dpi, True).wait_recv())

        def body(rows):
            total = self.got[z, rows, :].astype(F32)
            total += jnp.where(z > 0, self.held[z, rows, :].astype(F32), 0.0)
            result[rows, :] = total + jnp.where(z < chips - 1, self.held[chips, rows, :].astype(F32), 0.0)

        self.each(body)
        for r in range(1, chips):
            pl.when(z + r < chips)(lambda: self.up(z + r, self.dpi + 2).wait_send())
            pl.when(z - r >= 0)(lambda: self.down(z - r, self.dpi - 2, r == 1).wait_send())


def feed_kernel(
    second_ref, incoming_ref, first_hbm, own_ref,
    whole_out, out_hbm, grad_hbm, rest_hbm, mine_ref,
    second_turned_ref, incoming_turned_ref, w_ref, terms_ref, got_ref, held_ref, active_ref, both_ref, out_ref, grad_ref, stage_ref,
    load_sem, store_sem, stage_sem, own_sem, ahead_send, ahead_recv, sum_send, sum_recv,
    *, tiles, ready, summed,
):
    dps = lax.axis_size("dp")
    chips = dps // 2
    seq, dpi = lax.axis_index("seq"), lax.axis_index("dp")
    chip, core = dpi // 2, dpi % 2
    length, model = second_ref.shape
    width = 3 * TILE
    later = own_ref.shape[1] // width if ready < tiles else 0
    loose = ready >= chips + 2
    above, below = ((chip + 1) % chips) * 2 + core, ((chip + chips - 1) % chips) * 2 + core
    greet([(seq, above), (seq, below), (seq, chip * 2 + 1 - core)])

    def columns(t):
        return pl.ds(pl.multiple_of(t * width, width), width)

    def load(t, source=first_hbm):
        return pltpu.make_async_copy(source.at[:, :, columns(t)], w_ref.at[t % 2], load_sem.at[t % 2])

    def start_load(t):
        pl.when(t < ready)(lambda: load(t).start())
        if later > 0:
            first = columns(t - ready)
            ahead = pltpu.make_async_copy(whole_out.at[:, :, first], w_ref.at[t % 2], load_sem.at[t % 2])
            pl.when(within(t, ready, tiles))(ahead.start)

    def store(t):
        return pltpu.make_async_copy(
            terms_ref.at[t % 3], rest_hbm.at[:, :, :, columns(t - summed)], store_sem.at[t % 3]
        )

    def gather(q):
        return ChipGather(
            whole_out, columns(q), (ahead_send.at[q], ahead_recv.at[q]), seq, dpi, chips, own_ref
        )

    def scatter(t):
        return ChipScatter(
            terms_ref.at[t % 3], got_ref.at[t], held_ref.at[t], (sum_send.at[t], sum_recv.at[t]), seq, dpi, chips
        )

    def within(value, low, high):
        return (value >= low) & (value < high)

    load(0).start()
    own = pltpu.make_async_copy(own_ref, whole_out.at[dpi], own_sem)
    own.start()
    out_ref[...] = jnp.zeros_like(out_ref)
    grad_ref[...] = jnp.zeros_like(grad_ref)

    @pl.loop(0, length // TILE)
    def _(i):
        at = slot_rows(i, TILE)
        second_turned_ref[:, at] = second_ref[at, :].T
        incoming_turned_ref[:, at] = incoming_ref[at, :].T

    own.wait()
    far = list(range(chips - 1, 0, -1))
    thirds = [far[: -(-len(far) // 3)], far[-(-len(far) // 3) : -(-2 * len(far) // 3)], far[-(-2 * len(far) // 3) :]]

    @pl.loop(0, tiles)
    def _(t):
        def sent_at(tick):
            q = tick - tick // 3 if loose else tick
            return (tick >= 0) & (q < later) & ((tick % 3 != 2) if loose else True), q

        def pass_on(s):
            if later > 0:
                one, q = sent_at(t - s)

                @pl.when(one)
                def _():
                    gather(q).came(s)
                    gather(q).send(s)

        def sum_on(part):
            if part == 0:
                pl.when(within(t - 1, 0, summed))(lambda: scatter(t - 1).take())
            v = t - 1 - part
            j = v - v // 3

            @pl.when((v >= 0) & (v % 3 != 2) & (j < summed))
            def _():
                sums = scatter(j)
                if part == 3:
                    sums.finish(mine_ref.at[j])
                else:
                    for r in thirds[part]:
                        sums.step(r)

        if later > 0:
            one, q = sent_at(t)
            pl.when(one)(lambda: gather(q).send(0))
            arrived, q_last = sent_at(t - chips)

            @pl.when(arrived)
            def _():
                for s in range(chips):
                    gather(q_last).came_across(s)
                    gather(q_last).sent(s)

        start_load(t + 1)
        pltpu.make_async_copy(
            first_hbm.at[:, :, pl.ds(0, width)], w_ref.at[t % 2], load_sem.at[t % 2]
        ).wait()
        pl.when(t - 3 >= summed)(lambda: store(t - 3).wait())

        w = w_ref[t % 2].reshape(model, width)
        for i in range(2):
            at = slice(i * length // 2, (i + 1) * length // 2)
            both = nn(second_ref[at, :], w[:, : 2 * TILE])
            back = nn(incoming_ref[at, :], w[:, 2 * TILE :])
            gate, up = both[:, :TILE], both[:, TILE:]
            sigma = jax.nn.sigmoid(gate)
            silu = gate * sigma
            active_ref[at, :] = (silu * up).astype(BF)
            both_ref[at, :TILE] = (back * up * sigma * (1.0 + gate * (1.0 - sigma))).astype(BF)
            both_ref[at, TILE:] = (back * silu).astype(BF)
        pass_on(1)
        sum_on(0)
        rows = (chips, 2, model // dps)
        terms_ref[t % 3, :, :, :, : 2 * TILE] = nn(second_turned_ref[...], both_ref[...], BF).reshape(rows + (2 * TILE,))
        terms_ref[t % 3, :, :, :, 2 * TILE :] = nn(incoming_turned_ref[...], active_ref[...], BF).reshape(rows + (TILE,))
        pl.when(t < summed)(lambda: scatter(t).give().start())
        pl.when(t >= summed)(lambda: store(t).start())
        for s in range(2, chips - 1):
            pass_on(s)
        sum_on(1)
        for i in range(2):
            at = slice(i * length // 2, (i + 1) * length // 2)
            w = w_ref[t % 2].reshape(model, width)
            grad_ref[at, :] += nt(both_ref[at, :], w[:, : 2 * TILE])
            out_ref[at, :] += nt(active_ref[at, :], w[:, 2 * TILE :])
            if i == 0:
                sum_on(2)
        pass_on(chips - 1)
        sum_on(3)

    for j in range(summed):
        for part in range(4):
            if 1 + j + j // 2 + part >= tiles:
                if part == 3:
                    scatter(j).finish(mine_ref.at[j])
                else:
                    for r in thirds[part]:
                        scatter(j).step(r)
    for t in range(max(summed, tiles - 3), tiles):
        store(t).wait()
    quarter = length // 4
    stores = []
    for i in range(8):
        src, dst = (grad_ref, grad_hbm) if i < 4 else (out_ref, out_hbm)
        at = pl.ds((i % 4) * quarter, quarter)
        if i >= 2:
            stores[i - 2].wait()
        stage_ref[i % 2] = src[at, :].astype(BF)
        stores.append(pltpu.make_async_copy(stage_ref.at[i % 2], dst.at[at], stage_sem.at[i % 2]))
        stores[-1].start()
    for copy in stores[-2:]:
        copy.wait()


def feed_call(second, incoming, first, own, summed):
    dps, share, columns = first.shape
    chips = dps // 2
    length, model = second.shape
    width = 3 * TILE
    ready = columns // width
    tiles = ready + own.shape[1] // width
    if tiles == ready:
        own = jnp.zeros((share, 128), BF)
    vmem, hbm = pl.BlockSpec(memory_space=pltpu.VMEM), pl.BlockSpec(memory_space=pl.ANY)
    shape, dma = jax.ShapeDtypeStruct, pltpu.SemaphoreType.DMA
    return pl.pallas_call(
        functools.partial(feed_kernel, tiles=tiles, ready=ready, summed=summed),
        out_shape=(
            shape((dps,) + own.shape, BF),
            shape((length, model), BF),
            shape((length, model), BF),
            shape((chips, 2, share, (tiles - summed) * width), BF),
            shape((summed, share, width), F32),
        ),
        in_specs=[vmem, vmem, hbm, vmem],
        out_specs=(hbm, hbm, hbm, hbm, vmem),
        scratch_shapes=[
            pltpu.VMEM((model, length), BF),
            pltpu.VMEM((model, length), BF),
            pltpu.VMEM((2, dps, share, width), BF),
            pltpu.VMEM((3, chips, 2, share, width), BF),
            pltpu.VMEM((summed, chips, share, width), BF),
            pltpu.VMEM((summed, chips + 1, share, width), BF),
            pltpu.VMEM((length, TILE), BF),
            pltpu.VMEM((length, 2 * TILE), BF),
            pltpu.VMEM((length, model), F32),
            pltpu.VMEM((length, model), F32),
            pltpu.VMEM((2, length // 4, model), BF),
            dma((2,)), dma((3,)), dma((2,)), dma,
            dma((max(tiles - ready, 1), 4, chips)), dma((max(tiles - ready, 1), 4, chips)),
            dma((summed, 3, chips)), dma((summed, 3, chips)),
        ],
        cost_estimate=pl.CostEstimate(flops=65 * 10**9, bytes_accessed=60 * 10**6, transcendentals=3 * 10**6),
        compiler_params=pltpu.CompilerParams(
            collective_id=4, has_side_effects=True, vmem_limit_bytes=63 * 2**20
        ),
        name="feed_forward",
    )(second, incoming, first, own)


def pack_kernel(gate_ref, up_ref, down_ref, first_ref, rest_ref):
    units = gate_ref.shape[1]
    split = first_ref.shape[1] // (3 * TILE)
    for t in range(-(-units // TILE)):
        size = min(TILE, units - t * TILE)
        ref, at = (first_ref, t) if t < split else (rest_ref, t - split)
        lanes = slice(t * TILE, t * TILE + size)
        for i, part in enumerate((gate_ref[:, lanes], up_ref[:, lanes], down_ref[:, lanes])):
            low = (3 * at + i) * TILE
            ref[:, low : low + size] = part
            if size < TILE:
                ref[:, low + size : low + TILE] = jnp.zeros((part.shape[0], TILE - size), BF)


def pack_call(gate, up, down, ready):
    rows, units = gate.shape
    tiles = -(-units // TILE)
    vmem = pl.BlockSpec(memory_space=pltpu.VMEM)
    width = 3 * TILE
    return pl.pallas_call(
        pack_kernel,
        out_shape=[
            jax.ShapeDtypeStruct((rows, ready * width), BF),
            jax.ShapeDtypeStruct((rows, max(tiles - ready, 1) * width), BF),
        ],
        in_specs=[vmem] * 3,
        out_specs=[vmem] * 2,
        cost_estimate=pl.CostEstimate(flops=0, bytes_accessed=10**7, transcendentals=0),
        compiler_params=pltpu.CompilerParams(vmem_limit_bytes=32 * 2**20),
        name="pack_weights",
    )(gate, up, down)


def unpack_kernel(summed_ref, rest_ref, gate_ref, up_ref, down_ref):
    units = gate_ref.shape[1]
    split = summed_ref.shape[0]
    for t in range(-(-units // TILE)):
        size = min(TILE, units - t * TILE)
        lanes = slice(t * TILE, t * TILE + size)
        for i in range(3):
            if t < split:
                part = summed_ref[t, :, i * TILE : i * TILE + size]
            else:
                low = (3 * (t - split) + i) * TILE
                part = rest_ref[:, low : low + size].astype(F32)
            (gate_ref, up_ref, down_ref)[i][:, lanes] = part


def unpack_call(summed, rest, units):
    rows = rest.shape[0]
    vmem = pl.BlockSpec(memory_space=pltpu.VMEM)
    return pl.pallas_call(
        unpack_kernel,
        out_shape=[jax.ShapeDtypeStruct((rows, units), F32)] * 3,
        in_specs=[vmem] * 2,
        out_specs=[vmem] * 3,
        cost_estimate=pl.CostEstimate(flops=0, bytes_accessed=10**7, transcendentals=0),
        compiler_params=pltpu.CompilerParams(vmem_limit_bytes=32 * 2**20),
        name="unpack_gradients",
    )(summed, rest)


def end_kernel(
    normed_grad_ref, hidden_grad_ref, x_ref, gain_ref, qkv_ref, out_ref, small_ref,
    input_grad_ref, qkv_out_ref, out_out_ref, small_out_ref,
    qkv_got_ref, out_got_ref, small_got_ref,
    qkv_move_ref, out_move_ref, small_move_ref, qkv_came_ref, out_came_ref, small_came_ref,
    came_ref, sums_ref, one_ref, two_ref,
    sum_send, sum_recv, core_send, core_recv, ring_send, ring_recv, seq_send, seq_recv,
):
    seqs, dps = lax.axis_size("seq"), lax.axis_size("dp")
    chips = dps // 2
    seq, dpi = lax.axis_index("seq"), lax.axis_index("dp")
    chip, core = dpi // 2, dpi % 2
    ahead = ((chip + 1) % chips) * 2 + core
    behind = ((chip + chips - 1) % chips) * 2 + core
    sibling = chip * 2 + 1 - core
    greet([(seq ^ k, dpi) for k in range(1, seqs)] + [(seq, other) for other in (ahead, behind, sibling)])
    rows = x_ref.shape[0]
    piece = rows // PIECES

    cores = [
        remote(src.at[..., 1 - core, :, :], dst, core_send.at[i], core_recv.at[i], (seq, sibling))
        for i, (src, dst) in enumerate(
            ((qkv_ref, qkv_got_ref), (out_ref, out_got_ref), (small_ref, small_got_ref))
        )
    ]
    for copy in cores:
        copy.start()
    total = SeqSum(normed_grad_ref, rows, came_ref, sums_ref, one_ref, two_ref, (sum_send, sum_recv), dpi, seq)
    total.begin()
    for copy in cores:
        copy.wait_recv()

    def term(which, step):
        parts = [
            qkv_ref[:, which, core].astype(F32) + qkv_got_ref[:, which].astype(F32),
            out_ref[which, core].astype(F32) + out_got_ref[which].astype(F32),
            small_ref[which, core].astype(F32) + small_got_ref[which].astype(F32),
        ]
        if step > 0:
            came = (qkv_came_ref, out_came_ref, small_came_ref)
            parts = [part + field[step - 1].astype(F32) for part, field in zip(parts, came)]
        return parts

    def ring(step):
        return [
            remote(src.at[step], dst.at[step], ring_send.at[i, step], ring_recv.at[i, step], (seq, ahead))
            for i, (src, dst) in enumerate(
                ((qkv_move_ref, qkv_came_ref), (out_move_ref, out_came_ref), (small_move_ref, small_came_ref))
            )
        ]

    def input_piece(c):
        at = pl.ds(c * piece, piece)
        x = x_ref[at, :].astype(F32)
        factor = lax.rsqrt(jnp.mean(x * x, axis=-1, keepdims=True) + EPS)
        unit = x * factor
        scaled = total.take(c) * gain_ref[...]
        grad = scaled - unit * jnp.mean(scaled * unit, axis=-1, keepdims=True)
        input_grad_ref[at, :] = (hidden_grad_ref[at, :] + factor * grad).astype(BF)

    for step in range(chips - 1):
        if step > 0:
            for copy in ring(step - 1):
                copy.wait_recv()
        for field, part in zip((qkv_move_ref, out_move_ref, small_move_ref), term((chip + chips - 1 - step) % chips, step)):
            field[step] = part.astype(BF)
        for copy in ring(step):
            copy.start()
        if step == 0:
            total.middle()
        if step == 1:
            for c in range(PIECES):
                input_piece(c)
    for copy in ring(chips - 2):
        copy.wait_recv()
    qkv, out, small = term(chip, chips - 1)
    out_out_ref[...] = out
    qkv_move_ref[chips - 1] = qkv.astype(BF)
    small_move_ref[chips - 1] = small.astype(BF)
    last = [
        remote(
            src, dst.at[seq], seq_send.at[i, k], seq_recv.at[i, k], (seq ^ k, dpi)
        )
        for k in range(1, seqs)
        for i, (src, dst) in enumerate(
            ((qkv_move_ref.at[chips - 1, seq ^ k], qkv_out_ref), (small_move_ref.at[chips - 1], small_out_ref))
        )
    ]
    for copy in last:
        copy.start()
    qkv_out_ref[seq] = qkv_move_ref[chips - 1, seq]
    small_out_ref[seq] = small_move_ref[chips - 1]
    total.finish()
    for copy in cores + [copy for step in range(chips - 1) for copy in ring(step)]:
        copy.wait_send()
    for copy in last:
        copy.wait()


def end_call(normed_grad, hidden_grad, x, gain, qkv, out, small):
    seqs, chips, _, share, wide = qkv.shape
    rows, model = x.shape
    vmem = pl.BlockSpec(memory_space=pltpu.VMEM)
    shape, dma = jax.ShapeDtypeStruct, pltpu.SemaphoreType.DMA
    held = pltpu.VMEM((PIECES, rows // PIECES, model), BF)
    blocks = ((seqs, share, wide), (share, model), small.shape[2:])
    return pl.pallas_call(
        end_kernel,
        out_shape=(
            shape((rows, model), BF),
            shape(blocks[0], BF),
            shape(blocks[1], F32),
            shape((seqs,) + blocks[2], BF),
        ),
        in_specs=[vmem] * 7,
        out_specs=(vmem,) * 4,
        scratch_shapes=[
            pltpu.VMEM((seqs, chips, share, wide), BF),
            pltpu.VMEM((chips, share, model), BF),
            pltpu.VMEM((chips,) + blocks[2], BF),
        ]
        + [pltpu.VMEM((chips,) + block, BF) for block in blocks]
        + [pltpu.VMEM((chips - 1,) + block, BF) for block in blocks]
        + [
            held, held, held, held,
            dma((3, PIECES)), dma((3, PIECES)), dma((3,)), dma((3,)),
            dma((3, chips)), dma((3, chips)), dma((2, seqs)), dma((2, seqs)),
        ],
        cost_estimate=pl.CostEstimate(flops=10**8, bytes_accessed=2 * 10**7, transcendentals=0),
        compiler_params=pltpu.CompilerParams(
            collective_id=3, has_side_effects=True, vmem_limit_bytes=48 * 2**20
        ),
        name="end_sums",
    )(normed_grad, hidden_grad, x, gain[None], qkv, out, small)


def pair_tiles(left, right):
    units = left.shape[1]
    cuts = list(range(0, units, TILE)) + [units]
    return jnp.concatenate(
        [field[:, low:high] for low, high in zip(cuts[:-1], cuts[1:]) for field in (left, right)], axis=1
    )


def split_tiles(both):
    units = both.shape[1] // 2
    cuts = list(range(0, units, TILE)) + [units]
    spans = list(zip(cuts[:-1], cuts[1:]))
    return (
        jnp.concatenate([both[:, 2 * low : low + high] for low, high in spans], axis=1),
        jnp.concatenate([both[:, low + high : 2 * high] for low, high in spans], axis=1),
    )


def shards(
    inputs,
    block_ids,
    cotangent,
    first_gain,
    query_weight,
    query_bias,
    key_weight,
    key_bias,
    value_weight,
    value_bias,
    output_weight,
    second_gain,
    gate_weight,
    up_weight,
    down_weight,
):
    seqs = lax.axis_size("seq")
    seq = lax.axis_index("seq")
    dps = lax.axis_size("dp")
    dpi = lax.axis_index("dp")
    chips, chip, core = dps // 2, dpi // 2, dpi % 2
    heads = H // seqs
    copies = seqs // KEY_VALUE_HEADS
    wq = heads * HEAD_SIZE
    wide = wq + 2 * HEAD_SIZE
    tokens_here, model = inputs.shape[1:]
    share = first_gain.shape[0]
    kv_share = key_bias.shape[0]
    hidden_units = gate_weight.shape[1]

    small = jnp.concatenate([first_gain, second_gain, query_bias, key_bias, value_bias])
    packed = jnp.concatenate(
        [
            query_weight.reshape(share, seqs, wq),
            jnp.repeat(key_weight.reshape(share, KEY_VALUE_HEADS, HEAD_SIZE), copies, axis=1),
            jnp.repeat(value_weight.reshape(share, KEY_VALUE_HEADS, HEAD_SIZE), copies, axis=1),
        ],
        axis=-1,
    ).transpose(1, 0, 2)
    one = small.shape[0]
    small = jnp.pad(small[None], ((0, 15), (0, -one % 128)))
    tiles = -(-hidden_units // TILE)
    ready = READY if chips <= 4 else tiles
    first, later = pack_call(gate_weight, up_weight, down_weight.T, ready)
    later = later if ready < tiles else later[:, :0]
    first = lax.all_gather(first, "dp", axis=0, tiled=True).reshape(dps, model // dps, -1)
    tokens, incoming, blocks, smalls, weight_qkv, weight_out = start_call(
        inputs[0], cotangent[0], block_ids.reshape(-1, 128), small, packed, output_weight
    )
    blocks = blocks.reshape(-1)
    weight_qkv = weight_qkv.reshape(model, wide)
    out_head = weight_out[0].reshape(dps * share, model)
    weight_out = weight_out.reshape(model, model)
    smalls = smalls[:, :, 0, :one].transpose(1, 0, 2).astype(F32)
    gain_first = smalls[:, :, :share].reshape(model)
    gain_second = smalls[:, :, share : 2 * share].reshape(model)
    bias_q = lax.dynamic_index_in_dim(smalls, seq, 0, keepdims=False)[:, 2 * share : 3 * share].reshape(wq)
    group = seq // copies
    bias_k = smalls[:, :, 3 * share : 3 * share + kv_share].reshape(KEY_VALUE_HEADS, HEAD_SIZE)
    bias_v = smalls[:, :, 3 * share + kv_share :].reshape(KEY_VALUE_HEADS, HEAD_SIZE)
    bias = jnp.concatenate(
        [
            bias_q,
            lax.dynamic_index_in_dim(bias_k, group, 0, keepdims=False),
            lax.dynamic_index_in_dim(bias_v, group, 0, keepdims=False),
        ]
    )
    length = tokens.shape[0]
    cosine, sine = rope_tables(length)

    normed, qkv, mixed, logsum, hidden, second = attend_call(
        tokens, weight_qkv, bias[None], cosine, sine, blocks, gain_first, gain_second, weight_out
    )
    second, out_head = lax.optimization_barrier((second, out_head))
    _, out_sum, second_sum, rest, summed = feed_call(second, incoming, first, later, SUMMED)
    rest = rest.reshape(model, -1)
    rest = lax.psum_scatter(rest, "dp", scatter_dimension=0, tiled=True)
    gate_grad, up_grad, down_grad = unpack_call(summed, rest, hidden_units)
    normed_grad, grad_hidden, qkv_grad, out_weight_grad, bias_grad, gain_one_grad, gain_two_grad, layer_out = backward_call(
        second_sum, out_sum, cotangent[0], gain_first, gain_second, logsum, cosine, sine, blocks,
        hidden, tokens, normed, weight_qkv, out_head, qkv, mixed,
    )
    bias_grad, gain_one_grad, gain_two_grad = bias_grad[0], gain_one_grad[0], gain_two_grad[0]

    place = lambda field, count, at: jnp.where(
        (jnp.arange(count) == at)[:, None], field[None], 0.0
    ).reshape(seqs, dps, -1)
    small_grad = jnp.concatenate(
        [
            gain_one_grad.reshape(seqs, dps, share),
            gain_two_grad.reshape(seqs, dps, share),
            place(bias_grad[:wq], seqs, seq),
            place(bias_grad[wq : wq + HEAD_SIZE], KEY_VALUE_HEADS, group),
            place(bias_grad[wq + HEAD_SIZE :], KEY_VALUE_HEADS, group),
        ],
        axis=-1,
    )
    small_rows = -(-seqs * one // wide)
    small_grad = small_grad.transpose(1, 0, 2).reshape(dps, seqs * one).astype(BF)
    small_grad = jnp.pad(small_grad, ((0, 0), (0, small_rows * wide - seqs * one)))
    small_grad = jnp.pad(small_grad.reshape(dps, -1, wide), ((0, 0), (0, 16 - small_rows), (0, 0)))
    input_grad, parts, out_weight_grad, smalls = end_call(
        normed_grad, grad_hidden, inputs[0], gain_first,
        qkv_grad.reshape(seqs, chips, 2, share, wide),
        out_weight_grad.reshape(chips, 2, share, model),
        small_grad.reshape(chips, 2, 16, wide),
    )
    smalls = smalls[:, :small_rows].reshape(seqs, -1)[:, : seqs * one].reshape(seqs, seqs, one)
    small_sum = jnp.sum(
        lax.dynamic_index_in_dim(smalls, seq, 1, keepdims=False).astype(F32), axis=0
    )
    query_weight_grad = jnp.concatenate([part[:share, :wq] for part in parts], axis=1).astype(F32)
    pairs = [
        sum(part[:share, wq:].astype(F32) for part in parts[g * copies : (g + 1) * copies])
        for g in range(KEY_VALUE_HEADS)
    ]
    key_weight_grad = jnp.concatenate([pair[:, :HEAD_SIZE] for pair in pairs], axis=1)
    value_weight_grad = jnp.concatenate([pair[:, HEAD_SIZE:] for pair in pairs], axis=1)
    gain_one_grad, gain_two_grad, query_bias_grad, key_bias_grad, value_bias_grad = jnp.split(
        small_sum, [share, 2 * share, 3 * share, 3 * share + kv_share]
    )

    return (
        layer_out[None],
        input_grad[None],
        gain_one_grad,
        query_weight_grad,
        query_bias_grad,
        key_weight_grad,
        key_bias_grad,
        value_weight_grad,
        value_bias_grad,
        out_weight_grad,
        gain_two_grad,
        gate_grad,
        up_grad,
        down_grad.T,
    )


def solution(mesh):
    tokens = P("dp", "seq", None)
    whole = P(("seq", "dp"))
    matrix = P(("seq", "dp"), None)
    feed = P("dp", "seq")
    in_specs = (
        tokens,
        P("dp", "seq"),
        tokens,
        whole,
        matrix,
        whole,
        matrix,
        whole,
        matrix,
        whole,
        matrix,
        whole,
        feed,
        feed,
        P("seq", "dp"),
    )
    out_specs = (
        tokens,
        tokens,
        whole,
        matrix,
        whole,
        matrix,
        whole,
        matrix,
        whole,
        matrix,
        whole,
        feed,
        feed,
        P("seq", "dp"),
    )
    return jax.shard_map(shards, mesh=mesh, in_specs=in_specs, out_specs=out_specs, check_vma=False)
```

```python
import functools

import jax
import jax.numpy as jnp
import numpy as np
from jax import lax
from jax.experimental import pallas as pl
from jax.experimental.pallas import tpu as pltpu
from jax.sharding import PartitionSpec as P

H = 12
KEY_VALUE_HEADS = 2
HEAD_SIZE = 128
EPS = 1e-06
THETA = 1000000.0
SCALE = HEAD_SIZE ** (-0.5)
BF = jnp.bfloat16
F32 = jnp.float32


def dot(a, b, dims, out=F32):
    return lax.dot_general(a, b, (dims, ((), ())), preferred_element_type=F32).astype(out)


def nn(a, b, out=F32):
    return dot(a, b, ((1,), (0,)), out)


def nt(a, b, out=F32):
    return dot(a, b, ((1,), (1,)), out)


def tn(a, b, out=F32):
    return dot(a, b, ((0,), (0,)), out)


def rope_tables(length):
    exponent = np.arange(0, HEAD_SIZE, 2).astype(np.float32) / np.float32(HEAD_SIZE)
    freqs = np.float32(THETA) ** (-exponent)
    angles = np.arange(length).astype(np.float32)[:, None] * freqs[None, :]
    cosine, sine = np.cos(angles), np.sin(angles)
    return (
        jnp.asarray(np.concatenate([cosine, cosine], axis=-1), F32),
        jnp.asarray(np.concatenate([-sine, sine], axis=-1), F32),
    )


def remote(src, dst, send, recv, where):
    return pltpu.make_async_remote_copy(
        src_ref=src, dst_ref=dst, send_sem=send, recv_sem=recv,
        device_id=where, device_id_type=pl.DeviceIdType.MESH,
    )


def greet(partners):
    barrier = pltpu.get_barrier_semaphore()
    for partner in partners:
        pl.semaphore_signal(barrier, inc=1, device_id=partner, device_id_type=pl.DeviceIdType.MESH)
    pl.semaphore_wait(barrier, len(partners))


def far_sends(field, half, seq, dpi, send, recv):
    def rows(k, low):
        return field.at[pl.ds(pl.multiple_of((seq ^ k) * 2 * half + low, half), half)]

    return [
        remote(rows(2, 0), rows(2, 0), send.at[0], recv.at[0], (seq ^ 1, dpi)),
        remote(rows(1, half), rows(1, half), send.at[1], recv.at[1], (seq ^ 2, dpi)),
    ]


def start_kernel(
    x_in, c_in, ids_in, small_in, pack_in, out_in,
    x_out, c_out, ids_out, small_out, pack_out, out_out,
    local_sem, seq_send, seq_recv, far_send, far_recv, ring_send, ring_recv, core_send, core_recv,
    out_send, out_recv, slot_send, slot_recv,
):
    seqs, dps = lax.axis_size("seq"), lax.axis_size("dp")
    chips = dps // 2
    seq, dpi = lax.axis_index("seq"), lax.axis_index("dp")
    chip, core = dpi // 2, dpi % 2
    sibling = chip * 2 + 1 - core
    others = [((chip + h) % chips) * 2 + core for h in range(1, chips)]
    greet([(seq ^ k, dpi) for k in range(1, seqs)] + [(seq, other) for other in others + [sibling]])

    rows = x_in.shape[0]
    half = rows // 2

    def to_slots(i, src, dst, slots):
        return [remote(src, dst, seq_send.at[i, k], seq_recv.at[i, k], (seq ^ k, dpi)) for k in slots]

    def block(index, low=0, count=rows):
        return pl.ds(pl.multiple_of(index * rows + low, half), count)

    small_sends = to_slots(0, small_in, small_out.at[dpi, seq], range(1, seqs))
    pack_sends = [
        remote(
            pack_in.at[seq ^ k], pack_out.at[seq, dpi], seq_send.at[1, k], seq_recv.at[1, k], (seq ^ k, dpi)
        )
        for k in range(1, seqs)
    ]
    id_sends = to_slots(2, ids_in, ids_out.at[seq], range(1, seqs))
    x_sends = to_slots(3, x_in, x_out.at[block(seq)], (1, 2))
    c_sends = to_slots(4, c_in, c_out.at[block(seq)], (1, 2))
    locals_ = [
        pltpu.make_async_copy(small_in, small_out.at[dpi, seq], local_sem.at[0]),
        pltpu.make_async_copy(pack_in.at[seq], pack_out.at[seq, dpi], local_sem.at[1]),
        pltpu.make_async_copy(out_in, out_out.at[0, dpi], local_sem.at[2]),
        pltpu.make_async_copy(ids_in, ids_out.at[seq], local_sem.at[3]),
        pltpu.make_async_copy(x_in, x_out.at[block(seq)], local_sem.at[4]),
        pltpu.make_async_copy(c_in, c_out.at[block(seq)], local_sem.at[5]),
    ]
    def fields(at, which):
        every = (out_out.at[0, at], small_out.at[at], pack_out.at[:, at])
        return [(i, every[i]) for i in which]

    def hop_sends(hop, which):
        to = ((chip + chips - hop) % chips) * 2 + core
        return [
            remote(out_in if i == 0 else field, field, ring_send.at[i, hop], ring_recv.at[i, hop], (seq, to))
            for i, field in fields(dpi, which)
        ]

    def core_sends(hop, which=(0, 1, 2)):
        at = ((chip + hop) % chips) * 2 + core
        return [
            remote(field, field, core_send.at[i, hop], core_recv.at[i, hop], (seq, sibling))
            for i, field in fields(at, which)
        ]

    def out_sends(hop):
        at = ((chip + hop) % chips) * 2 + core
        src = out_out.at[0, at] if hop else out_in
        return [
            remote(src, out_out.at[k, at], out_send.at[k, hop], out_recv.at[k, hop], (seq ^ k, dpi))
            for k in range(1, seqs)
        ]

    order = sorted(range(1, chips), key=lambda hop: min(hop, chips - hop))
    flying, outs = [], []
    for hop in order:
        flying += hop_sends(hop, (0,))
    first = small_sends + pack_sends + locals_[:3] + x_sends + id_sends + locals_[3:]
    for copy in flying + first:
        copy.start()
    for copy in locals_[:3] + small_sends + pack_sends:
        copy.wait()
    more = [copy for hop in order for copy in hop_sends(hop, (1, 2))]
    for copy in more:
        copy.start()
    flying += more
    for hop in [0] + order:
        if hop > 0:
            for copy in hop_sends(hop, (0,)):
                copy.wait_recv()
        cores, more = core_sends(hop, (0,)), out_sends(hop)
        for copy in cores + more:
            copy.start()
        flying += cores
        outs += more
    for copy in x_sends:
        copy.wait()
    far_x = far_sends(x_out, half, seq, dpi, far_send.at[0], far_recv.at[0])
    for copy in far_x + c_sends:
        copy.start()
    for hop in [0] + order:
        if hop > 0:
            for copy in hop_sends(hop, (1, 2)):
                copy.wait_recv()
        cores = core_sends(hop, (1, 2))
        for copy in cores:
            copy.start()
        flying += cores
    for copy in c_sends:
        copy.wait()
    far_c = far_sends(c_out, half, seq, dpi, far_send.at[1], far_recv.at[1])
    for copy in far_c:
        copy.start()
    for copy in outs:
        copy.wait_recv()
    slots = [
        remote(
            out_out.at[k, ((chip + hop) % chips) * 2 + core], out_out.at[k, ((chip + hop) % chips) * 2 + core],
            slot_send.at[k, hop], slot_recv.at[k, hop], (seq, sibling),
        )
        for k in range(1, seqs)
        for hop in range(chips)
    ]
    for copy in slots:
        copy.start()
    for copy in flying + outs:
        copy.wait_send()
    for hop in range(chips):
        for copy in core_sends(hop):
            copy.wait_recv()
    for copy in slots + far_x + far_c + id_sends + locals_[3:]:
        copy.wait()


def start_call(x, c, ids, small, pack, out):
    seqs, dps = lax.axis_size("seq"), lax.axis_size("dp")
    chips = dps // 2
    share, wide = pack.shape[1:]
    any_space = pl.BlockSpec(memory_space=pl.ANY)
    shapes = (
        jax.ShapeDtypeStruct((seqs * x.shape[0], x.shape[1]), x.dtype),
        jax.ShapeDtypeStruct((seqs * c.shape[0], c.shape[1]), c.dtype),
        jax.ShapeDtypeStruct((seqs,) + ids.shape, ids.dtype),
        jax.ShapeDtypeStruct((dps, seqs) + small.shape, small.dtype),
        jax.ShapeDtypeStruct((seqs, dps, share, wide), pack.dtype),
        jax.ShapeDtypeStruct((seqs, dps) + out.shape, out.dtype),
    )
    dma = pltpu.SemaphoreType.DMA
    return pl.pallas_call(
        start_kernel,
        out_shape=shapes,
        in_specs=[pl.BlockSpec(memory_space=pltpu.VMEM)] * 6,
        out_specs=(any_space,) * 6,
        scratch_shapes=[
            dma((6,)), dma((5, seqs)), dma((5, seqs)), dma((2, 2)), dma((2, 2)),
            dma((3, chips)), dma((3, chips)), dma((3, chips)), dma((3, chips)),
            dma((seqs, chips)), dma((seqs, chips)), dma((seqs, chips)), dma((seqs, chips)),
        ],
        compiler_params=pltpu.CompilerParams(collective_id=0, has_side_effects=True),
        name="start_gather",
    )(x, c, ids, small, pack, out)


def attend_kernel(
    x_ref, w_ref, bias_ref, cos_ref, sin_ref, ids_row_ref, ids_col_ref, gain_one_ref, gain_two_ref, out_ref,
    normed_ref, qkv_ref, mixed_ref, lse_ref, hidden_ref, second_ref,
    all_ref, send_sem, recv_sem,
):
    seqs = lax.axis_size("seq")
    seq, dpi = lax.axis_index("seq"), lax.axis_index("dp")
    greet([(seq ^ k, dpi) for k in range(1, seqs)])
    length, model = x_ref.shape
    wq = mixed_ref.shape[1]
    heads = wq // HEAD_SIZE
    rows = length // seqs
    @pl.loop(0, seqs)
    def _(i):
        at = pl.ds(pl.multiple_of(i * rows, rows), rows)
        x = x_ref[at, :].astype(F32)
        factor = lax.rsqrt(jnp.mean(x * x, axis=-1, keepdims=True) + EPS)
        normed_ref[at, :] = (x * factor * gain_one_ref[...]).astype(BF)

    @pl.loop(0, 2)
    def _(i):
        at = pl.ds(pl.multiple_of(i * 2 * rows, 2 * rows), 2 * rows)
        pre = jnp.dot(normed_ref[at, :], w_ref[...], preferred_element_type=F32) + bias_ref[...]
        cosine, sine = cos_ref[at, :], sin_ref[at, :]
        for h in range(heads + 1):
            u = pre[:, h * HEAD_SIZE : (h + 1) * HEAD_SIZE]
            turned = pltpu.roll(u, HEAD_SIZE // 2, 1)
            qkv_ref[at, h * HEAD_SIZE : (h + 1) * HEAD_SIZE] = (u * cosine + turned * sine).astype(BF)
        qkv_ref[at, wq + HEAD_SIZE :] = pre[:, wq + HEAD_SIZE :].astype(BF)

    copies = []
    for t in range(seqs):
        at = slice(t * rows, (t + 1) * rows)
        reach = min(t + 2, seqs) * rows
        keys = qkv_ref[:reach, wq : wq + HEAD_SIZE]
        values = qkv_ref[:reach, wq + HEAD_SIZE :]
        allowed = ids_row_ref[:, :reach] <= ids_col_ref[at, :]
        sums = []
        for h in range(heads):
            lanes = slice(h * HEAD_SIZE, (h + 1) * HEAD_SIZE)
            scores = nt(qkv_ref[at, lanes], keys) * SCALE
            scores = jnp.where(allowed, scores, -1000000000.0)
            peak = jnp.max(scores, axis=-1, keepdims=True)
            raised = jnp.exp(scores - peak)
            total = jnp.sum(raised, axis=-1, keepdims=True)
            low = (raised * (1.0 / total)).astype(BF)
            mixed_ref[at, lanes] = nn(low, values).astype(BF)
            sums.append(peak + jnp.log(total))
        lse_ref[at, :heads] = jnp.concatenate(sums, axis=1)
        more = [
            remote(
                mixed_ref.at[pl.ds(t * rows, rows)], all_ref.at[pl.ds(t * rows, rows), pl.ds(k * wq, wq)],
                send_sem.at[k, t], recv_sem.at[k, t], (seq ^ k, dpi),
            )
            for k in range(1, seqs)
        ]
        for copy in more:
            copy.start()
        copies.append(more)
        all_ref[at, :wq] = mixed_ref[at, :]

    for t in range(seqs):
        at = slice(t * rows, (t + 1) * rows)
        for copy in copies[t]:
            copy.wait_recv()
        hidden = x_ref[at, :].astype(F32) + nn(all_ref[at, :], out_ref[...])
        hidden_ref[at, :] = hidden
        factor = lax.rsqrt(jnp.mean(hidden * hidden, axis=-1, keepdims=True) + EPS)
        second_ref[at, :] = (hidden * factor * gain_two_ref[...]).astype(BF)
    for t in range(seqs):
        for copy in copies[t]:
            copy.wait_send()


def attend_call(x, w, bias, cosine, sine, ids, gain_one, gain_two, out):
    seqs = lax.axis_size("seq")
    length, model = x.shape
    wide = w.shape[1]
    wq = wide - 2 * HEAD_SIZE
    vmem = pl.BlockSpec(memory_space=pltpu.VMEM)
    shape = jax.ShapeDtypeStruct
    return pl.pallas_call(
        attend_kernel,
        out_shape=(
            shape((length, model), BF),
            shape((length, wide), BF),
            shape((length, wq), BF),
            shape((length, 128), F32),
            shape((length, model), F32),
            shape((length, model), BF),
        ),
        in_specs=[vmem] * 10,
        out_specs=(vmem,) * 6,
        scratch_shapes=[
            pltpu.VMEM((length, seqs * wq), BF),
            pltpu.SemaphoreType.DMA((seqs, seqs)),
            pltpu.SemaphoreType.DMA((seqs, seqs)),
        ],
        cost_estimate=pl.CostEstimate(flops=9 * 10**9, bytes_accessed=30 * 10**6, transcendentals=3 * 10**6),
        compiler_params=pltpu.CompilerParams(
            collective_id=1, has_side_effects=True, vmem_limit_bytes=60 * 2**20
        ),
        name="attend",
    )(x, w, bias, cosine, sine, ids[None], ids[:, None], gain_one[None], gain_two[None], out)


PIECES = 4
READY = 6
SUMMED = 4


def slot_rows(index, rows):
    return pl.ds(pl.multiple_of(index * rows, rows), rows)


class SeqSum:
    def __init__(self, field, rows, came, sums, from_one, from_two, sems, dpi, seq):
        self.field, self.rows, self.piece = field, rows, rows // PIECES
        self.came, self.sums, self.got = came, sums, {1: from_one, 2: from_two}
        self.send, self.recv = sems
        self.dpi, self.seq = dpi, seq
        self.started = []

    def at(self, k, c):
        start = (self.seq ^ k) * self.rows + c * self.piece
        return pl.ds(pl.multiple_of(start, self.piece), self.piece)

    def pass_on(self, c):
        by = 1 + c % 2
        return remote(
            self.field.at[self.at(3, c)], self.came.at[c], self.send.at[0, c], self.recv.at[0, c], (self.seq ^ by, self.dpi)
        )

    def direct(self, k, c):
        late = (k == 2) == (c % 2 == 0)
        src = self.sums.at[c] if late else self.field.at[self.at(k, c)]
        return remote(src, self.got[k].at[c], self.send.at[k, c], self.recv.at[k, c], (self.seq ^ k, self.dpi))

    def begin(self):
        for c in range(PIECES):
            self.pass_on(c).start()
            self.direct(1 + c % 2, c).start()

    def middle(self):
        for c in range(PIECES):
            k = 2 - c % 2
            self.pass_on(c).wait_recv()
            own = self.field[self.at(k, c), :].astype(F32)
            self.sums[c] = (self.came[c].astype(F32) + own).astype(BF)
            self.direct(k, c).start()

    def take(self, c):
        for k in (1, 2):
            self.direct(k, c).wait_recv()
        total = self.field[self.at(0, c), :].astype(F32) + self.got[1][c].astype(F32)
        return total + self.got[2][c].astype(F32)

    def finish(self):
        for c in range(PIECES):
            self.pass_on(c).wait_send()
            for k in (1, 2):
                self.direct(k, c).wait_send()


def backward_kernel(
    second_grad_ref, cotangent_ref, gain_one_ref, gain_two_ref, lse_ref, cos_ref, sin_ref,
    ids_row_ref, ids_col_ref, hidden_hbm, tokens_hbm, normed_hbm, w_hbm, out_hbm, qkv_hbm, mixed_hbm,
    normed_grad_ref, hidden_grad_ref, w_grad_ref, out_grad_ref, bias_grad_ref, gain_grad_ref, gain_two_grad_ref,
    hidden_ref, tokens_ref, normed_ref, w_ref, out_ref, qkv_ref, mixed_ref,
    branch_ref, mixed_grad_ref, pre_grad_ref, key_grad_ref, value_grad_ref,
    came_ref, sums_ref, one_ref, two_ref,
    load_sem, sum_send, sum_recv, branch_send, branch_recv,
):
    seqs = lax.axis_size("seq")
    seq, dpi = lax.axis_index("seq"), lax.axis_index("dp")
    length, model = second_grad_ref.shape
    rows = length // seqs
    piece = rows // PIECES
    wq = mixed_ref.shape[1]
    heads = wq // HEAD_SIZE
    loads = [
        pltpu.make_async_copy(src, dst, load_sem.at[i])
        for i, (src, dst) in enumerate(
            (
                (hidden_hbm.at[slot_rows(seq, rows)], hidden_ref),
                (out_hbm, out_ref), (qkv_hbm, qkv_ref), (w_hbm, w_ref),
                (tokens_hbm, tokens_ref), (normed_hbm, normed_ref), (mixed_hbm, mixed_ref),
            )
        )
    ]
    for load in loads:
        load.start()
    greet([(seq ^ k, dpi) for k in range(1, seqs)])

    total = SeqSum(second_grad_ref, rows, came_ref, sums_ref, one_ref, two_ref, (sum_send, sum_recv), dpi, seq)
    total.begin()
    loads[0].wait()
    total.middle()

    def branch_at(k, c):
        start = (seq ^ k) * rows + c * piece
        return branch_ref.at[pl.ds(pl.multiple_of(start, piece), piece)]

    def branch_copy(k, c):
        if k < 3:
            return remote(
                branch_at(0, c), branch_at(0, c), branch_send.at[k, c], branch_recv.at[k, c], (seq ^ k, dpi)
            )
        came, to = (2, 1) if c % 2 == 0 else (1, 2)
        return remote(
            branch_at(came, c), branch_at(came, c), branch_send.at[3, c], branch_recv.at[3, c], (seq ^ to, dpi)
        )

    gain_two_grad_ref[...] = jnp.zeros_like(gain_two_grad_ref)
    for c in range(PIECES):
        at = pl.ds(c * piece, piece)
        grad = total.take(c)
        hidden = hidden_ref[at, :]
        factor = lax.rsqrt(jnp.mean(hidden * hidden, axis=-1, keepdims=True) + EPS)
        unit = hidden * factor
        gain_two_grad_ref[...] += jnp.sum(grad * unit, axis=0, keepdims=True)
        scaled = grad * gain_two_ref[...]
        grad = cotangent_ref[at, :].astype(F32) + factor * (
            scaled - unit * jnp.mean(scaled * unit, axis=-1, keepdims=True)
        )
        hidden_grad_ref[at, :] = grad
        start = pl.multiple_of(seq * rows + c * piece, piece)
        branch_ref[pl.ds(start, piece), :] = grad.astype(BF)
        for k in (1, 2):
            branch_copy(k, c).start()
    total.finish()
    for load in loads[1:3]:
        load.wait()

    key_grad_ref[...] = jnp.zeros_like(key_grad_ref)
    value_grad_ref[...] = jnp.zeros_like(value_grad_ref)

    def rot_back(w, at):
        return w * cos_ref[at, :] + pltpu.roll(w * sin_ref[at, :], HEAD_SIZE // 2, 1)

    def attend_back(k):
        at = slot_rows(seq ^ k, rows)
        mixed_grad_ref[at, :] = nt(branch_ref[at, :], out_ref[...]).astype(BF)
        allowed = ids_row_ref[...] <= ids_col_ref[at, :]
        keys = qkv_ref[:, wq : wq + HEAD_SIZE]
        values = qkv_ref[:, wq + HEAD_SIZE :]
        for h in range(heads):
            lanes = slice(h * HEAD_SIZE, (h + 1) * HEAD_SIZE)
            queries = qkv_ref[at, lanes]
            grad = mixed_grad_ref[at, lanes]
            scores = jnp.where(allowed, nt(queries, keys) * SCALE, -1000000000.0)
            probs = jnp.exp(scores - lse_ref[at, h : h + 1])
            prob_grad = nt(grad, values)
            delta = jnp.sum(probs * prob_grad, axis=-1, keepdims=True)
            score_grad = (probs * (prob_grad - delta)).astype(BF)
            pre_grad_ref[at, lanes] = rot_back(nn(score_grad, keys) * SCALE, at).astype(BF)
            key_grad_ref[...] += tn(score_grad, queries)
            value_grad_ref[...] += tn(probs.astype(BF), grad)

    attend_back(0)
    for k in (1, 2):
        for c in range(PIECES):
            branch_copy(k, c).wait_recv()
            if (k == 2) == (c % 2 == 0):
                branch_copy(3, c).start()
        attend_back(k)
    for c in range(PIECES):
        branch_copy(3, c).wait_recv()
    attend_back(3)
    for c in range(PIECES):
        for k in (1, 2, 3):
            branch_copy(k, c).wait_send()

    every = pl.ds(0, length)
    pre_grad_ref[:, wq : wq + HEAD_SIZE] = rot_back(key_grad_ref[...] * SCALE, every).astype(BF)
    pre_grad_ref[:, wq + HEAD_SIZE :] = value_grad_ref[...].astype(BF)
    bias_grad_ref[...] = jnp.sum(pre_grad_ref[...].astype(F32), axis=0, keepdims=True)
    for load in loads[3:]:
        load.wait()
    gain_grad_ref[...] = jnp.zeros_like(gain_grad_ref)

    @pl.loop(0, seqs)
    def _(i):
        at = slot_rows(i, rows)
        grad = nt(pre_grad_ref[at, :], w_ref[...])
        x = tokens_ref[at, :].astype(F32)
        factor = lax.rsqrt(jnp.mean(x * x, axis=-1, keepdims=True) + EPS)
        gain_grad_ref[...] += jnp.sum(grad * (x * factor), axis=0, keepdims=True)
        normed_grad_ref[at, :] = grad.astype(BF)

    @pl.loop(0, model // wq)
    def _(i):
        lanes = pl.ds(pl.multiple_of(i * wq, HEAD_SIZE), wq)
        w_grad_ref[pl.ds(pl.multiple_of(i * wq, HEAD_SIZE), wq), :] = tn(normed_ref[:, lanes], pre_grad_ref[...]).astype(BF)
        out_grad_ref[:, lanes] = tn(mixed_ref[...], branch_ref[:, lanes]).astype(BF)


def backward_call(
    second_grad, cotangent, gain_one, gain_two, logsum, cosine, sine, ids, hidden, tokens, normed, w, out, qkv, mixed
):
    seqs = lax.axis_size("seq")
    length, model = tokens.shape
    rows = length // seqs
    wide = w.shape[1]
    wq = mixed.shape[1]
    vmem, hbm = pl.BlockSpec(memory_space=pltpu.VMEM), pl.BlockSpec(memory_space=pl.ANY)
    shape, dma = jax.ShapeDtypeStruct, pltpu.SemaphoreType.DMA
    held = pltpu.VMEM((PIECES, rows // PIECES, model), BF)
    return pl.pallas_call(
        backward_kernel,
        out_shape=(
            shape((length, model), BF),
            shape((rows, model), F32),
            shape((model, wide), BF),
            shape((wq, model), BF),
            shape((1, wide), F32),
            shape((1, model), F32),
            shape((1, model), F32),
        ),
        in_specs=[vmem] * 9 + [hbm] * 7,
        out_specs=(vmem,) * 7,
        scratch_shapes=[pltpu.VMEM((rows, model), F32)]
        + [pltpu.VMEM(field.shape, field.dtype) for field in (tokens, normed, w, out, qkv, mixed)]
        + [
            pltpu.VMEM((length, model), BF),
            pltpu.VMEM((length, wq), BF),
            pltpu.VMEM((length, wide), BF),
            pltpu.VMEM((length, HEAD_SIZE), F32),
            pltpu.VMEM((length, HEAD_SIZE), F32),
            held, held, held, held,
            dma((7,)), dma((3, PIECES)), dma((3, PIECES)), dma((4, PIECES)), dma((4, PIECES)),
        ],
        cost_estimate=pl.CostEstimate(flops=13 * 10**9, bytes_accessed=30 * 10**6, transcendentals=3 * 10**6),
        compiler_params=pltpu.CompilerParams(
            collective_id=2, has_side_effects=True, vmem_limit_bytes=62 * 2**20
        ),
        name="backward",
    )(
        second_grad, cotangent, gain_one[None], gain_two[None], logsum, cosine, sine,
        ids[None], ids[:, None], hidden, tokens, normed, w, out, qkv, mixed,
    )


TILE = 256


class ChipGather:
    def __init__(self, whole, columns, sems, seq, dpi, chips, own=None):
        self.whole, self.columns, self.sems, self.own = whole, columns, sems, own
        self.seq, self.dpi, self.chips = seq, dpi, chips
        self.chip, self.core = dpi // 2, dpi % 2

    def copy(self, kind, s, chip, core, to):
        block = self.whole.at[chip * 2 + core, :, self.columns]
        send, recv = self.sems
        src = block if s or self.own is None else self.own.at[:, self.columns]
        return remote(src, block, send.at[kind, s], recv.at[kind, s], (self.seq, to))

    def copies(self, s):
        z, c = self.chip, self.core
        low, high = z - s, z + s
        sibling = z * 2 + 1 - c
        out = [
            ((low >= 0) & (z < self.chips - 1), self.copy(0, s, low, c, self.dpi + 2)),
            ((high < self.chips) & (z > 0), self.copy(1, s, high, c, self.dpi - 2)),
            (low >= 0, self.copy(2, s, low, c, sibling)),
        ]
        if s > 0:
            out.append((high < self.chips, self.copy(3, s, high, c, sibling)))
        return out

    def send(self, s):
        for condition, copy in self.copies(s):
            pl.when(condition)(copy.start)

    def sent(self, s):
        for condition, copy in self.copies(s):
            pl.when(condition)(copy.wait_send)

    def came(self, s):
        z, c = self.chip, self.core
        pl.when(z - s >= 0)(self.copy(0, s - 1, z - s, c, self.dpi).wait_recv)
        pl.when(z + s < self.chips)(self.copy(1, s - 1, z + s, c, self.dpi).wait_recv)

    def came_across(self, s):
        z, c = self.chip, self.core
        pl.when(z - s >= 0)(self.copy(2, s, z - s, 1 - c, self.dpi).wait_recv)
        if s > 0:
            pl.when(z + s < self.chips)(self.copy(3, s, z + s, 1 - c, self.dpi).wait_recv)


class ChipScatter:
    def __init__(self, terms, got, held, sems, seq, dpi, chips):
        self.terms, self.got, self.held, self.sems = terms, got, held, sems
        self.seq, self.dpi, self.chips = seq, dpi, chips
        self.chip, self.core = dpi // 2, dpi % 2

    def give(self):
        send, recv = self.sems
        return remote(
            self.terms.at[:, 1 - self.core], self.got, send.at[2, 0], recv.at[2, 0], (self.seq, self.chip * 2 + 1 - self.core)
        )

    def up(self, d, to, field=None):
        send, recv = self.sems
        return remote((field or self.held).at[d], self.held.at[d], send.at[0, d], recv.at[0, d], (self.seq, to))

    def down(self, d, to, last, field=None):
        send, recv = self.sems
        slot = self.chips if last else d
        return remote((field or self.held).at[d], self.held.at[slot], send.at[1, d], recv.at[1, d], (self.seq, to))

    def each(self, body):
        size = self.got.shape[1]
        chunk = 16 if size % 16 == 0 else size

        @pl.loop(0, size // chunk)
        def _(i):
            body(pl.ds(pl.multiple_of(i * chunk, chunk), chunk))

    def take(self):
        self.give().wait()

        @pl.loop(0, self.chips)
        def _(d):
            def body(rows):
                own = self.terms[d, self.core, rows, :].astype(F32)
                self.got[d, rows, :] = (own + self.got[d, rows, :].astype(F32)).astype(BF)

            self.each(body)

    def add(self, d):
        def body(rows):
            total = self.got[d, rows, :].astype(F32) + self.held[d, rows, :].astype(F32)
            self.held[d, rows, :] = total.astype(BF)

        self.each(body)

    def step(self, r):
        z, chips = self.chip, self.chips

        @pl.when(z + r < chips)
        def _():
            d = z + r

            @pl.when(z > 0)
            def _():
                self.up(d, self.dpi).wait_recv()
                self.add(d)
                self.up(d, self.dpi + 2).start()

            @pl.when(z == 0)
            def _():
                self.up(d, self.dpi + 2, self.got).start()

        @pl.when(z - r >= 0)
        def _():
            d = z - r

            @pl.when(z < chips - 1)
            def _():
                self.down(d, self.dpi, False).wait_recv()
                self.add(d)
                self.down(d, self.dpi - 2, r == 1).start()

            @pl.when(z == chips - 1)
            def _():
                self.down(d, self.dpi - 2, r == 1, self.got).start()

    def finish(self, result):
        z, chips = self.chip, self.chips
        pl.when(z > 0)(lambda: self.up(z, self.dpi).wait_recv())
        pl.when(z < chips - 1)(lambda: self.down(z, self.dpi, True).wait_recv())

        def body(rows):
            total = self.got[z, rows, :].astype(F32)
            total += jnp.where(z > 0, self.held[z, rows, :].astype(F32), 0.0)
            result[rows, :] = total + jnp.where(z < chips - 1, self.held[chips, rows, :].astype(F32), 0.0)

        self.each(body)
        for r in range(1, chips):
            pl.when(z + r < chips)(lambda: self.up(z + r, self.dpi + 2).wait_send())
            pl.when(z - r >= 0)(lambda: self.down(z - r, self.dpi - 2, r == 1).wait_send())


def feed_kernel(
    second_ref, incoming_ref, first_hbm, own_ref,
    whole_out, out_hbm, grad_hbm, rest_hbm, mine_ref,
    second_turned_ref, incoming_turned_ref, w_ref, terms_ref, got_ref, held_ref, active_ref, both_ref, out_ref, grad_ref, stage_ref,
    load_sem, store_sem, stage_sem, own_sem, ahead_send, ahead_recv, sum_send, sum_recv,
    *, tiles, ready, summed,
):
    dps = lax.axis_size("dp")
    chips = dps // 2
    seq, dpi = lax.axis_index("seq"), lax.axis_index("dp")
    chip, core = dpi // 2, dpi % 2
    length, model = second_ref.shape
    width = 3 * TILE
    later = own_ref.shape[1] // width if ready < tiles else 0
    loose = ready >= chips + 2
    above, below = ((chip + 1) % chips) * 2 + core, ((chip + chips - 1) % chips) * 2 + core
    greet([(seq, above), (seq, below), (seq, chip * 2 + 1 - core)])

    def columns(t):
        return pl.ds(pl.multiple_of(t * width, width), width)

    def load(t, source=first_hbm):
        return pltpu.make_async_copy(source.at[:, :, columns(t)], w_ref.at[t % 2], load_sem.at[t % 2])

    def start_load(t):
        pl.when(t < ready)(lambda: load(t).start())
        if later > 0:
            first = columns(t - ready)
            ahead = pltpu.make_async_copy(whole_out.at[:, :, first], w_ref.at[t % 2], load_sem.at[t % 2])
            pl.when(within(t, ready, tiles))(ahead.start)

    def store(t):
        return pltpu.make_async_copy(
            terms_ref.at[t % 3], rest_hbm.at[:, :, :, columns(t - summed)], store_sem.at[t % 3]
        )

    def gather(q):
        return ChipGather(
            whole_out, columns(q), (ahead_send.at[q], ahead_recv.at[q]), seq, dpi, chips, own_ref
        )

    def scatter(t):
        return ChipScatter(
            terms_ref.at[t % 3], got_ref.at[t], held_ref.at[t], (sum_send.at[t], sum_recv.at[t]), seq, dpi, chips
        )

    def within(value, low, high):
        return (value >= low) & (value < high)

    load(0).start()
    own = pltpu.make_async_copy(own_ref, whole_out.at[dpi], own_sem)
    own.start()
    out_ref[...] = jnp.zeros_like(out_ref)
    grad_ref[...] = jnp.zeros_like(grad_ref)

    @pl.loop(0, length // TILE)
    def _(i):
        at = slot_rows(i, TILE)
        second_turned_ref[:, at] = second_ref[at, :].T
        incoming_turned_ref[:, at] = incoming_ref[at, :].T

    own.wait()
    far = list(range(chips - 1, 0, -1))
    thirds = [far[: -(-len(far) // 3)], far[-(-len(far) // 3) : -(-2 * len(far) // 3)], far[-(-2 * len(far) // 3) :]]

    @pl.loop(0, tiles)
    def _(t):
        def sent_at(tick):
            q = tick - tick // 3 if loose else tick
            return (tick >= 0) & (q < later) & ((tick % 3 != 2) if loose else True), q

        def pass_on(s):
            if later > 0:
                one, q = sent_at(t - s)

                @pl.when(one)
                def _():
                    gather(q).came(s)
                    gather(q).send(s)

        def sum_on(part):
            if part == 0:
                pl.when(within(t - 1, 0, summed))(lambda: scatter(t - 1).take())
            v = t - 1 - part
            j = v - v // 3

            @pl.when((v >= 0) & (v % 3 != 2) & (j < summed))
            def _():
                sums = scatter(j)
                if part == 3:
                    sums.finish(mine_ref.at[j])
                else:
                    for r in thirds[part]:
                        sums.step(r)

        if later > 0:
            one, q = sent_at(t)
            pl.when(one)(lambda: gather(q).send(0))
            arrived, q_last = sent_at(t - chips)

            @pl.when(arrived)
            def _():
                for s in range(chips):
                    gather(q_last).came_across(s)
                    gather(q_last).sent(s)

        start_load(t + 1)
        pltpu.make_async_copy(
            first_hbm.at[:, :, pl.ds(0, width)], w_ref.at[t % 2], load_sem.at[t % 2]
        ).wait()
        pl.when(t - 3 >= summed)(lambda: store(t - 3).wait())

        w = w_ref[t % 2].reshape(model, width)
        for i in range(2):
            at = slice(i * length // 2, (i + 1) * length // 2)
            both = nn(second_ref[at, :], w[:, : 2 * TILE])
            back = nn(incoming_ref[at, :], w[:, 2 * TILE :])
            gate, up = both[:, :TILE], both[:, TILE:]
            sigma = jax.nn.sigmoid(gate)
            silu = gate * sigma
            active_ref[at, :] = (silu * up).astype(BF)
            both_ref[at, :TILE] = (back * up * sigma * (1.0 + gate * (1.0 - sigma))).astype(BF)
            both_ref[at, TILE:] = (back * silu).astype(BF)
        pass_on(1)
        sum_on(0)
        rows = (chips, 2, model // dps)
        terms_ref[t % 3, :, :, :, : 2 * TILE] = nn(second_turned_ref[...], both_ref[...], BF).reshape(rows + (2 * TILE,))
        terms_ref[t % 3, :, :, :, 2 * TILE :] = nn(incoming_turned_ref[...], active_ref[...], BF).reshape(rows + (TILE,))
        pl.when(t < summed)(lambda: scatter(t).give().start())
        pl.when(t >= summed)(lambda: store(t).start())
        for s in range(2, chips - 1):
            pass_on(s)
        sum_on(1)
        for i in range(2):
            at = slice(i * length // 2, (i + 1) * length // 2)
            w = w_ref[t % 2].reshape(model, width)
            grad_ref[at, :] += nt(both_ref[at, :], w[:, : 2 * TILE])
            out_ref[at, :] += nt(active_ref[at, :], w[:, 2 * TILE :])
            if i == 0:
                sum_on(2)
        pass_on(chips - 1)
        sum_on(3)

    for j in range(summed):
        for part in range(4):
            if 1 + j + j // 2 + part >= tiles:
                if part == 3:
                    scatter(j).finish(mine_ref.at[j])
                else:
                    for r in thirds[part]:
                        scatter(j).step(r)
    for t in range(max(summed, tiles - 3), tiles):
        store(t).wait()
    quarter = length // 4
    stores = []
    for i in range(8):
        src, dst = (grad_ref, grad_hbm) if i < 4 else (out_ref, out_hbm)
        at = pl.ds((i % 4) * quarter, quarter)
        if i >= 2:
            stores[i - 2].wait()
        stage_ref[i % 2] = src[at, :].astype(BF)
        stores.append(pltpu.make_async_copy(stage_ref.at[i % 2], dst.at[at], stage_sem.at[i % 2]))
        stores[-1].start()
    for copy in stores[-2:]:
        copy.wait()


def feed_call(second, incoming, first, own, summed):
    dps, share, columns = first.shape
    chips = dps // 2
    length, model = second.shape
    width = 3 * TILE
    ready = columns // width
    tiles = ready + own.shape[1] // width
    if tiles == ready:
        own = jnp.zeros((share, 128), BF)
    vmem, hbm = pl.BlockSpec(memory_space=pltpu.VMEM), pl.BlockSpec(memory_space=pl.ANY)
    shape, dma = jax.ShapeDtypeStruct, pltpu.SemaphoreType.DMA
    return pl.pallas_call(
        functools.partial(feed_kernel, tiles=tiles, ready=ready, summed=summed),
        out_shape=(
            shape((dps,) + own.shape, BF),
            shape((length, model), BF),
            shape((length, model), BF),
            shape((chips, 2, share, (tiles - summed) * width), BF),
            shape((summed, share, width), F32),
        ),
        in_specs=[vmem, vmem, hbm, vmem],
        out_specs=(hbm, hbm, hbm, hbm, vmem),
        scratch_shapes=[
            pltpu.VMEM((model, length), BF),
            pltpu.VMEM((model, length), BF),
            pltpu.VMEM((2, dps, share, width), BF),
            pltpu.VMEM((3, chips, 2, share, width), BF),
            pltpu.VMEM((summed, chips, share, width), BF),
            pltpu.VMEM((summed, chips + 1, share, width), BF),
            pltpu.VMEM((length, TILE), BF),
            pltpu.VMEM((length, 2 * TILE), BF),
            pltpu.VMEM((length, model), F32),
            pltpu.VMEM((length, model), F32),
            pltpu.VMEM((2, length // 4, model), BF),
            dma((2,)), dma((3,)), dma((2,)), dma,
            dma((max(tiles - ready, 1), 4, chips)), dma((max(tiles - ready, 1), 4, chips)),
            dma((summed, 3, chips)), dma((summed, 3, chips)),
        ],
        cost_estimate=pl.CostEstimate(flops=65 * 10**9, bytes_accessed=60 * 10**6, transcendentals=3 * 10**6),
        compiler_params=pltpu.CompilerParams(
            collective_id=4, has_side_effects=True, vmem_limit_bytes=63 * 2**20
        ),
        name="feed_forward",
    )(second, incoming, first, own)


def pack_kernel(gate_ref, up_ref, down_ref, first_ref, rest_ref):
    units = gate_ref.shape[1]
    split = first_ref.shape[1] // (3 * TILE)
    for t in range(-(-units // TILE)):
        size = min(TILE, units - t * TILE)
        ref, at = (first_ref, t) if t < split else (rest_ref, t - split)
        lanes = slice(t * TILE, t * TILE + size)
        for i, part in enumerate((gate_ref[:, lanes], up_ref[:, lanes], down_ref[:, lanes])):
            low = (3 * at + i) * TILE
            ref[:, low : low + size] = part
            if size < TILE:
                ref[:, low + size : low + TILE] = jnp.zeros((part.shape[0], TILE - size), BF)


def pack_call(gate, up, down, ready):
    rows, units = gate.shape
    tiles = -(-units // TILE)
    vmem = pl.BlockSpec(memory_space=pltpu.VMEM)
    width = 3 * TILE
    return pl.pallas_call(
        pack_kernel,
        out_shape=[
            jax.ShapeDtypeStruct((rows, ready * width), BF),
            jax.ShapeDtypeStruct((rows, max(tiles - ready, 1) * width), BF),
        ],
        in_specs=[vmem] * 3,
        out_specs=[vmem] * 2,
        cost_estimate=pl.CostEstimate(flops=0, bytes_accessed=10**7, transcendentals=0),
        compiler_params=pltpu.CompilerParams(vmem_limit_bytes=32 * 2**20),
        name="pack_weights",
    )(gate, up, down)


def unpack_kernel(summed_ref, rest_ref, *refs):
    count = len(refs) // 2 - 1
    gate_ref, up_ref, down_ref = refs[count : count + 3]
    for src, dst in zip(refs[:count], refs[count + 3 :]):
        dst[...] = src[...]
    units = gate_ref.shape[1]
    split = summed_ref.shape[0]
    for t in range(-(-units // TILE)):
        size = min(TILE, units - t * TILE)
        lanes = slice(t * TILE, t * TILE + size)
        for i in range(3):
            if t < split:
                part = summed_ref[t, :, i * TILE : i * TILE + size]
            else:
                low = (3 * (t - split) + i) * TILE
                part = rest_ref[:, low : low + size].astype(F32)
            (gate_ref, up_ref, down_ref)[i][:, lanes] = part


def unpack_call(summed, rest, units, *given):
    rows = rest.shape[0]
    vmem = pl.BlockSpec(memory_space=pltpu.VMEM)
    return pl.pallas_call(
        unpack_kernel,
        out_shape=[jax.ShapeDtypeStruct((rows, units), F32)] * 3
        + [jax.ShapeDtypeStruct(field.shape, field.dtype) for field in given],
        in_specs=[vmem] * (2 + len(given)),
        out_specs=[vmem] * (3 + len(given)),
        cost_estimate=pl.CostEstimate(flops=0, bytes_accessed=10**7, transcendentals=0),
        compiler_params=pltpu.CompilerParams(vmem_limit_bytes=32 * 2**20),
        name="unpack_gradients",
    )(summed, rest, *given)


def end_kernel(
    normed_grad_ref, hidden_grad_ref, x_ref, gain_ref, qkv_ref, out_ref, small_ref, feed_ref, hidden_hbm,
    input_grad_ref, qkv_out_ref, out_out_ref, small_out_ref, layer_out_ref,
    qkv_got_ref, out_got_ref, small_got_ref,
    qkv_move_ref, out_move_ref, small_move_ref, qkv_came_ref, out_came_ref, small_came_ref,
    came_ref, sums_ref, one_ref, two_ref, came2_ref, sums2_ref, one2_ref, two2_ref, hidden_ref,
    sum_send, sum_recv, sum2_send, sum2_recv, load_sem, core_send, core_recv, ring_send, ring_recv, seq_send, seq_recv,
):
    seqs, dps = lax.axis_size("seq"), lax.axis_size("dp")
    chips = dps // 2
    seq, dpi = lax.axis_index("seq"), lax.axis_index("dp")
    chip, core = dpi // 2, dpi % 2
    ahead = ((chip + 1) % chips) * 2 + core
    behind = ((chip + chips - 1) % chips) * 2 + core
    sibling = chip * 2 + 1 - core
    greet([(seq ^ k, dpi) for k in range(1, seqs)] + [(seq, other) for other in (ahead, behind, sibling)])
    rows = x_ref.shape[0]
    piece = rows // PIECES

    cores = [
        remote(src.at[..., 1 - core, :, :], dst, core_send.at[i], core_recv.at[i], (seq, sibling))
        for i, (src, dst) in enumerate(
            ((qkv_ref, qkv_got_ref), (out_ref, out_got_ref), (small_ref, small_got_ref))
        )
    ]
    for copy in cores:
        copy.start()
    total = SeqSum(normed_grad_ref, rows, came_ref, sums_ref, one_ref, two_ref, (sum_send, sum_recv), dpi, seq)
    total.begin()
    feed = SeqSum(feed_ref, rows, came2_ref, sums2_ref, one2_ref, two2_ref, (sum2_send, sum2_recv), dpi, seq)
    load = pltpu.make_async_copy(hidden_hbm.at[slot_rows(seq, rows)], hidden_ref, load_sem)
    load.start()
    for copy in cores:
        copy.wait_recv()

    def term(which, step):
        parts = [
            qkv_ref[:, which, core].astype(F32) + qkv_got_ref[:, which].astype(F32),
            out_ref[which, core].astype(F32) + out_got_ref[which].astype(F32),
            small_ref[which, core].astype(F32) + small_got_ref[which].astype(F32),
        ]
        if step > 0:
            came = (qkv_came_ref, out_came_ref, small_came_ref)
            parts = [part + field[step - 1].astype(F32) for part, field in zip(parts, came)]
        return parts

    def ring(step):
        return [
            remote(src.at[step], dst.at[step], ring_send.at[i, step], ring_recv.at[i, step], (seq, ahead))
            for i, (src, dst) in enumerate(
                ((qkv_move_ref, qkv_came_ref), (out_move_ref, out_came_ref), (small_move_ref, small_came_ref))
            )
        ]

    def input_piece(c):
        at = pl.ds(c * piece, piece)
        x = x_ref[at, :].astype(F32)
        factor = lax.rsqrt(jnp.mean(x * x, axis=-1, keepdims=True) + EPS)
        unit = x * factor
        scaled = total.take(c) * gain_ref[...]
        grad = scaled - unit * jnp.mean(scaled * unit, axis=-1, keepdims=True)
        input_grad_ref[at, :] = (hidden_grad_ref[at, :] + factor * grad).astype(BF)

    for step in range(chips - 1):
        if step > 0:
            for copy in ring(step - 1):
                copy.wait_recv()
        for field, part in zip((qkv_move_ref, out_move_ref, small_move_ref), term((chip + chips - 1 - step) % chips, step)):
            field[step] = part.astype(BF)
        for copy in ring(step):
            copy.start()
        if step == 0:
            total.middle()
            feed.begin()
        if step == 1:
            for c in range(PIECES):
                input_piece(c)
            feed.middle()
    load.wait()
    for c in range(PIECES):
        at = pl.ds(c * piece, piece)
        layer_out_ref[at, :] = (hidden_ref[at, :] + feed.take(c)).astype(BF)
    for copy in ring(chips - 2):
        copy.wait_recv()
    qkv, out, small = term(chip, chips - 1)
    out_out_ref[...] = out
    qkv_move_ref[chips - 1] = qkv.astype(BF)
    small_move_ref[chips - 1] = small.astype(BF)
    last = [
        remote(
            src, dst.at[seq], seq_send.at[i, k], seq_recv.at[i, k], (seq ^ k, dpi)
        )
        for k in range(1, seqs)
        for i, (src, dst) in enumerate(
            ((qkv_move_ref.at[chips - 1, seq ^ k], qkv_out_ref), (small_move_ref.at[chips - 1], small_out_ref))
        )
    ]
    for copy in last:
        copy.start()
    qkv_out_ref[seq] = qkv_move_ref[chips - 1, seq]
    small_out_ref[seq] = small_move_ref[chips - 1]
    total.finish()
    feed.finish()
    for copy in cores + [copy for step in range(chips - 1) for copy in ring(step)]:
        copy.wait_send()
    for copy in last:
        copy.wait()


def end_call(normed_grad, hidden_grad, x, gain, qkv, out, small, feed, hidden):
    seqs, chips, _, share, wide = qkv.shape
    rows, model = x.shape
    vmem = pl.BlockSpec(memory_space=pltpu.VMEM)
    shape, dma = jax.ShapeDtypeStruct, pltpu.SemaphoreType.DMA
    held = pltpu.VMEM((PIECES, rows // PIECES, model), BF)
    blocks = ((seqs, share, wide), (share, model), small.shape[2:])
    return pl.pallas_call(
        end_kernel,
        out_shape=(
            shape((rows, model), BF),
            shape(blocks[0], BF),
            shape(blocks[1], F32),
            shape((seqs,) + blocks[2], BF),
            shape((rows, model), BF),
        ),
        in_specs=[vmem] * 8 + [pl.BlockSpec(memory_space=pl.ANY)],
        out_specs=(vmem,) * 5,
        scratch_shapes=[
            pltpu.VMEM((seqs, chips, share, wide), BF),
            pltpu.VMEM((chips, share, model), BF),
            pltpu.VMEM((chips,) + blocks[2], BF),
        ]
        + [pltpu.VMEM((chips,) + block, BF) for block in blocks]
        + [pltpu.VMEM((chips - 1,) + block, BF) for block in blocks]
        + [
            held, held, held, held, held, held, held, held, pltpu.VMEM((rows, model), F32),
            dma((3, PIECES)), dma((3, PIECES)), dma((3, PIECES)), dma((3, PIECES)), dma, dma((3,)), dma((3,)),
            dma((3, chips)), dma((3, chips)), dma((2, seqs)), dma((2, seqs)),
        ],
        cost_estimate=pl.CostEstimate(flops=10**8, bytes_accessed=2 * 10**7, transcendentals=0),
        compiler_params=pltpu.CompilerParams(
            collective_id=3, has_side_effects=True, vmem_limit_bytes=48 * 2**20
        ),
        name="end_sums",
    )(normed_grad, hidden_grad, x, gain[None], qkv, out, small, feed, hidden)


def pair_tiles(left, right):
    units = left.shape[1]
    cuts = list(range(0, units, TILE)) + [units]
    return jnp.concatenate(
        [field[:, low:high] for low, high in zip(cuts[:-1], cuts[1:]) for field in (left, right)], axis=1
    )


def split_tiles(both):
    units = both.shape[1] // 2
    cuts = list(range(0, units, TILE)) + [units]
    spans = list(zip(cuts[:-1], cuts[1:]))
    return (
        jnp.concatenate([both[:, 2 * low : low + high] for low, high in spans], axis=1),
        jnp.concatenate([both[:, low + high : 2 * high] for low, high in spans], axis=1),
    )


def shards(
    inputs,
    block_ids,
    cotangent,
    first_gain,
    query_weight,
    query_bias,
    key_weight,
    key_bias,
    value_weight,
    value_bias,
    output_weight,
    second_gain,
    gate_weight,
    up_weight,
    down_weight,
):
    seqs = lax.axis_size("seq")
    seq = lax.axis_index("seq")
    dps = lax.axis_size("dp")
    dpi = lax.axis_index("dp")
    chips, chip, core = dps // 2, dpi // 2, dpi % 2
    heads = H // seqs
    copies = seqs // KEY_VALUE_HEADS
    wq = heads * HEAD_SIZE
    wide = wq + 2 * HEAD_SIZE
    tokens_here, model = inputs.shape[1:]
    share = first_gain.shape[0]
    kv_share = key_bias.shape[0]
    hidden_units = gate_weight.shape[1]

    small = jnp.concatenate([first_gain, second_gain, query_bias, key_bias, value_bias])
    packed = jnp.concatenate(
        [
            query_weight.reshape(share, seqs, wq),
            jnp.repeat(key_weight.reshape(share, KEY_VALUE_HEADS, HEAD_SIZE), copies, axis=1),
            jnp.repeat(value_weight.reshape(share, KEY_VALUE_HEADS, HEAD_SIZE), copies, axis=1),
        ],
        axis=-1,
    ).transpose(1, 0, 2)
    one = small.shape[0]
    small = jnp.pad(small[None], ((0, 15), (0, -one % 128)))
    tiles = -(-hidden_units // TILE)
    ready = READY if chips <= 4 else tiles
    first, later = pack_call(gate_weight, up_weight, down_weight.T, ready)
    later = later if ready < tiles else later[:, :0]
    first = lax.all_gather(first, "dp", axis=0, tiled=True).reshape(dps, model // dps, -1)
    tokens, incoming, blocks, smalls, weight_qkv, weight_out = start_call(
        inputs[0], cotangent[0], block_ids.reshape(-1, 128), small, packed, output_weight
    )
    blocks = blocks.reshape(-1)
    weight_qkv = weight_qkv.reshape(model, wide)
    out_head = weight_out[0].reshape(dps * share, model)
    weight_out = weight_out.reshape(model, model)
    smalls = smalls[:, :, 0, :one].transpose(1, 0, 2).astype(F32)
    gain_first = smalls[:, :, :share].reshape(model)
    gain_second = smalls[:, :, share : 2 * share].reshape(model)
    bias_q = lax.dynamic_index_in_dim(smalls, seq, 0, keepdims=False)[:, 2 * share : 3 * share].reshape(wq)
    group = seq // copies
    bias_k = smalls[:, :, 3 * share : 3 * share + kv_share].reshape(KEY_VALUE_HEADS, HEAD_SIZE)
    bias_v = smalls[:, :, 3 * share + kv_share :].reshape(KEY_VALUE_HEADS, HEAD_SIZE)
    bias = jnp.concatenate(
        [
            bias_q,
            lax.dynamic_index_in_dim(bias_k, group, 0, keepdims=False),
            lax.dynamic_index_in_dim(bias_v, group, 0, keepdims=False),
        ]
    )
    length = tokens.shape[0]
    cosine, sine = rope_tables(length)

    normed, qkv, mixed, logsum, hidden, second = attend_call(
        tokens, weight_qkv, bias[None], cosine, sine, blocks, gain_first, gain_second, weight_out
    )
    second, out_head = lax.optimization_barrier((second, out_head))
    _, out_sum, second_sum, rest, summed = feed_call(second, incoming, first, later, SUMMED)
    rest = rest.reshape(model, -1)
    rest = lax.psum_scatter(rest, "dp", scatter_dimension=0, tiled=True)
    normed_grad, grad_hidden, qkv_grad, out_weight_grad, bias_grad, gain_one_grad, gain_two_grad = backward_call(
        second_sum, cotangent[0], gain_first, gain_second, logsum, cosine, sine, blocks,
        hidden, tokens, normed, weight_qkv, out_head, qkv, mixed,
    )
    bias_grad, gain_one_grad, gain_two_grad = bias_grad[0], gain_one_grad[0], gain_two_grad[0]

    place = lambda field, count, at: jnp.where(
        (jnp.arange(count) == at)[:, None], field[None], 0.0
    ).reshape(seqs, dps, -1)
    small_grad = jnp.concatenate(
        [
            gain_one_grad.reshape(seqs, dps, share),
            gain_two_grad.reshape(seqs, dps, share),
            place(bias_grad[:wq], seqs, seq),
            place(bias_grad[wq : wq + HEAD_SIZE], KEY_VALUE_HEADS, group),
            place(bias_grad[wq + HEAD_SIZE :], KEY_VALUE_HEADS, group),
        ],
        axis=-1,
    )
    small_rows = -(-seqs * one // wide)
    small_grad = small_grad.transpose(1, 0, 2).reshape(dps, seqs * one).astype(BF)
    small_grad = jnp.pad(small_grad, ((0, 0), (0, small_rows * wide - seqs * one)))
    small_grad = jnp.pad(small_grad.reshape(dps, -1, wide), ((0, 0), (0, 16 - small_rows), (0, 0)))
    input_grad, parts, out_weight_grad, smalls, layer_out = end_call(
        normed_grad, grad_hidden, inputs[0], gain_first,
        qkv_grad.reshape(seqs, chips, 2, share, wide),
        out_weight_grad.reshape(chips, 2, share, model),
        small_grad.reshape(chips, 2, 16, wide),
        out_sum, hidden,
    )
    smalls = smalls[:, :small_rows].reshape(seqs, -1)[:, : seqs * one].reshape(seqs, seqs, one)
    small_sum = jnp.sum(
        lax.dynamic_index_in_dim(smalls, seq, 1, keepdims=False).astype(F32), axis=0
    )
    query_weight_grad = jnp.concatenate([part[:share, :wq] for part in parts], axis=1).astype(F32)
    pairs = [
        sum(part[:share, wq:].astype(F32) for part in parts[g * copies : (g + 1) * copies])
        for g in range(KEY_VALUE_HEADS)
    ]
    key_weight_grad = jnp.concatenate([pair[:, :HEAD_SIZE] for pair in pairs], axis=1)
    value_weight_grad = jnp.concatenate([pair[:, HEAD_SIZE:] for pair in pairs], axis=1)
    gain_one_grad, gain_two_grad, query_bias_grad, key_bias_grad, value_bias_grad = jnp.split(
        small_sum, [share, 2 * share, 3 * share, 3 * share + kv_share]
    )

    gate_grad, up_grad, down_grad, layer_out, input_grad, out_weight_grad = unpack_call(
        summed, rest, hidden_units, layer_out, input_grad, out_weight_grad
    )
    return (
        layer_out[None],
        input_grad[None],
        gain_one_grad,
        query_weight_grad,
        query_bias_grad,
        key_weight_grad,
        key_bias_grad,
        value_weight_grad,
        value_bias_grad,
        out_weight_grad,
        gain_two_grad,
        gate_grad,
        up_grad,
        down_grad.T,
    )


def solution(mesh):
    tokens = P("dp", "seq", None)
    whole = P(("seq", "dp"))
    matrix = P(("seq", "dp"), None)
    feed = P("dp", "seq")
    in_specs = (
        tokens,
        P("dp", "seq"),
        tokens,
        whole,
        matrix,
        whole,
        matrix,
        whole,
        matrix,
        whole,
        matrix,
        whole,
        feed,
        feed,
        P("seq", "dp"),
    )
    out_specs = (
        tokens,
        tokens,
        whole,
        matrix,
        whole,
        matrix,
        whole,
        matrix,
        whole,
        matrix,
        whole,
        feed,
        feed,
        P("seq", "dp"),
    )
    return jax.shard_map(shards, mesh=mesh, in_specs=in_specs, out_specs=out_specs, check_vma=False)
```

```python
import functools

import jax
import jax.numpy as jnp
import numpy as np
from jax import lax
from jax.experimental import pallas as pl
from jax.experimental.pallas import tpu as pltpu
from jax.sharding import PartitionSpec as P

H = 12
KEY_VALUE_HEADS = 2
HEAD_SIZE = 128
EPS = 1e-06
THETA = 1000000.0
SCALE = HEAD_SIZE ** (-0.5)
BF = jnp.bfloat16
F32 = jnp.float32


def dot(a, b, dims, out=F32):
    return lax.dot_general(a, b, (dims, ((), ())), preferred_element_type=F32).astype(out)


def nn(a, b, out=F32):
    return dot(a, b, ((1,), (0,)), out)


def nt(a, b, out=F32):
    return dot(a, b, ((1,), (1,)), out)


def tn(a, b, out=F32):
    return dot(a, b, ((0,), (0,)), out)


def rope_tables(length):
    exponent = np.arange(0, HEAD_SIZE, 2).astype(np.float32) / np.float32(HEAD_SIZE)
    freqs = np.float32(THETA) ** (-exponent)
    angles = np.arange(length).astype(np.float32)[:, None] * freqs[None, :]
    cosine, sine = np.cos(angles), np.sin(angles)
    return (
        jnp.asarray(np.concatenate([cosine, cosine], axis=-1), F32),
        jnp.asarray(np.concatenate([-sine, sine], axis=-1), F32),
    )


def remote(src, dst, send, recv, where):
    return pltpu.make_async_remote_copy(
        src_ref=src, dst_ref=dst, send_sem=send, recv_sem=recv,
        device_id=where, device_id_type=pl.DeviceIdType.MESH,
    )


def greet(partners):
    barrier = pltpu.get_barrier_semaphore()
    for partner in partners:
        pl.semaphore_signal(barrier, inc=1, device_id=partner, device_id_type=pl.DeviceIdType.MESH)
    pl.semaphore_wait(barrier, len(partners))


def far_sends(field, half, seq, dpi, send, recv):
    def rows(k, low):
        return field.at[pl.ds(pl.multiple_of((seq ^ k) * 2 * half + low, half), half)]

    return [
        remote(rows(2, 0), rows(2, 0), send.at[0], recv.at[0], (seq ^ 1, dpi)),
        remote(rows(1, half), rows(1, half), send.at[1], recv.at[1], (seq ^ 2, dpi)),
    ]


def start_kernel(
    x_in, c_in, ids_in, small_in, pack_in, out_in,
    x_out, c_out, ids_out, small_out, pack_out, out_out,
    local_sem, seq_send, seq_recv, far_send, far_recv, ring_send, ring_recv, core_send, core_recv,
    out_send, out_recv, slot_send, slot_recv,
):
    seqs, dps = lax.axis_size("seq"), lax.axis_size("dp")
    chips = dps // 2
    seq, dpi = lax.axis_index("seq"), lax.axis_index("dp")
    chip, core = dpi // 2, dpi % 2
    sibling = chip * 2 + 1 - core
    others = [((chip + h) % chips) * 2 + core for h in range(1, chips)]
    greet([(seq ^ k, dpi) for k in range(1, seqs)] + [(seq, other) for other in others + [sibling]])

    rows = x_in.shape[0]
    half = rows // 2

    def to_slots(i, src, dst, slots):
        return [remote(src, dst, seq_send.at[i, k], seq_recv.at[i, k], (seq ^ k, dpi)) for k in slots]

    def block(index, low=0, count=rows):
        return pl.ds(pl.multiple_of(index * rows + low, half), count)

    small_sends = to_slots(0, small_in, small_out.at[dpi, seq], range(1, seqs))
    pack_sends = [
        remote(
            pack_in.at[seq ^ k], pack_out.at[seq, dpi], seq_send.at[1, k], seq_recv.at[1, k], (seq ^ k, dpi)
        )
        for k in range(1, seqs)
    ]
    id_sends = to_slots(2, ids_in, ids_out.at[seq], range(1, seqs))
    x_sends = to_slots(3, x_in, x_out.at[block(seq)], (1, 2))
    c_sends = to_slots(4, c_in, c_out.at[block(seq)], (1, 2))
    locals_ = [
        pltpu.make_async_copy(small_in, small_out.at[dpi, seq], local_sem.at[0]),
        pltpu.make_async_copy(pack_in.at[seq], pack_out.at[seq, dpi], local_sem.at[1]),
        pltpu.make_async_copy(out_in, out_out.at[0, dpi], local_sem.at[2]),
        pltpu.make_async_copy(ids_in, ids_out.at[seq], local_sem.at[3]),
        pltpu.make_async_copy(x_in, x_out.at[block(seq)], local_sem.at[4]),
        pltpu.make_async_copy(c_in, c_out.at[block(seq)], local_sem.at[5]),
    ]
    def fields(at, which):
        every = (out_out.at[0, at], small_out.at[at], pack_out.at[:, at])
        return [(i, every[i]) for i in which]

    def hop_sends(hop, which):
        to = ((chip + chips - hop) % chips) * 2 + core
        return [
            remote(out_in if i == 0 else field, field, ring_send.at[i, hop], ring_recv.at[i, hop], (seq, to))
            for i, field in fields(dpi, which)
        ]

    def core_sends(hop, which=(0, 1, 2)):
        at = ((chip + hop) % chips) * 2 + core
        return [
            remote(field, field, core_send.at[i, hop], core_recv.at[i, hop], (seq, sibling))
            for i, field in fields(at, which)
        ]

    def out_sends(hop):
        at = ((chip + hop) % chips) * 2 + core
        src = out_out.at[0, at] if hop else out_in
        return [
            remote(src, out_out.at[k, at], out_send.at[k, hop], out_recv.at[k, hop], (seq ^ k, dpi))
            for k in range(1, seqs)
        ]

    line = chips == 4
    order = [2, 1, 3] if line else sorted(range(1, chips), key=lambda hop: min(hop, chips - hop))
    ends = ((1, chip != 0), (3, chip != chips - 1))

    def hops_do(which, what):
        for hop in order:
            for copy in hop_sends(hop, which):
                if line and hop != 2:
                    pl.when(dict(ends)[hop])(getattr(copy, what))
                else:
                    getattr(copy, what)()

    def relays(which):
        low = chip == 2
        end, far = jnp.where(low, 3, 0), jnp.where(low, 0, 3)
        return [
            remote(field, field, ring_send.at[i, 0], ring_recv.at[i, jnp.where(low, 1, 3)], (seq, end * 2 + core))
            for i, field in fields(far * 2 + core, which)
        ]

    def relay(which, what):
        if line:
            for copy in relays(which):
                pl.when((chip == 1) | (chip == 2))(getattr(copy, what))

    flying, outs = [], []
    hops_do((0,), "start")
    first = small_sends + pack_sends + locals_[:3] + x_sends + id_sends + locals_[3:]
    for copy in first:
        copy.start()
    for copy in locals_[:3] + small_sends + pack_sends:
        copy.wait()
    hops_do((1, 2), "start")
    for hop in [0] + order:
        if hop > 0:
            for copy in hop_sends(hop, (0,)):
                copy.wait_recv()
            if hop == 2:
                relay((0,), "start")
        cores, more = core_sends(hop, (0,)), out_sends(hop)
        for copy in cores + more:
            copy.start()
        flying += cores
        outs += more
    for copy in x_sends:
        copy.wait()
    far_x = far_sends(x_out, half, seq, dpi, far_send.at[0], far_recv.at[0])
    for copy in far_x + c_sends:
        copy.start()
    for hop in [0] + order:
        if hop > 0:
            for copy in hop_sends(hop, (1, 2)):
                copy.wait_recv()
            if hop == 2:
                relay((1, 2), "start")
        cores = core_sends(hop, (1, 2))
        for copy in cores:
            copy.start()
        flying += cores
    for copy in c_sends:
        copy.wait()
    far_c = far_sends(c_out, half, seq, dpi, far_send.at[1], far_recv.at[1])
    for copy in far_c:
        copy.start()
    for copy in outs:
        copy.wait_recv()
    slots = [
        remote(
            out_out.at[k, ((chip + hop) % chips) * 2 + core], out_out.at[k, ((chip + hop) % chips) * 2 + core],
            slot_send.at[k, hop], slot_recv.at[k, hop], (seq, sibling),
        )
        for k in range(1, seqs)
        for hop in range(chips)
    ]
    for copy in slots:
        copy.start()
    hops_do((0, 1, 2), "wait_send")
    relay((0, 1, 2), "wait_send")
    for copy in flying + outs:
        copy.wait_send()
    for hop in range(chips):
        for copy in core_sends(hop):
            copy.wait_recv()
    for copy in slots + far_x + far_c + id_sends + locals_[3:]:
        copy.wait()


def start_call(x, c, ids, small, pack, out):
    seqs, dps = lax.axis_size("seq"), lax.axis_size("dp")
    chips = dps // 2
    share, wide = pack.shape[1:]
    any_space = pl.BlockSpec(memory_space=pl.ANY)
    shapes = (
        jax.ShapeDtypeStruct((seqs * x.shape[0], x.shape[1]), x.dtype),
        jax.ShapeDtypeStruct((seqs * c.shape[0], c.shape[1]), c.dtype),
        jax.ShapeDtypeStruct((seqs,) + ids.shape, ids.dtype),
        jax.ShapeDtypeStruct((dps, seqs) + small.shape, small.dtype),
        jax.ShapeDtypeStruct((seqs, dps, share, wide), pack.dtype),
        jax.ShapeDtypeStruct((seqs, dps) + out.shape, out.dtype),
    )
    dma = pltpu.SemaphoreType.DMA
    return pl.pallas_call(
        start_kernel,
        out_shape=shapes,
        in_specs=[pl.BlockSpec(memory_space=pltpu.VMEM)] * 6,
        out_specs=(any_space,) * 6,
        scratch_shapes=[
            dma((6,)), dma((5, seqs)), dma((5, seqs)), dma((2, 2)), dma((2, 2)),
            dma((3, chips)), dma((3, chips)), dma((3, chips)), dma((3, chips)),
            dma((seqs, chips)), dma((seqs, chips)), dma((seqs, chips)), dma((seqs, chips)),
        ],
        compiler_params=pltpu.CompilerParams(collective_id=0, has_side_effects=True),
        name="start_gather",
    )(x, c, ids, small, pack, out)


def attend_kernel(
    x_ref, w_ref, bias_ref, cos_ref, sin_ref, ids_row_ref, ids_col_ref, gain_one_ref, gain_two_ref, out_ref,
    normed_ref, qkv_ref, mixed_ref, lse_ref, hidden_ref, second_ref,
    all_ref, send_sem, recv_sem,
):
    seqs = lax.axis_size("seq")
    seq, dpi = lax.axis_index("seq"), lax.axis_index("dp")
    greet([(seq ^ k, dpi) for k in range(1, seqs)])
    length, model = x_ref.shape
    wq = mixed_ref.shape[1]
    heads = wq // HEAD_SIZE
    rows = length // seqs
    @pl.loop(0, seqs)
    def _(i):
        at = pl.ds(pl.multiple_of(i * rows, rows), rows)
        x = x_ref[at, :].astype(F32)
        factor = lax.rsqrt(jnp.mean(x * x, axis=-1, keepdims=True) + EPS)
        normed_ref[at, :] = (x * factor * gain_one_ref[...]).astype(BF)

    @pl.loop(0, 2)
    def _(i):
        at = pl.ds(pl.multiple_of(i * 2 * rows, 2 * rows), 2 * rows)
        pre = jnp.dot(normed_ref[at, :], w_ref[...], preferred_element_type=F32) + bias_ref[...]
        cosine, sine = cos_ref[at, :], sin_ref[at, :]
        for h in range(heads + 1):
            u = pre[:, h * HEAD_SIZE : (h + 1) * HEAD_SIZE]
            turned = pltpu.roll(u, HEAD_SIZE // 2, 1)
            qkv_ref[at, h * HEAD_SIZE : (h + 1) * HEAD_SIZE] = (u * cosine + turned * sine).astype(BF)
        qkv_ref[at, wq + HEAD_SIZE :] = pre[:, wq + HEAD_SIZE :].astype(BF)

    copies = []
    for t in range(seqs):
        at = slice(t * rows, (t + 1) * rows)
        reach = min(t + 2, seqs) * rows
        keys = qkv_ref[:reach, wq : wq + HEAD_SIZE]
        values = qkv_ref[:reach, wq + HEAD_SIZE :]
        allowed = ids_row_ref[:, :reach] <= ids_col_ref[at, :]
        sums = []
        for h in range(heads):
            lanes = slice(h * HEAD_SIZE, (h + 1) * HEAD_SIZE)
            scores = nt(qkv_ref[at, lanes], keys) * SCALE
            scores = jnp.where(allowed, scores, -1000000000.0)
            peak = jnp.max(scores, axis=-1, keepdims=True)
            raised = jnp.exp(scores - peak)
            total = jnp.sum(raised, axis=-1, keepdims=True)
            low = (raised * (1.0 / total)).astype(BF)
            mixed_ref[at, lanes] = nn(low, values).astype(BF)
            sums.append(peak + jnp.log(total))
        lse_ref[at, :heads] = jnp.concatenate(sums, axis=1)
        more = [
            remote(
                mixed_ref.at[pl.ds(t * rows, rows)], all_ref.at[pl.ds(t * rows, rows), pl.ds(k * wq, wq)],
                send_sem.at[k, t], recv_sem.at[k, t], (seq ^ k, dpi),
            )
            for k in range(1, seqs)
        ]
        for copy in more:
            copy.start()
        copies.append(more)
        all_ref[at, :wq] = mixed_ref[at, :]

    for t in range(seqs):
        at = slice(t * rows, (t + 1) * rows)
        for copy in copies[t]:
            copy.wait_recv()
        hidden = x_ref[at, :].astype(F32) + nn(all_ref[at, :], out_ref[...])
        hidden_ref[at, :] = hidden
        factor = lax.rsqrt(jnp.mean(hidden * hidden, axis=-1, keepdims=True) + EPS)
        second_ref[at, :] = (hidden * factor * gain_two_ref[...]).astype(BF)
    for t in range(seqs):
        for copy in copies[t]:
            copy.wait_send()


def attend_call(x, w, bias, cosine, sine, ids, gain_one, gain_two, out):
    seqs = lax.axis_size("seq")
    length, model = x.shape
    wide = w.shape[1]
    wq = wide - 2 * HEAD_SIZE
    vmem = pl.BlockSpec(memory_space=pltpu.VMEM)
    shape = jax.ShapeDtypeStruct
    return pl.pallas_call(
        attend_kernel,
        out_shape=(
            shape((length, model), BF),
            shape((length, wide), BF),
            shape((length, wq), BF),
            shape((length, 128), F32),
            shape((length, model), F32),
            shape((length, model), BF),
        ),
        in_specs=[vmem] * 10,
        out_specs=(vmem,) * 6,
        scratch_shapes=[
            pltpu.VMEM((length, seqs * wq), BF),
            pltpu.SemaphoreType.DMA((seqs, seqs)),
            pltpu.SemaphoreType.DMA((seqs, seqs)),
        ],
        cost_estimate=pl.CostEstimate(flops=9 * 10**9, bytes_accessed=30 * 10**6, transcendentals=3 * 10**6),
        compiler_params=pltpu.CompilerParams(
            collective_id=1, has_side_effects=True, vmem_limit_bytes=60 * 2**20
        ),
        name="attend",
    )(x, w, bias, cosine, sine, ids[None], ids[:, None], gain_one[None], gain_two[None], out)


PIECES = 4
READY = 6
SUMMED = 4


def slot_rows(index, rows):
    return pl.ds(pl.multiple_of(index * rows, rows), rows)


class SeqSum:
    def __init__(self, field, rows, came, sums, from_one, from_two, sems, dpi, seq):
        self.field, self.rows, self.piece = field, rows, rows // PIECES
        self.came, self.sums, self.got = came, sums, {1: from_one, 2: from_two}
        self.send, self.recv = sems
        self.dpi, self.seq = dpi, seq
        self.started = []

    def at(self, k, c):
        start = (self.seq ^ k) * self.rows + c * self.piece
        return pl.ds(pl.multiple_of(start, self.piece), self.piece)

    def pass_on(self, c):
        by = 1 + c % 2
        return remote(
            self.field.at[self.at(3, c)], self.came.at[c], self.send.at[0, c], self.recv.at[0, c], (self.seq ^ by, self.dpi)
        )

    def direct(self, k, c):
        late = (k == 2) == (c % 2 == 0)
        src = self.sums.at[c] if late else self.field.at[self.at(k, c)]
        return remote(src, self.got[k].at[c], self.send.at[k, c], self.recv.at[k, c], (self.seq ^ k, self.dpi))

    def begin(self):
        for c in range(PIECES):
            self.pass_on(c).start()
            self.direct(1 + c % 2, c).start()

    def middle(self):
        for c in range(PIECES):
            k = 2 - c % 2
            self.pass_on(c).wait_recv()
            own = self.field[self.at(k, c), :].astype(F32)
            self.sums[c] = (self.came[c].astype(F32) + own).astype(BF)
            self.direct(k, c).start()

    def take(self, c):
        for k in (1, 2):
            self.direct(k, c).wait_recv()
        total = self.field[self.at(0, c), :].astype(F32) + self.got[1][c].astype(F32)
        return total + self.got[2][c].astype(F32)

    def finish(self):
        for c in range(PIECES):
            self.pass_on(c).wait_send()
            for k in (1, 2):
                self.direct(k, c).wait_send()


def backward_kernel(
    second_grad_ref, cotangent_ref, gain_one_ref, gain_two_ref, lse_ref, cos_ref, sin_ref,
    ids_row_ref, ids_col_ref, hidden_hbm, tokens_hbm, normed_hbm, w_hbm, out_hbm, qkv_hbm, mixed_hbm,
    normed_grad_ref, hidden_grad_ref, w_grad_ref, out_grad_ref, bias_grad_ref, gain_grad_ref, gain_two_grad_ref,
    hidden_ref, tokens_ref, normed_ref, w_ref, out_ref, qkv_ref, mixed_ref,
    branch_ref, mixed_grad_ref, pre_grad_ref, key_grad_ref, value_grad_ref,
    came_ref, sums_ref, one_ref, two_ref,
    load_sem, sum_send, sum_recv, branch_send, branch_recv,
):
    seqs = lax.axis_size("seq")
    seq, dpi = lax.axis_index("seq"), lax.axis_index("dp")
    length, model = second_grad_ref.shape
    rows = length // seqs
    piece = rows // PIECES
    wq = mixed_ref.shape[1]
    heads = wq // HEAD_SIZE
    loads = [
        pltpu.make_async_copy(src, dst, load_sem.at[i])
        for i, (src, dst) in enumerate(
            (
                (hidden_hbm.at[slot_rows(seq, rows)], hidden_ref),
                (out_hbm, out_ref), (qkv_hbm, qkv_ref), (w_hbm, w_ref),
                (tokens_hbm, tokens_ref), (normed_hbm, normed_ref), (mixed_hbm, mixed_ref),
            )
        )
    ]
    for load in loads:
        load.start()
    greet([(seq ^ k, dpi) for k in range(1, seqs)])

    total = SeqSum(second_grad_ref, rows, came_ref, sums_ref, one_ref, two_ref, (sum_send, sum_recv), dpi, seq)
    total.begin()
    loads[0].wait()
    total.middle()

    def branch_at(k, c):
        start = (seq ^ k) * rows + c * piece
        return branch_ref.at[pl.ds(pl.multiple_of(start, piece), piece)]

    def branch_copy(k, c):
        if k < 3:
            return remote(
                branch_at(0, c), branch_at(0, c), branch_send.at[k, c], branch_recv.at[k, c], (seq ^ k, dpi)
            )
        came, to = (2, 1) if c % 2 == 0 else (1, 2)
        return remote(
            branch_at(came, c), branch_at(came, c), branch_send.at[3, c], branch_recv.at[3, c], (seq ^ to, dpi)
        )

    gain_two_grad_ref[...] = jnp.zeros_like(gain_two_grad_ref)
    for c in range(PIECES):
        at = pl.ds(c * piece, piece)
        grad = total.take(c)
        hidden = hidden_ref[at, :]
        factor = lax.rsqrt(jnp.mean(hidden * hidden, axis=-1, keepdims=True) + EPS)
        unit = hidden * factor
        gain_two_grad_ref[...] += jnp.sum(grad * unit, axis=0, keepdims=True)
        scaled = grad * gain_two_ref[...]
        grad = cotangent_ref[at, :].astype(F32) + factor * (
            scaled - unit * jnp.mean(scaled * unit, axis=-1, keepdims=True)
        )
        hidden_grad_ref[at, :] = grad
        start = pl.multiple_of(seq * rows + c * piece, piece)
        branch_ref[pl.ds(start, piece), :] = grad.astype(BF)
        for k in (1, 2):
            branch_copy(k, c).start()
    total.finish()
    for load in loads[1:3]:
        load.wait()

    key_grad_ref[...] = jnp.zeros_like(key_grad_ref)
    value_grad_ref[...] = jnp.zeros_like(value_grad_ref)

    def rot_back(w, at):
        return w * cos_ref[at, :] + pltpu.roll(w * sin_ref[at, :], HEAD_SIZE // 2, 1)

    def attend_back(k):
        at = slot_rows(seq ^ k, rows)
        mixed_grad_ref[at, :] = nt(branch_ref[at, :], out_ref[...]).astype(BF)
        allowed = ids_row_ref[...] <= ids_col_ref[at, :]
        keys = qkv_ref[:, wq : wq + HEAD_SIZE]
        values = qkv_ref[:, wq + HEAD_SIZE :]
        for h in range(heads):
            lanes = slice(h * HEAD_SIZE, (h + 1) * HEAD_SIZE)
            queries = qkv_ref[at, lanes]
            grad = mixed_grad_ref[at, lanes]
            scores = jnp.where(allowed, nt(queries, keys) * SCALE, -1000000000.0)
            probs = jnp.exp(scores - lse_ref[at, h : h + 1])
            prob_grad = nt(grad, values)
            delta = jnp.sum(probs * prob_grad, axis=-1, keepdims=True)
            score_grad = (probs * (prob_grad - delta)).astype(BF)
            pre_grad_ref[at, lanes] = rot_back(nn(score_grad, keys) * SCALE, at).astype(BF)
            key_grad_ref[...] += tn(score_grad, queries)
            value_grad_ref[...] += tn(probs.astype(BF), grad)

    attend_back(0)
    for k in (1, 2):
        for c in range(PIECES):
            branch_copy(k, c).wait_recv()
            if (k == 2) == (c % 2 == 0):
                branch_copy(3, c).start()
        attend_back(k)
    for c in range(PIECES):
        branch_copy(3, c).wait_recv()
    attend_back(3)
    for c in range(PIECES):
        for k in (1, 2, 3):
            branch_copy(k, c).wait_send()

    every = pl.ds(0, length)
    pre_grad_ref[:, wq : wq + HEAD_SIZE] = rot_back(key_grad_ref[...] * SCALE, every).astype(BF)
    pre_grad_ref[:, wq + HEAD_SIZE :] = value_grad_ref[...].astype(BF)
    bias_grad_ref[...] = jnp.sum(pre_grad_ref[...].astype(F32), axis=0, keepdims=True)
    for load in loads[3:]:
        load.wait()
    gain_grad_ref[...] = jnp.zeros_like(gain_grad_ref)

    @pl.loop(0, seqs)
    def _(i):
        at = slot_rows(i, rows)
        grad = nt(pre_grad_ref[at, :], w_ref[...])
        x = tokens_ref[at, :].astype(F32)
        factor = lax.rsqrt(jnp.mean(x * x, axis=-1, keepdims=True) + EPS)
        gain_grad_ref[...] += jnp.sum(grad * (x * factor), axis=0, keepdims=True)
        normed_grad_ref[at, :] = grad.astype(BF)

    @pl.loop(0, model // wq)
    def _(i):
        lanes = pl.ds(pl.multiple_of(i * wq, HEAD_SIZE), wq)
        w_grad_ref[pl.ds(pl.multiple_of(i * wq, HEAD_SIZE), wq), :] = tn(normed_ref[:, lanes], pre_grad_ref[...]).astype(BF)
        out_grad_ref[:, lanes] = tn(mixed_ref[...], branch_ref[:, lanes]).astype(BF)


def backward_call(
    second_grad, cotangent, gain_one, gain_two, logsum, cosine, sine, ids, hidden, tokens, normed, w, out, qkv, mixed
):
    seqs = lax.axis_size("seq")
    length, model = tokens.shape
    rows = length // seqs
    wide = w.shape[1]
    wq = mixed.shape[1]
    vmem, hbm = pl.BlockSpec(memory_space=pltpu.VMEM), pl.BlockSpec(memory_space=pl.ANY)
    shape, dma = jax.ShapeDtypeStruct, pltpu.SemaphoreType.DMA
    held = pltpu.VMEM((PIECES, rows // PIECES, model), BF)
    return pl.pallas_call(
        backward_kernel,
        out_shape=(
            shape((length, model), BF),
            shape((rows, model), F32),
            shape((model, wide), BF),
            shape((wq, model), BF),
            shape((1, wide), F32),
            shape((1, model), F32),
            shape((1, model), F32),
        ),
        in_specs=[vmem] * 9 + [hbm] * 7,
        out_specs=(vmem,) * 7,
        scratch_shapes=[pltpu.VMEM((rows, model), F32)]
        + [pltpu.VMEM(field.shape, field.dtype) for field in (tokens, normed, w, out, qkv, mixed)]
        + [
            pltpu.VMEM((length, model), BF),
            pltpu.VMEM((length, wq), BF),
            pltpu.VMEM((length, wide), BF),
            pltpu.VMEM((length, HEAD_SIZE), F32),
            pltpu.VMEM((length, HEAD_SIZE), F32),
            held, held, held, held,
            dma((7,)), dma((3, PIECES)), dma((3, PIECES)), dma((4, PIECES)), dma((4, PIECES)),
        ],
        cost_estimate=pl.CostEstimate(flops=13 * 10**9, bytes_accessed=30 * 10**6, transcendentals=3 * 10**6),
        compiler_params=pltpu.CompilerParams(
            collective_id=2, has_side_effects=True, vmem_limit_bytes=62 * 2**20
        ),
        name="backward",
    )(
        second_grad, cotangent, gain_one[None], gain_two[None], logsum, cosine, sine,
        ids[None], ids[:, None], hidden, tokens, normed, w, out, qkv, mixed,
    )


TILE = 256


class ChipGather:
    def __init__(self, whole, columns, sems, seq, dpi, chips, own=None):
        self.whole, self.columns, self.sems, self.own = whole, columns, sems, own
        self.seq, self.dpi, self.chips = seq, dpi, chips
        self.chip, self.core = dpi // 2, dpi % 2

    def copy(self, kind, s, chip, core, to):
        block = self.whole.at[chip * 2 + core, :, self.columns]
        send, recv = self.sems
        src = block if s or self.own is None else self.own.at[:, self.columns]
        return remote(src, block, send.at[kind, s], recv.at[kind, s], (self.seq, to))

    def copies(self, s):
        z, c = self.chip, self.core
        low, high = z - s, z + s
        sibling = z * 2 + 1 - c
        out = [
            ((low >= 0) & (z < self.chips - 1), self.copy(0, s, low, c, self.dpi + 2)),
            ((high < self.chips) & (z > 0), self.copy(1, s, high, c, self.dpi - 2)),
            (low >= 0, self.copy(2, s, low, c, sibling)),
        ]
        if s > 0:
            out.append((high < self.chips, self.copy(3, s, high, c, sibling)))
        return out

    def send(self, s):
        for condition, copy in self.copies(s):
            pl.when(condition)(copy.start)

    def sent(self, s):
        for condition, copy in self.copies(s):
            pl.when(condition)(copy.wait_send)

    def came(self, s):
        z, c = self.chip, self.core
        pl.when(z - s >= 0)(self.copy(0, s - 1, z - s, c, self.dpi).wait_recv)
        pl.when(z + s < self.chips)(self.copy(1, s - 1, z + s, c, self.dpi).wait_recv)

    def came_across(self, s):
        z, c = self.chip, self.core
        pl.when(z - s >= 0)(self.copy(2, s, z - s, 1 - c, self.dpi).wait_recv)
        if s > 0:
            pl.when(z + s < self.chips)(self.copy(3, s, z + s, 1 - c, self.dpi).wait_recv)


class ChipScatter:
    def __init__(self, terms, got, held, sems, seq, dpi, chips):
        self.terms, self.got, self.held, self.sems = terms, got, held, sems
        self.seq, self.dpi, self.chips = seq, dpi, chips
        self.chip, self.core = dpi // 2, dpi % 2

    def give(self):
        send, recv = self.sems
        return remote(
            self.terms.at[:, 1 - self.core], self.got, send.at[2, 0], recv.at[2, 0], (self.seq, self.chip * 2 + 1 - self.core)
        )

    def up(self, d, to, field=None):
        send, recv = self.sems
        return remote((field or self.held).at[d], self.held.at[d], send.at[0, d], recv.at[0, d], (self.seq, to))

    def down(self, d, to, last, field=None):
        send, recv = self.sems
        slot = self.chips if last else d
        return remote((field or self.held).at[d], self.held.at[slot], send.at[1, d], recv.at[1, d], (self.seq, to))

    def each(self, body):
        size = self.got.shape[1]
        chunk = 16 if size % 16 == 0 else size

        @pl.loop(0, size // chunk)
        def _(i):
            body(pl.ds(pl.multiple_of(i * chunk, chunk), chunk))

    def take(self):
        self.give().wait()

        @pl.loop(0, self.chips)
        def _(d):
            def body(rows):
                own = self.terms[d, self.core, rows, :].astype(F32)
                self.got[d, rows, :] = (own + self.got[d, rows, :].astype(F32)).astype(BF)

            self.each(body)

    def add(self, d):
        def body(rows):
            total = self.got[d, rows, :].astype(F32) + self.held[d, rows, :].astype(F32)
            self.held[d, rows, :] = total.astype(BF)

        self.each(body)

    def step(self, r):
        z, chips = self.chip, self.chips

        @pl.when(z + r < chips)
        def _():
            d = z + r

            @pl.when(z > 0)
            def _():
                self.up(d, self.dpi).wait_recv()
                self.add(d)
                self.up(d, self.dpi + 2).start()

            @pl.when(z == 0)
            def _():
                self.up(d, self.dpi + 2, self.got).start()

        @pl.when(z - r >= 0)
        def _():
            d = z - r

            @pl.when(z < chips - 1)
            def _():
                self.down(d, self.dpi, False).wait_recv()
                self.add(d)
                self.down(d, self.dpi - 2, r == 1).start()

            @pl.when(z == chips - 1)
            def _():
                self.down(d, self.dpi - 2, r == 1, self.got).start()

    def finish(self, result):
        z, chips = self.chip, self.chips
        pl.when(z > 0)(lambda: self.up(z, self.dpi).wait_recv())
        pl.when(z < chips - 1)(lambda: self.down(z, self.dpi, True).wait_recv())

        def body(rows):
            total = self.got[z, rows, :].astype(F32)
            total += jnp.where(z > 0, self.held[z, rows, :].astype(F32), 0.0)
            result[rows, :] = total + jnp.where(z < chips - 1, self.held[chips, rows, :].astype(F32), 0.0)

        self.each(body)
        for r in range(1, chips):
            pl.when(z + r < chips)(lambda: self.up(z + r, self.dpi + 2).wait_send())
            pl.when(z - r >= 0)(lambda: self.down(z - r, self.dpi - 2, r == 1).wait_send())


def feed_kernel(
    second_ref, incoming_ref, first_hbm, own_ref,
    whole_out, out_hbm, grad_hbm, rest_hbm, mine_ref,
    second_turned_ref, incoming_turned_ref, w_ref, terms_ref, got_ref, held_ref, active_ref, both_ref, out_ref, grad_ref, stage_ref,
    load_sem, store_sem, stage_sem, own_sem, ahead_send, ahead_recv, sum_send, sum_recv,
    *, tiles, ready, summed,
):
    dps = lax.axis_size("dp")
    chips = dps // 2
    seq, dpi = lax.axis_index("seq"), lax.axis_index("dp")
    chip, core = dpi // 2, dpi % 2
    length, model = second_ref.shape
    width = 3 * TILE
    later = own_ref.shape[1] // width if ready < tiles else 0
    loose = ready >= chips + 2
    above, below = ((chip + 1) % chips) * 2 + core, ((chip + chips - 1) % chips) * 2 + core
    greet([(seq, above), (seq, below), (seq, chip * 2 + 1 - core)])

    def columns(t):
        return pl.ds(pl.multiple_of(t * width, width), width)

    def load(t, source=first_hbm):
        return pltpu.make_async_copy(source.at[:, :, columns(t)], w_ref.at[t % 2], load_sem.at[t % 2])

    def start_load(t):
        pl.when(t < ready)(lambda: load(t).start())
        if later > 0:
            first = columns(t - ready)
            ahead = pltpu.make_async_copy(whole_out.at[:, :, first], w_ref.at[t % 2], load_sem.at[t % 2])
            pl.when(within(t, ready, tiles))(ahead.start)

    def store(t):
        return pltpu.make_async_copy(
            terms_ref.at[t % 3], rest_hbm.at[:, :, :, columns(t - summed)], store_sem.at[t % 3]
        )

    def gather(q):
        return ChipGather(
            whole_out, columns(q), (ahead_send.at[q], ahead_recv.at[q]), seq, dpi, chips, own_ref
        )

    def scatter(t):
        return ChipScatter(
            terms_ref.at[t % 3], got_ref.at[t], held_ref.at[t], (sum_send.at[t], sum_recv.at[t]), seq, dpi, chips
        )

    def within(value, low, high):
        return (value >= low) & (value < high)

    load(0).start()
    own = pltpu.make_async_copy(own_ref, whole_out.at[dpi], own_sem)
    own.start()
    out_ref[...] = jnp.zeros_like(out_ref)
    grad_ref[...] = jnp.zeros_like(grad_ref)

    @pl.loop(0, length // TILE)
    def _(i):
        at = slot_rows(i, TILE)
        second_turned_ref[:, at] = second_ref[at, :].T
        incoming_turned_ref[:, at] = incoming_ref[at, :].T

    own.wait()
    far = list(range(chips - 1, 0, -1))
    thirds = [far[: -(-len(far) // 3)], far[-(-len(far) // 3) : -(-2 * len(far) // 3)], far[-(-2 * len(far) // 3) :]]

    @pl.loop(0, tiles)
    def _(t):
        def sent_at(tick):
            q = tick - tick // 3 if loose else tick
            return (tick >= 0) & (q < later) & ((tick % 3 != 2) if loose else True), q

        def pass_on(s):
            if later > 0:
                one, q = sent_at(t - s)

                @pl.when(one)
                def _():
                    gather(q).came(s)
                    gather(q).send(s)

        def sum_on(part):
            if part == 0:
                pl.when(within(t - 1, 0, summed))(lambda: scatter(t - 1).take())
            v = t - 1 - part
            j = v - v // 3

            @pl.when((v >= 0) & (v % 3 != 2) & (j < summed))
            def _():
                sums = scatter(j)
                if part == 3:
                    sums.finish(mine_ref.at[j])
                else:
                    for r in thirds[part]:
                        sums.step(r)

        if later > 0:
            one, q = sent_at(t)
            pl.when(one)(lambda: gather(q).send(0))
            arrived, q_last = sent_at(t - chips)

            @pl.when(arrived)
            def _():
                for s in range(chips):
                    gather(q_last).came_across(s)
                    gather(q_last).sent(s)

        start_load(t + 1)
        pltpu.make_async_copy(
            first_hbm.at[:, :, pl.ds(0, width)], w_ref.at[t % 2], load_sem.at[t % 2]
        ).wait()
        pl.when(t - 3 >= summed)(lambda: store(t - 3).wait())

        w = w_ref[t % 2].reshape(model, width)
        for i in range(2):
            at = slice(i * length // 2, (i + 1) * length // 2)
            both = nn(second_ref[at, :], w[:, : 2 * TILE])
            back = nn(incoming_ref[at, :], w[:, 2 * TILE :])
            gate, up = both[:, :TILE], both[:, TILE:]
            sigma = jax.nn.sigmoid(gate)
            silu = gate * sigma
            active_ref[at, :] = (silu * up).astype(BF)
            both_ref[at, :TILE] = (back * up * sigma * (1.0 + gate * (1.0 - sigma))).astype(BF)
            both_ref[at, TILE:] = (back * silu).astype(BF)
        pass_on(1)
        sum_on(0)
        rows = (chips, 2, model // dps)
        terms_ref[t % 3, :, :, :, : 2 * TILE] = nn(second_turned_ref[...], both_ref[...], BF).reshape(rows + (2 * TILE,))
        terms_ref[t % 3, :, :, :, 2 * TILE :] = nn(incoming_turned_ref[...], active_ref[...], BF).reshape(rows + (TILE,))
        pl.when(t < summed)(lambda: scatter(t).give().start())
        pl.when(t >= summed)(lambda: store(t).start())
        for s in range(2, chips - 1):
            pass_on(s)
        sum_on(1)
        for i in range(2):
            at = slice(i * length // 2, (i + 1) * length // 2)
            w = w_ref[t % 2].reshape(model, width)
            grad_ref[at, :] += nt(both_ref[at, :], w[:, : 2 * TILE])
            out_ref[at, :] += nt(active_ref[at, :], w[:, 2 * TILE :])
            if i == 0:
                sum_on(2)
        pass_on(chips - 1)
        sum_on(3)

    for j in range(summed):
        for part in range(4):
            if 1 + j + j // 2 + part >= tiles:
                if part == 3:
                    scatter(j).finish(mine_ref.at[j])
                else:
                    for r in thirds[part]:
                        scatter(j).step(r)
    for t in range(max(summed, tiles - 3), tiles):
        store(t).wait()
    quarter = length // 4
    stores = []
    for i in range(8):
        src, dst = (grad_ref, grad_hbm) if i < 4 else (out_ref, out_hbm)
        at = pl.ds((i % 4) * quarter, quarter)
        if i >= 2:
            stores[i - 2].wait()
        stage_ref[i % 2] = src[at, :].astype(BF)
        stores.append(pltpu.make_async_copy(stage_ref.at[i % 2], dst.at[at], stage_sem.at[i % 2]))
        stores[-1].start()
    for copy in stores[-2:]:
        copy.wait()


def feed_call(second, incoming, first, own, summed):
    dps, share, columns = first.shape
    chips = dps // 2
    length, model = second.shape
    width = 3 * TILE
    ready = columns // width
    tiles = ready + own.shape[1] // width
    if tiles == ready:
        own = jnp.zeros((share, 128), BF)
    vmem, hbm = pl.BlockSpec(memory_space=pltpu.VMEM), pl.BlockSpec(memory_space=pl.ANY)
    shape, dma = jax.ShapeDtypeStruct, pltpu.SemaphoreType.DMA
    return pl.pallas_call(
        functools.partial(feed_kernel, tiles=tiles, ready=ready, summed=summed),
        out_shape=(
            shape((dps,) + own.shape, BF),
            shape((length, model), BF),
            shape((length, model), BF),
            shape((chips, 2, share, (tiles - summed) * width), BF),
            shape((summed, share, width), F32),
        ),
        in_specs=[vmem, vmem, hbm, vmem],
        out_specs=(hbm, hbm, hbm, hbm, vmem),
        scratch_shapes=[
            pltpu.VMEM((model, length), BF),
            pltpu.VMEM((model, length), BF),
            pltpu.VMEM((2, dps, share, width), BF),
            pltpu.VMEM((3, chips, 2, share, width), BF),
            pltpu.VMEM((summed, chips, share, width), BF),
            pltpu.VMEM((summed, chips + 1, share, width), BF),
            pltpu.VMEM((length, TILE), BF),
            pltpu.VMEM((length, 2 * TILE), BF),
            pltpu.VMEM((length, model), F32),
            pltpu.VMEM((length, model), F32),
            pltpu.VMEM((2, length // 4, model), BF),
            dma((2,)), dma((3,)), dma((2,)), dma,
            dma((max(tiles - ready, 1), 4, chips)), dma((max(tiles - ready, 1), 4, chips)),
            dma((summed, 3, chips)), dma((summed, 3, chips)),
        ],
        cost_estimate=pl.CostEstimate(flops=65 * 10**9, bytes_accessed=60 * 10**6, transcendentals=3 * 10**6),
        compiler_params=pltpu.CompilerParams(
            collective_id=4, has_side_effects=True, vmem_limit_bytes=63 * 2**20
        ),
        name="feed_forward",
    )(second, incoming, first, own)


def pack_kernel(gate_ref, up_ref, down_ref, first_ref, rest_ref):
    units = gate_ref.shape[1]
    split = first_ref.shape[1] // (3 * TILE)
    for t in range(-(-units // TILE)):
        size = min(TILE, units - t * TILE)
        ref, at = (first_ref, t) if t < split else (rest_ref, t - split)
        lanes = slice(t * TILE, t * TILE + size)
        for i, part in enumerate((gate_ref[:, lanes], up_ref[:, lanes], down_ref[:, lanes])):
            low = (3 * at + i) * TILE
            ref[:, low : low + size] = part
            if size < TILE:
                ref[:, low + size : low + TILE] = jnp.zeros((part.shape[0], TILE - size), BF)


def pack_call(gate, up, down, ready):
    rows, units = gate.shape
    tiles = -(-units // TILE)
    vmem = pl.BlockSpec(memory_space=pltpu.VMEM)
    width = 3 * TILE
    return pl.pallas_call(
        pack_kernel,
        out_shape=[
            jax.ShapeDtypeStruct((rows, ready * width), BF),
            jax.ShapeDtypeStruct((rows, max(tiles - ready, 1) * width), BF),
        ],
        in_specs=[vmem] * 3,
        out_specs=[vmem] * 2,
        cost_estimate=pl.CostEstimate(flops=0, bytes_accessed=10**7, transcendentals=0),
        compiler_params=pltpu.CompilerParams(vmem_limit_bytes=32 * 2**20),
        name="pack_weights",
    )(gate, up, down)


def unpack_kernel(summed_ref, rest_ref, *refs):
    count = len(refs) // 2 - 1
    gate_ref, up_ref, down_ref = refs[count : count + 3]
    for src, dst in zip(refs[:count], refs[count + 3 :]):
        dst[...] = src[...]
    units = gate_ref.shape[1]
    split = summed_ref.shape[0]
    for t in range(-(-units // TILE)):
        size = min(TILE, units - t * TILE)
        lanes = slice(t * TILE, t * TILE + size)
        for i in range(3):
            if t < split:
                part = summed_ref[t, :, i * TILE : i * TILE + size]
            else:
                low = (3 * (t - split) + i) * TILE
                part = rest_ref[:, low : low + size].astype(F32)
            (gate_ref, up_ref, down_ref)[i][:, lanes] = part


def unpack_call(summed, rest, units, *given):
    rows = rest.shape[0]
    vmem = pl.BlockSpec(memory_space=pltpu.VMEM)
    return pl.pallas_call(
        unpack_kernel,
        out_shape=[jax.ShapeDtypeStruct((rows, units), F32)] * 3
        + [jax.ShapeDtypeStruct(field.shape, field.dtype) for field in given],
        in_specs=[vmem] * (2 + len(given)),
        out_specs=[vmem] * (3 + len(given)),
        cost_estimate=pl.CostEstimate(flops=0, bytes_accessed=10**7, transcendentals=0),
        compiler_params=pltpu.CompilerParams(vmem_limit_bytes=32 * 2**20),
        name="unpack_gradients",
    )(summed, rest, *given)


def end_kernel(
    normed_grad_ref, hidden_grad_ref, x_ref, gain_ref, qkv_ref, out_ref, small_ref, feed_ref, hidden_hbm,
    input_grad_ref, qkv_out_ref, out_out_ref, small_out_ref, layer_out_ref,
    qkv_got_ref, out_got_ref, small_got_ref,
    qkv_move_ref, out_move_ref, small_move_ref, qkv_came_ref, out_came_ref, small_came_ref,
    came_ref, sums_ref, one_ref, two_ref, came2_ref, sums2_ref, one2_ref, two2_ref, hidden_ref,
    sum_send, sum_recv, sum2_send, sum2_recv, load_sem, core_send, core_recv, ring_send, ring_recv, seq_send, seq_recv,
):
    seqs, dps = lax.axis_size("seq"), lax.axis_size("dp")
    chips = dps // 2
    seq, dpi = lax.axis_index("seq"), lax.axis_index("dp")
    chip, core = dpi // 2, dpi % 2
    ahead = ((chip + 1) % chips) * 2 + core
    behind = ((chip + chips - 1) % chips) * 2 + core
    sibling = chip * 2 + 1 - core
    greet([(seq ^ k, dpi) for k in range(1, seqs)] + [(seq, other) for other in (ahead, behind, sibling)])
    rows = x_ref.shape[0]
    piece = rows // PIECES

    cores = [
        remote(src.at[..., 1 - core, :, :], dst, core_send.at[i], core_recv.at[i], (seq, sibling))
        for i, (src, dst) in enumerate(
            ((qkv_ref, qkv_got_ref), (out_ref, out_got_ref), (small_ref, small_got_ref))
        )
    ]
    for copy in cores:
        copy.start()
    total = SeqSum(normed_grad_ref, rows, came_ref, sums_ref, one_ref, two_ref, (sum_send, sum_recv), dpi, seq)
    total.begin()
    feed = SeqSum(feed_ref, rows, came2_ref, sums2_ref, one2_ref, two2_ref, (sum2_send, sum2_recv), dpi, seq)
    load = pltpu.make_async_copy(hidden_hbm.at[slot_rows(seq, rows)], hidden_ref, load_sem)
    load.start()
    for copy in cores:
        copy.wait_recv()

    def term(which, step):
        parts = [
            qkv_ref[:, which, core].astype(F32) + qkv_got_ref[:, which].astype(F32),
            out_ref[which, core].astype(F32) + out_got_ref[which].astype(F32),
            small_ref[which, core].astype(F32) + small_got_ref[which].astype(F32),
        ]
        if step > 0:
            came = (qkv_came_ref, out_came_ref, small_came_ref)
            parts = [part + field[step - 1].astype(F32) for part, field in zip(parts, came)]
        return parts

    def ring(step):
        return [
            remote(src.at[step], dst.at[step], ring_send.at[i, step], ring_recv.at[i, step], (seq, ahead))
            for i, (src, dst) in enumerate(
                ((qkv_move_ref, qkv_came_ref), (out_move_ref, out_came_ref), (small_move_ref, small_came_ref))
            )
        ]

    def input_piece(c):
        at = pl.ds(c * piece, piece)
        x = x_ref[at, :].astype(F32)
        factor = lax.rsqrt(jnp.mean(x * x, axis=-1, keepdims=True) + EPS)
        unit = x * factor
        scaled = total.take(c) * gain_ref[...]
        grad = scaled - unit * jnp.mean(scaled * unit, axis=-1, keepdims=True)
        input_grad_ref[at, :] = (hidden_grad_ref[at, :] + factor * grad).astype(BF)

    for step in range(chips - 1):
        if step > 0:
            for copy in ring(step - 1):
                copy.wait_recv()
        for field, part in zip((qkv_move_ref, out_move_ref, small_move_ref), term((chip + chips - 1 - step) % chips, step)):
            field[step] = part.astype(BF)
        for copy in ring(step):
            copy.start()
        if step == 0:
            total.middle()
            feed.begin()
        if step == 1:
            for c in range(PIECES):
                input_piece(c)
            feed.middle()
    load.wait()
    for c in range(PIECES):
        at = pl.ds(c * piece, piece)
        layer_out_ref[at, :] = (hidden_ref[at, :] + feed.take(c)).astype(BF)
    for copy in ring(chips - 2):
        copy.wait_recv()
    qkv, out, small = term(chip, chips - 1)
    out_out_ref[...] = out
    qkv_move_ref[chips - 1] = qkv.astype(BF)
    small_move_ref[chips - 1] = small.astype(BF)
    last = [
        remote(
            src, dst.at[seq], seq_send.at[i, k], seq_recv.at[i, k], (seq ^ k, dpi)
        )
        for k in range(1, seqs)
        for i, (src, dst) in enumerate(
            ((qkv_move_ref.at[chips - 1, seq ^ k], qkv_out_ref), (small_move_ref.at[chips - 1], small_out_ref))
        )
    ]
    for copy in last:
        copy.start()
    qkv_out_ref[seq] = qkv_move_ref[chips - 1, seq]
    small_out_ref[seq] = small_move_ref[chips - 1]
    total.finish()
    feed.finish()
    for copy in cores + [copy for step in range(chips - 1) for copy in ring(step)]:
        copy.wait_send()
    for copy in last:
        copy.wait()


def end_call(normed_grad, hidden_grad, x, gain, qkv, out, small, feed, hidden):
    seqs, chips, _, share, wide = qkv.shape
    rows, model = x.shape
    vmem = pl.BlockSpec(memory_space=pltpu.VMEM)
    shape, dma = jax.ShapeDtypeStruct, pltpu.SemaphoreType.DMA
    held = pltpu.VMEM((PIECES, rows // PIECES, model), BF)
    blocks = ((seqs, share, wide), (share, model), small.shape[2:])
    return pl.pallas_call(
        end_kernel,
        out_shape=(
            shape((rows, model), BF),
            shape(blocks[0], BF),
            shape(blocks[1], F32),
            shape((seqs,) + blocks[2], BF),
            shape((rows, model), BF),
        ),
        in_specs=[vmem] * 8 + [pl.BlockSpec(memory_space=pl.ANY)],
        out_specs=(vmem,) * 5,
        scratch_shapes=[
            pltpu.VMEM((seqs, chips, share, wide), BF),
            pltpu.VMEM((chips, share, model), BF),
            pltpu.VMEM((chips,) + blocks[2], BF),
        ]
        + [pltpu.VMEM((chips,) + block, BF) for block in blocks]
        + [pltpu.VMEM((chips - 1,) + block, BF) for block in blocks]
        + [
            held, held, held, held, held, held, held, held, pltpu.VMEM((rows, model), F32),
            dma((3, PIECES)), dma((3, PIECES)), dma((3, PIECES)), dma((3, PIECES)), dma, dma((3,)), dma((3,)),
            dma((3, chips)), dma((3, chips)), dma((2, seqs)), dma((2, seqs)),
        ],
        cost_estimate=pl.CostEstimate(flops=10**8, bytes_accessed=2 * 10**7, transcendentals=0),
        compiler_params=pltpu.CompilerParams(
            collective_id=3, has_side_effects=True, vmem_limit_bytes=48 * 2**20
        ),
        name="end_sums",
    )(normed_grad, hidden_grad, x, gain[None], qkv, out, small, feed, hidden)


def pair_tiles(left, right):
    units = left.shape[1]
    cuts = list(range(0, units, TILE)) + [units]
    return jnp.concatenate(
        [field[:, low:high] for low, high in zip(cuts[:-1], cuts[1:]) for field in (left, right)], axis=1
    )


def split_tiles(both):
    units = both.shape[1] // 2
    cuts = list(range(0, units, TILE)) + [units]
    spans = list(zip(cuts[:-1], cuts[1:]))
    return (
        jnp.concatenate([both[:, 2 * low : low + high] for low, high in spans], axis=1),
        jnp.concatenate([both[:, low + high : 2 * high] for low, high in spans], axis=1),
    )


def shards(
    inputs,
    block_ids,
    cotangent,
    first_gain,
    query_weight,
    query_bias,
    key_weight,
    key_bias,
    value_weight,
    value_bias,
    output_weight,
    second_gain,
    gate_weight,
    up_weight,
    down_weight,
):
    seqs = lax.axis_size("seq")
    seq = lax.axis_index("seq")
    dps = lax.axis_size("dp")
    dpi = lax.axis_index("dp")
    chips, chip, core = dps // 2, dpi // 2, dpi % 2
    heads = H // seqs
    copies = seqs // KEY_VALUE_HEADS
    wq = heads * HEAD_SIZE
    wide = wq + 2 * HEAD_SIZE
    tokens_here, model = inputs.shape[1:]
    share = first_gain.shape[0]
    kv_share = key_bias.shape[0]
    hidden_units = gate_weight.shape[1]

    small = jnp.concatenate([first_gain, second_gain, query_bias, key_bias, value_bias])
    packed = jnp.concatenate(
        [
            query_weight.reshape(share, seqs, wq),
            jnp.repeat(key_weight.reshape(share, KEY_VALUE_HEADS, HEAD_SIZE), copies, axis=1),
            jnp.repeat(value_weight.reshape(share, KEY_VALUE_HEADS, HEAD_SIZE), copies, axis=1),
        ],
        axis=-1,
    ).transpose(1, 0, 2)
    one = small.shape[0]
    small = jnp.pad(small[None], ((0, 15), (0, -one % 128)))
    tiles = -(-hidden_units // TILE)
    ready = READY if chips <= 4 else tiles
    first, later = pack_call(gate_weight, up_weight, down_weight.T, ready)
    later = later if ready < tiles else later[:, :0]
    first = lax.all_gather(first, "dp", axis=0, tiled=True).reshape(dps, model // dps, -1)
    tokens, incoming, blocks, smalls, weight_qkv, weight_out = start_call(
        inputs[0], cotangent[0], block_ids.reshape(-1, 128), small, packed, output_weight
    )
    blocks = blocks.reshape(-1)
    weight_qkv = weight_qkv.reshape(model, wide)
    smalls = smalls[:, :, 0, :one].transpose(1, 0, 2).astype(F32)
    gain_first = smalls[:, :, :share].reshape(model)
    gain_second = smalls[:, :, share : 2 * share].reshape(model)
    bias_q = lax.dynamic_index_in_dim(smalls, seq, 0, keepdims=False)[:, 2 * share : 3 * share].reshape(wq)
    group = seq // copies
    bias_k = smalls[:, :, 3 * share : 3 * share + kv_share].reshape(KEY_VALUE_HEADS, HEAD_SIZE)
    bias_v = smalls[:, :, 3 * share + kv_share :].reshape(KEY_VALUE_HEADS, HEAD_SIZE)
    bias = jnp.concatenate(
        [
            bias_q,
            lax.dynamic_index_in_dim(bias_k, group, 0, keepdims=False),
            lax.dynamic_index_in_dim(bias_v, group, 0, keepdims=False),
        ]
    )
    length = tokens.shape[0]
    cosine, sine = rope_tables(length)

    normed, qkv, mixed, logsum, hidden, second = attend_call(
        tokens, weight_qkv, bias[None], cosine, sine, blocks, gain_first, gain_second, weight_out.reshape(model, model)
    )
    second, weight_out = lax.optimization_barrier((second, weight_out))
    out_head = weight_out[0].reshape(dps * share, model)
    _, out_sum, second_sum, rest, summed = feed_call(second, incoming, first, later, SUMMED)
    rest = rest.reshape(model, -1)
    rest = lax.psum_scatter(rest, "dp", scatter_dimension=0, tiled=True)
    normed_grad, grad_hidden, qkv_grad, out_weight_grad, bias_grad, gain_one_grad, gain_two_grad = backward_call(
        second_sum, cotangent[0], gain_first, gain_second, logsum, cosine, sine, blocks,
        hidden, tokens, normed, weight_qkv, out_head, qkv, mixed,
    )
    bias_grad, gain_one_grad, gain_two_grad = bias_grad[0], gain_one_grad[0], gain_two_grad[0]

    place = lambda field, count, at: jnp.where(
        (jnp.arange(count) == at)[:, None], field[None], 0.0
    ).reshape(seqs, dps, -1)
    small_grad = jnp.concatenate(
        [
            gain_one_grad.reshape(seqs, dps, share),
            gain_two_grad.reshape(seqs, dps, share),
            place(bias_grad[:wq], seqs, seq),
            place(bias_grad[wq : wq + HEAD_SIZE], KEY_VALUE_HEADS, group),
            place(bias_grad[wq + HEAD_SIZE :], KEY_VALUE_HEADS, group),
        ],
        axis=-1,
    )
    small_rows = -(-seqs * one // wide)
    small_grad = small_grad.transpose(1, 0, 2).reshape(dps, seqs * one).astype(BF)
    small_grad = jnp.pad(small_grad, ((0, 0), (0, small_rows * wide - seqs * one)))
    small_grad = jnp.pad(small_grad.reshape(dps, -1, wide), ((0, 0), (0, 16 - small_rows), (0, 0)))
    input_grad, parts, out_weight_grad, smalls, layer_out = end_call(
        normed_grad, grad_hidden, inputs[0], gain_first,
        qkv_grad.reshape(seqs, chips, 2, share, wide),
        out_weight_grad.reshape(chips, 2, share, model),
        small_grad.reshape(chips, 2, 16, wide),
        out_sum, hidden,
    )
    smalls = smalls[:, :small_rows].reshape(seqs, -1)[:, : seqs * one].reshape(seqs, seqs, one)
    small_sum = jnp.sum(
        lax.dynamic_index_in_dim(smalls, seq, 1, keepdims=False).astype(F32), axis=0
    )
    query_weight_grad = jnp.concatenate([part[:share, :wq] for part in parts], axis=1).astype(F32)
    pairs = [
        sum(part[:share, wq:].astype(F32) for part in parts[g * copies : (g + 1) * copies])
        for g in range(KEY_VALUE_HEADS)
    ]
    key_weight_grad = jnp.concatenate([pair[:, :HEAD_SIZE] for pair in pairs], axis=1)
    value_weight_grad = jnp.concatenate([pair[:, HEAD_SIZE:] for pair in pairs], axis=1)
    gain_one_grad, gain_two_grad, query_bias_grad, key_bias_grad, value_bias_grad = jnp.split(
        small_sum, [share, 2 * share, 3 * share, 3 * share + kv_share]
    )

    gate_grad, up_grad, down_grad, layer_out, input_grad, out_weight_grad = unpack_call(
        summed, rest, hidden_units, layer_out, input_grad, out_weight_grad
    )
    return (
        layer_out[None],
        input_grad[None],
        gain_one_grad,
        query_weight_grad,
        query_bias_grad,
        key_weight_grad,
        key_bias_grad,
        value_weight_grad,
        value_bias_grad,
        out_weight_grad,
        gain_two_grad,
        gate_grad,
        up_grad,
        down_grad.T,
    )


def solution(mesh):
    tokens = P("dp", "seq", None)
    whole = P(("seq", "dp"))
    matrix = P(("seq", "dp"), None)
    feed = P("dp", "seq")
    in_specs = (
        tokens,
        P("dp", "seq"),
        tokens,
        whole,
        matrix,
        whole,
        matrix,
        whole,
        matrix,
        whole,
        matrix,
        whole,
        feed,
        feed,
        P("seq", "dp"),
    )
    out_specs = (
        tokens,
        tokens,
        whole,
        matrix,
        whole,
        matrix,
        whole,
        matrix,
        whole,
        matrix,
        whole,
        feed,
        feed,
        P("seq", "dp"),
    )
    return jax.shard_map(shards, mesh=mesh, in_specs=in_specs, out_specs=out_specs, check_vma=False)
```

```python
import functools

import jax
import jax.numpy as jnp
import numpy as np
from jax import lax
from jax.experimental import pallas as pl
from jax.experimental.pallas import tpu as pltpu
from jax.sharding import PartitionSpec as P

H = 12
KEY_VALUE_HEADS = 2
HEAD_SIZE = 128
EPS = 1e-06
THETA = 1000000.0
SCALE = HEAD_SIZE ** (-0.5)
BF = jnp.bfloat16
F32 = jnp.float32


def dot(a, b, dims, out=F32):
    return lax.dot_general(a, b, (dims, ((), ())), preferred_element_type=F32).astype(out)


def nn(a, b, out=F32):
    return dot(a, b, ((1,), (0,)), out)


def nt(a, b, out=F32):
    return dot(a, b, ((1,), (1,)), out)


def tn(a, b, out=F32):
    return dot(a, b, ((0,), (0,)), out)


def rope_tables(length):
    exponent = np.arange(0, HEAD_SIZE, 2).astype(np.float32) / np.float32(HEAD_SIZE)
    freqs = np.float32(THETA) ** (-exponent)
    angles = np.arange(length).astype(np.float32)[:, None] * freqs[None, :]
    cosine, sine = np.cos(angles), np.sin(angles)
    return (
        jnp.asarray(np.concatenate([cosine, cosine], axis=-1), F32),
        jnp.asarray(np.concatenate([-sine, sine], axis=-1), F32),
    )


def remote(src, dst, send, recv, where):
    return pltpu.make_async_remote_copy(
        src_ref=src, dst_ref=dst, send_sem=send, recv_sem=recv,
        device_id=where, device_id_type=pl.DeviceIdType.MESH,
    )


def greet(partners):
    barrier = pltpu.get_barrier_semaphore()
    for partner in partners:
        pl.semaphore_signal(barrier, inc=1, device_id=partner, device_id_type=pl.DeviceIdType.MESH)
    pl.semaphore_wait(barrier, len(partners))


def far_sends(field, half, seq, dpi, send, recv):
    def rows(k, low):
        return field.at[pl.ds(pl.multiple_of((seq ^ k) * 2 * half + low, half), half)]

    return [
        remote(rows(2, 0), rows(2, 0), send.at[0], recv.at[0], (seq ^ 1, dpi)),
        remote(rows(1, half), rows(1, half), send.at[1], recv.at[1], (seq ^ 2, dpi)),
    ]


def start_kernel(
    x_in, c_in, ids_in, small_in, pack_in, out_in,
    x_out, c_out, ids_out, small_out, pack_out, out_out,
    local_sem, seq_send, seq_recv, far_send, far_recv, ring_send, ring_recv, core_send, core_recv,
    out_send, out_recv, slot_send, slot_recv,
):
    seqs, dps = lax.axis_size("seq"), lax.axis_size("dp")
    chips = dps // 2
    seq, dpi = lax.axis_index("seq"), lax.axis_index("dp")
    chip, core = dpi // 2, dpi % 2
    sibling = chip * 2 + 1 - core
    others = [((chip + h) % chips) * 2 + core for h in range(1, chips)]
    greet([(seq ^ k, dpi) for k in range(1, seqs)] + [(seq, other) for other in others + [sibling]])

    rows = x_in.shape[0]
    half = rows // 2

    def to_slots(i, src, dst, slots):
        return [remote(src, dst, seq_send.at[i, k], seq_recv.at[i, k], (seq ^ k, dpi)) for k in slots]

    def block(index, low=0, count=rows):
        return pl.ds(pl.multiple_of(index * rows + low, half), count)

    small_sends = to_slots(0, small_in, small_out.at[dpi, seq], range(1, seqs))
    pack_sends = [
        remote(
            pack_in.at[seq ^ k], pack_out.at[seq, dpi], seq_send.at[1, k], seq_recv.at[1, k], (seq ^ k, dpi)
        )
        for k in range(1, seqs)
    ]
    id_sends = to_slots(2, ids_in, ids_out.at[seq], range(1, seqs))
    x_sends = to_slots(3, x_in, x_out.at[block(seq)], (1, 2))
    c_sends = to_slots(4, c_in, c_out.at[block(seq)], (1, 2))
    locals_ = [
        pltpu.make_async_copy(small_in, small_out.at[dpi, seq], local_sem.at[0]),
        pltpu.make_async_copy(pack_in.at[seq], pack_out.at[seq, dpi], local_sem.at[1]),
        pltpu.make_async_copy(out_in, out_out.at[0, dpi], local_sem.at[2]),
        pltpu.make_async_copy(ids_in, ids_out.at[seq], local_sem.at[3]),
        pltpu.make_async_copy(x_in, x_out.at[block(seq)], local_sem.at[4]),
        pltpu.make_async_copy(c_in, c_out.at[block(seq)], local_sem.at[5]),
    ]
    def fields(at, which):
        every = (out_out.at[0, at], small_out.at[at], pack_out.at[:, at])
        return [(i, every[i]) for i in which]

    def hop_sends(hop, which):
        to = ((chip + chips - hop) % chips) * 2 + core
        return [
            remote(out_in if i == 0 else field, field, ring_send.at[i, hop], ring_recv.at[i, hop], (seq, to))
            for i, field in fields(dpi, which)
        ]

    def core_sends(hop, which=(0, 1, 2)):
        at = ((chip + hop) % chips) * 2 + core
        return [
            remote(field, field, core_send.at[i, hop], core_recv.at[i, hop], (seq, sibling))
            for i, field in fields(at, which)
        ]

    def out_sends(hop):
        at = ((chip + hop) % chips) * 2 + core
        src = out_out.at[0, at] if hop else out_in
        return [
            remote(src, out_out.at[k, at], out_send.at[k, hop], out_recv.at[k, hop], (seq ^ k, dpi))
            for k in range(1, seqs)
        ]

    line = chips == 4
    order = [2, 1, 3] if line else sorted(range(1, chips), key=lambda hop: min(hop, chips - hop))
    ends = ((1, chip != 0), (3, chip != chips - 1))

    def hops_do(which, what):
        for hop in order:
            for copy in hop_sends(hop, which):
                if line and hop != 2:
                    pl.when(dict(ends)[hop])(getattr(copy, what))
                else:
                    getattr(copy, what)()

    def relays(which):
        low = chip == 2
        end, far = jnp.where(low, 3, 0), jnp.where(low, 0, 3)
        return [
            remote(field, field, ring_send.at[i, 0], ring_recv.at[i, jnp.where(low, 1, 3)], (seq, end * 2 + core))
            for i, field in fields(far * 2 + core, which)
        ]

    def relay(which, what):
        if line:
            for copy in relays(which):
                pl.when((chip == 1) | (chip == 2))(getattr(copy, what))

    flying, outs = [], []
    hops_do((0,), "start")
    first = small_sends + pack_sends + locals_[:3] + x_sends + id_sends + locals_[3:]
    for copy in first:
        copy.start()
    for copy in locals_[:3] + small_sends + pack_sends:
        copy.wait()
    hops_do((1, 2), "start")
    for hop in [0] + order:
        if hop > 0:
            for copy in hop_sends(hop, (0,)):
                copy.wait_recv()
            if hop == 2:
                relay((0,), "start")
        cores, more = core_sends(hop, (0,)), out_sends(hop)
        for copy in cores + more:
            copy.start()
        flying += cores
        outs += more
    for copy in x_sends:
        copy.wait()
    far_x = far_sends(x_out, half, seq, dpi, far_send.at[0], far_recv.at[0])
    for copy in far_x + c_sends:
        copy.start()
    for hop in [0] + order:
        if hop > 0:
            for copy in hop_sends(hop, (1, 2)):
                copy.wait_recv()
            if hop == 2:
                relay((1, 2), "start")
        cores = core_sends(hop, (1, 2))
        for copy in cores:
            copy.start()
        flying += cores
    for copy in c_sends:
        copy.wait()
    far_c = far_sends(c_out, half, seq, dpi, far_send.at[1], far_recv.at[1])
    for copy in far_c:
        copy.start()
    for copy in outs:
        copy.wait_recv()
    slots = [
        remote(
            out_out.at[k, ((chip + hop) % chips) * 2 + core], out_out.at[k, ((chip + hop) % chips) * 2 + core],
            slot_send.at[k, hop], slot_recv.at[k, hop], (seq, sibling),
        )
        for k in range(1, seqs)
        for hop in range(chips)
    ]
    for copy in slots:
        copy.start()
    hops_do((0, 1, 2), "wait_send")
    relay((0, 1, 2), "wait_send")
    for copy in flying + outs:
        copy.wait_send()
    for hop in range(chips):
        for copy in core_sends(hop):
            copy.wait_recv()
    for copy in slots + far_x + far_c + id_sends + locals_[3:]:
        copy.wait()


def start_call(x, c, ids, small, pack, out):
    seqs, dps = lax.axis_size("seq"), lax.axis_size("dp")
    chips = dps // 2
    share, wide = pack.shape[1:]
    any_space = pl.BlockSpec(memory_space=pl.ANY)
    shapes = (
        jax.ShapeDtypeStruct((seqs * x.shape[0], x.shape[1]), x.dtype),
        jax.ShapeDtypeStruct((seqs * c.shape[0], c.shape[1]), c.dtype),
        jax.ShapeDtypeStruct((seqs,) + ids.shape, ids.dtype),
        jax.ShapeDtypeStruct((dps, seqs) + small.shape, small.dtype),
        jax.ShapeDtypeStruct((seqs, dps, share, wide), pack.dtype),
        jax.ShapeDtypeStruct((seqs, dps) + out.shape, out.dtype),
    )
    dma = pltpu.SemaphoreType.DMA
    return pl.pallas_call(
        start_kernel,
        out_shape=shapes,
        in_specs=[pl.BlockSpec(memory_space=pltpu.VMEM)] * 6,
        out_specs=(any_space,) * 6,
        scratch_shapes=[
            dma((6,)), dma((5, seqs)), dma((5, seqs)), dma((2, 2)), dma((2, 2)),
            dma((3, chips)), dma((3, chips)), dma((3, chips)), dma((3, chips)),
            dma((seqs, chips)), dma((seqs, chips)), dma((seqs, chips)), dma((seqs, chips)),
        ],
        compiler_params=pltpu.CompilerParams(collective_id=0, has_side_effects=True),
        name="start_gather",
    )(x, c, ids, small, pack, out)


def attend_kernel(
    x_ref, w_ref, bias_ref, cos_ref, sin_ref, ids_row_ref, ids_col_ref, gain_one_ref, gain_two_ref, out_ref,
    normed_ref, qkv_ref, mixed_ref, lse_ref, hidden_ref, second_ref,
    all_ref, send_sem, recv_sem,
):
    seqs = lax.axis_size("seq")
    seq, dpi = lax.axis_index("seq"), lax.axis_index("dp")
    greet([(seq ^ k, dpi) for k in range(1, seqs)])
    length, model = x_ref.shape
    wq = mixed_ref.shape[1]
    heads = wq // HEAD_SIZE
    rows = length // seqs
    @pl.loop(0, seqs)
    def _(i):
        at = pl.ds(pl.multiple_of(i * rows, rows), rows)
        x = x_ref[at, :].astype(F32)
        factor = lax.rsqrt(jnp.mean(x * x, axis=-1, keepdims=True) + EPS)
        normed_ref[at, :] = (x * factor * gain_one_ref[...]).astype(BF)

    @pl.loop(0, 2)
    def _(i):
        at = pl.ds(pl.multiple_of(i * 2 * rows, 2 * rows), 2 * rows)
        pre = jnp.dot(normed_ref[at, :], w_ref[...], preferred_element_type=F32) + bias_ref[...]
        cosine, sine = cos_ref[at, :], sin_ref[at, :]
        for h in range(heads + 1):
            u = pre[:, h * HEAD_SIZE : (h + 1) * HEAD_SIZE]
            turned = pltpu.roll(u, HEAD_SIZE // 2, 1)
            qkv_ref[at, h * HEAD_SIZE : (h + 1) * HEAD_SIZE] = (u * cosine + turned * sine).astype(BF)
        qkv_ref[at, wq + HEAD_SIZE :] = pre[:, wq + HEAD_SIZE :].astype(BF)

    copies = []
    for t in range(seqs):
        at = slice(t * rows, (t + 1) * rows)
        reach = min(t + 2, seqs) * rows
        keys = qkv_ref[:reach, wq : wq + HEAD_SIZE]
        values = qkv_ref[:reach, wq + HEAD_SIZE :]
        allowed = ids_row_ref[:, :reach] <= ids_col_ref[at, :]
        sums = []
        for h in range(heads):
            lanes = slice(h * HEAD_SIZE, (h + 1) * HEAD_SIZE)
            scores = nt(qkv_ref[at, lanes], keys) * SCALE
            scores = jnp.where(allowed, scores, -1000000000.0)
            peak = jnp.max(scores, axis=-1, keepdims=True)
            raised = jnp.exp(scores - peak)
            total = jnp.sum(raised, axis=-1, keepdims=True)
            low = (raised * (1.0 / total)).astype(BF)
            mixed_ref[at, lanes] = nn(low, values).astype(BF)
            sums.append(peak + jnp.log(total))
        lse_ref[at, :heads] = jnp.concatenate(sums, axis=1)
        more = [
            remote(
                mixed_ref.at[pl.ds(t * rows, rows)], all_ref.at[pl.ds(t * rows, rows), pl.ds(k * wq, wq)],
                send_sem.at[k, t], recv_sem.at[k, t], (seq ^ k, dpi),
            )
            for k in range(1, seqs)
        ]
        for copy in more:
            copy.start()
        copies.append(more)
        all_ref[at, :wq] = mixed_ref[at, :]

    for t in range(seqs):
        at = slice(t * rows, (t + 1) * rows)
        for copy in copies[t]:
            copy.wait_recv()
        hidden = x_ref[at, :].astype(F32) + nn(all_ref[at, :], out_ref[...])
        hidden_ref[at, :] = hidden
        factor = lax.rsqrt(jnp.mean(hidden * hidden, axis=-1, keepdims=True) + EPS)
        second_ref[at, :] = (hidden * factor * gain_two_ref[...]).astype(BF)
    for t in range(seqs):
        for copy in copies[t]:
            copy.wait_send()


def attend_call(x, w, bias, cosine, sine, ids, gain_one, gain_two, out):
    seqs = lax.axis_size("seq")
    length, model = x.shape
    wide = w.shape[1]
    wq = wide - 2 * HEAD_SIZE
    vmem = pl.BlockSpec(memory_space=pltpu.VMEM)
    shape = jax.ShapeDtypeStruct
    return pl.pallas_call(
        attend_kernel,
        out_shape=(
            shape((length, model), BF),
            shape((length, wide), BF),
            shape((length, wq), BF),
            shape((length, 128), F32),
            shape((length, model), F32),
            shape((length, model), BF),
        ),
        in_specs=[vmem] * 10,
        out_specs=(vmem,) * 6,
        scratch_shapes=[
            pltpu.VMEM((length, seqs * wq), BF),
            pltpu.SemaphoreType.DMA((seqs, seqs)),
            pltpu.SemaphoreType.DMA((seqs, seqs)),
        ],
        cost_estimate=pl.CostEstimate(flops=9 * 10**9, bytes_accessed=30 * 10**6, transcendentals=3 * 10**6),
        compiler_params=pltpu.CompilerParams(
            collective_id=1, has_side_effects=True, vmem_limit_bytes=60 * 2**20
        ),
        name="attend",
    )(x, w, bias, cosine, sine, ids[None], ids[:, None], gain_one[None], gain_two[None], out)


PIECES = 4
READY = 6
SUMMED = 4


def slot_rows(index, rows):
    return pl.ds(pl.multiple_of(index * rows, rows), rows)


class SeqSum:
    def __init__(self, field, rows, came, sums, from_one, from_two, sems, dpi, seq):
        self.field, self.rows, self.piece = field, rows, rows // PIECES
        self.came, self.sums, self.got = came, sums, {1: from_one, 2: from_two}
        self.send, self.recv = sems
        self.dpi, self.seq = dpi, seq
        self.started = []

    def at(self, k, c):
        start = (self.seq ^ k) * self.rows + c * self.piece
        return pl.ds(pl.multiple_of(start, self.piece), self.piece)

    def pass_on(self, c):
        by = 1 + c % 2
        return remote(
            self.field.at[self.at(3, c)], self.came.at[c], self.send.at[0, c], self.recv.at[0, c], (self.seq ^ by, self.dpi)
        )

    def direct(self, k, c):
        late = (k == 2) == (c % 2 == 0)
        src = self.sums.at[c] if late else self.field.at[self.at(k, c)]
        return remote(src, self.got[k].at[c], self.send.at[k, c], self.recv.at[k, c], (self.seq ^ k, self.dpi))

    def begin(self):
        for c in range(PIECES):
            self.pass_on(c).start()
            self.direct(1 + c % 2, c).start()

    def middle(self):
        for c in range(PIECES):
            k = 2 - c % 2
            self.pass_on(c).wait_recv()
            own = self.field[self.at(k, c), :].astype(F32)
            self.sums[c] = (self.came[c].astype(F32) + own).astype(BF)
            self.direct(k, c).start()

    def take(self, c):
        for k in (1, 2):
            self.direct(k, c).wait_recv()
        total = self.field[self.at(0, c), :].astype(F32) + self.got[1][c].astype(F32)
        return total + self.got[2][c].astype(F32)

    def finish(self):
        for c in range(PIECES):
            self.pass_on(c).wait_send()
            for k in (1, 2):
                self.direct(k, c).wait_send()


def backward_kernel(
    second_grad_ref, cotangent_ref, gain_one_ref, gain_two_ref, lse_ref, cos_ref, sin_ref,
    ids_row_ref, ids_col_ref, hidden_hbm, tokens_hbm, normed_hbm, w_hbm, out_hbm, qkv_hbm, mixed_hbm,
    normed_grad_ref, hidden_grad_ref, w_grad_ref, out_grad_ref, bias_grad_ref, gain_grad_ref, gain_two_grad_ref,
    hidden_ref, tokens_ref, normed_ref, w_ref, out_ref, qkv_ref, mixed_ref,
    branch_ref, mixed_grad_ref, pre_grad_ref, key_grad_ref, value_grad_ref,
    came_ref, sums_ref, one_ref, two_ref,
    load_sem, sum_send, sum_recv, branch_send, branch_recv,
):
    seqs = lax.axis_size("seq")
    seq, dpi = lax.axis_index("seq"), lax.axis_index("dp")
    length, model = second_grad_ref.shape
    rows = length // seqs
    piece = rows // PIECES
    wq = mixed_ref.shape[1]
    heads = wq // HEAD_SIZE
    loads = [
        pltpu.make_async_copy(src, dst, load_sem.at[i])
        for i, (src, dst) in enumerate(
            (
                (hidden_hbm.at[slot_rows(seq, rows)], hidden_ref),
                (out_hbm, out_ref), (qkv_hbm, qkv_ref), (w_hbm, w_ref),
                (tokens_hbm, tokens_ref), (normed_hbm, normed_ref), (mixed_hbm, mixed_ref),
            )
        )
    ]
    for load in loads:
        load.start()
    greet([(seq ^ k, dpi) for k in range(1, seqs)])

    total = SeqSum(second_grad_ref, rows, came_ref, sums_ref, one_ref, two_ref, (sum_send, sum_recv), dpi, seq)
    total.begin()
    loads[0].wait()
    total.middle()

    def branch_at(k, c):
        start = (seq ^ k) * rows + c * piece
        return branch_ref.at[pl.ds(pl.multiple_of(start, piece), piece)]

    def branch_copy(k, c):
        if k < 3:
            return remote(
                branch_at(0, c), branch_at(0, c), branch_send.at[k, c], branch_recv.at[k, c], (seq ^ k, dpi)
            )
        came, to = (2, 1) if c % 2 == 0 else (1, 2)
        return remote(
            branch_at(came, c), branch_at(came, c), branch_send.at[3, c], branch_recv.at[3, c], (seq ^ to, dpi)
        )

    gain_two_grad_ref[...] = jnp.zeros_like(gain_two_grad_ref)
    for c in range(PIECES):
        at = pl.ds(c * piece, piece)
        grad = total.take(c)
        hidden = hidden_ref[at, :]
        factor = lax.rsqrt(jnp.mean(hidden * hidden, axis=-1, keepdims=True) + EPS)
        unit = hidden * factor
        gain_two_grad_ref[...] += jnp.sum(grad * unit, axis=0, keepdims=True)
        scaled = grad * gain_two_ref[...]
        grad = cotangent_ref[at, :].astype(F32) + factor * (
            scaled - unit * jnp.mean(scaled * unit, axis=-1, keepdims=True)
        )
        hidden_grad_ref[at, :] = grad
        start = pl.multiple_of(seq * rows + c * piece, piece)
        branch_ref[pl.ds(start, piece), :] = grad.astype(BF)
        for k in (1, 2):
            branch_copy(k, c).start()
    total.finish()
    for load in loads[1:3]:
        load.wait()

    key_grad_ref[...] = jnp.zeros_like(key_grad_ref)
    value_grad_ref[...] = jnp.zeros_like(value_grad_ref)

    def rot_back(w, at):
        return w * cos_ref[at, :] + pltpu.roll(w * sin_ref[at, :], HEAD_SIZE // 2, 1)

    def attend_back(k):
        at = slot_rows(seq ^ k, rows)
        mixed_grad_ref[at, :] = nt(branch_ref[at, :], out_ref[...]).astype(BF)
        allowed = ids_row_ref[...] <= ids_col_ref[at, :]
        keys = qkv_ref[:, wq : wq + HEAD_SIZE]
        values = qkv_ref[:, wq + HEAD_SIZE :]
        for h in range(heads):
            lanes = slice(h * HEAD_SIZE, (h + 1) * HEAD_SIZE)
            queries = qkv_ref[at, lanes]
            grad = mixed_grad_ref[at, lanes]
            scores = jnp.where(allowed, nt(queries, keys) * SCALE, -1000000000.0)
            probs = jnp.exp(scores - lse_ref[at, h : h + 1])
            prob_grad = nt(grad, values)
            delta = jnp.sum(probs * prob_grad, axis=-1, keepdims=True)
            score_grad = (probs * (prob_grad - delta)).astype(BF)
            pre_grad_ref[at, lanes] = rot_back(nn(score_grad, keys) * SCALE, at).astype(BF)
            key_grad_ref[...] += tn(score_grad, queries)
            value_grad_ref[...] += tn(probs.astype(BF), grad)

    attend_back(0)
    for k in (1, 2):
        for c in range(PIECES):
            branch_copy(k, c).wait_recv()
            if (k == 2) == (c % 2 == 0):
                branch_copy(3, c).start()
        attend_back(k)
    for c in range(PIECES):
        branch_copy(3, c).wait_recv()
    attend_back(3)
    for c in range(PIECES):
        for k in (1, 2, 3):
            branch_copy(k, c).wait_send()

    every = pl.ds(0, length)
    pre_grad_ref[:, wq : wq + HEAD_SIZE] = rot_back(key_grad_ref[...] * SCALE, every).astype(BF)
    pre_grad_ref[:, wq + HEAD_SIZE :] = value_grad_ref[...].astype(BF)
    bias_grad_ref[...] = jnp.sum(pre_grad_ref[...].astype(F32), axis=0, keepdims=True)
    for load in loads[3:]:
        load.wait()
    gain_grad_ref[...] = jnp.zeros_like(gain_grad_ref)

    @pl.loop(0, seqs)
    def _(i):
        at = slot_rows(i, rows)
        grad = nt(pre_grad_ref[at, :], w_ref[...])
        x = tokens_ref[at, :].astype(F32)
        factor = lax.rsqrt(jnp.mean(x * x, axis=-1, keepdims=True) + EPS)
        gain_grad_ref[...] += jnp.sum(grad * (x * factor), axis=0, keepdims=True)
        normed_grad_ref[at, :] = grad.astype(BF)

    @pl.loop(0, model // wq)
    def _(i):
        lanes = pl.ds(pl.multiple_of(i * wq, HEAD_SIZE), wq)
        w_grad_ref[pl.ds(pl.multiple_of(i * wq, HEAD_SIZE), wq), :] = tn(normed_ref[:, lanes], pre_grad_ref[...]).astype(BF)
        out_grad_ref[:, lanes] = tn(mixed_ref[...], branch_ref[:, lanes]).astype(BF)


def backward_call(
    second_grad, cotangent, gain_one, gain_two, logsum, cosine, sine, ids, hidden, tokens, normed, w, out, qkv, mixed
):
    seqs = lax.axis_size("seq")
    length, model = tokens.shape
    rows = length // seqs
    wide = w.shape[1]
    wq = mixed.shape[1]
    vmem, hbm = pl.BlockSpec(memory_space=pltpu.VMEM), pl.BlockSpec(memory_space=pl.ANY)
    shape, dma = jax.ShapeDtypeStruct, pltpu.SemaphoreType.DMA
    held = pltpu.VMEM((PIECES, rows // PIECES, model), BF)
    return pl.pallas_call(
        backward_kernel,
        out_shape=(
            shape((length, model), BF),
            shape((rows, model), F32),
            shape((model, wide), BF),
            shape((wq, model), BF),
            shape((1, wide), F32),
            shape((1, model), F32),
            shape((1, model), F32),
        ),
        in_specs=[vmem] * 9 + [hbm] * 7,
        out_specs=(vmem,) * 7,
        scratch_shapes=[pltpu.VMEM((rows, model), F32)]
        + [pltpu.VMEM(field.shape, field.dtype) for field in (tokens, normed, w, out, qkv, mixed)]
        + [
            pltpu.VMEM((length, model), BF),
            pltpu.VMEM((length, wq), BF),
            pltpu.VMEM((length, wide), BF),
            pltpu.VMEM((length, HEAD_SIZE), F32),
            pltpu.VMEM((length, HEAD_SIZE), F32),
            held, held, held, held,
            dma((7,)), dma((3, PIECES)), dma((3, PIECES)), dma((4, PIECES)), dma((4, PIECES)),
        ],
        cost_estimate=pl.CostEstimate(flops=13 * 10**9, bytes_accessed=30 * 10**6, transcendentals=3 * 10**6),
        compiler_params=pltpu.CompilerParams(
            collective_id=2, has_side_effects=True, vmem_limit_bytes=62 * 2**20
        ),
        name="backward",
    )(
        second_grad, cotangent, gain_one[None], gain_two[None], logsum, cosine, sine,
        ids[None], ids[:, None], hidden, tokens, normed, w, out, qkv, mixed,
    )


TILE = 256


class ChipGather:
    def __init__(self, whole, columns, sems, seq, dpi, chips, own=None):
        self.whole, self.columns, self.sems, self.own = whole, columns, sems, own
        self.seq, self.dpi, self.chips = seq, dpi, chips
        self.chip, self.core = dpi // 2, dpi % 2

    def copy(self, kind, s, chip, core, to):
        block = self.whole.at[chip * 2 + core, :, self.columns]
        send, recv = self.sems
        src = block if s or self.own is None else self.own.at[:, self.columns]
        return remote(src, block, send.at[kind, s], recv.at[kind, s], (self.seq, to))

    def copies(self, s):
        z, c = self.chip, self.core
        low, high = z - s, z + s
        sibling = z * 2 + 1 - c
        out = [
            ((low >= 0) & (z < self.chips - 1), self.copy(0, s, low, c, self.dpi + 2)),
            ((high < self.chips) & (z > 0), self.copy(1, s, high, c, self.dpi - 2)),
            (low >= 0, self.copy(2, s, low, c, sibling)),
        ]
        if s > 0:
            out.append((high < self.chips, self.copy(3, s, high, c, sibling)))
        return out

    def send(self, s):
        for condition, copy in self.copies(s):
            pl.when(condition)(copy.start)

    def sent(self, s):
        for condition, copy in self.copies(s):
            pl.when(condition)(copy.wait_send)

    def came(self, s):
        z, c = self.chip, self.core
        pl.when(z - s >= 0)(self.copy(0, s - 1, z - s, c, self.dpi).wait_recv)
        pl.when(z + s < self.chips)(self.copy(1, s - 1, z + s, c, self.dpi).wait_recv)

    def came_across(self, s):
        z, c = self.chip, self.core
        pl.when(z - s >= 0)(self.copy(2, s, z - s, 1 - c, self.dpi).wait_recv)
        if s > 0:
            pl.when(z + s < self.chips)(self.copy(3, s, z + s, 1 - c, self.dpi).wait_recv)


class ChipScatter:
    def __init__(self, terms, got, held, sems, seq, dpi, chips):
        self.terms, self.got, self.held, self.sems = terms, got, held, sems
        self.seq, self.dpi, self.chips = seq, dpi, chips
        self.chip, self.core = dpi // 2, dpi % 2

    def give(self):
        send, recv = self.sems
        return remote(
            self.terms.at[:, 1 - self.core], self.got, send.at[2, 0], recv.at[2, 0], (self.seq, self.chip * 2 + 1 - self.core)
        )

    def up(self, d, to, field=None):
        send, recv = self.sems
        return remote((field or self.held).at[d], self.held.at[d], send.at[0, d], recv.at[0, d], (self.seq, to))

    def down(self, d, to, last, field=None):
        send, recv = self.sems
        slot = self.chips if last else d
        return remote((field or self.held).at[d], self.held.at[slot], send.at[1, d], recv.at[1, d], (self.seq, to))

    def each(self, body):
        size = self.got.shape[1]
        chunk = 16 if size % 16 == 0 else size

        @pl.loop(0, size // chunk)
        def _(i):
            body(pl.ds(pl.multiple_of(i * chunk, chunk), chunk))

    def take(self):
        self.give().wait()

        @pl.loop(0, self.chips)
        def _(d):
            def body(rows):
                own = self.terms[d, self.core, rows, :].astype(F32)
                self.got[d, rows, :] = (own + self.got[d, rows, :].astype(F32)).astype(BF)

            self.each(body)

    def add(self, d):
        def body(rows):
            total = self.got[d, rows, :].astype(F32) + self.held[d, rows, :].astype(F32)
            self.held[d, rows, :] = total.astype(BF)

        self.each(body)

    def step(self, r):
        z, chips = self.chip, self.chips

        @pl.when(z + r < chips)
        def _():
            d = z + r

            @pl.when(z > 0)
            def _():
                self.up(d, self.dpi).wait_recv()
                self.add(d)
                self.up(d, self.dpi + 2).start()

            @pl.when(z == 0)
            def _():
                self.up(d, self.dpi + 2, self.got).start()

        @pl.when(z - r >= 0)
        def _():
            d = z - r

            @pl.when(z < chips - 1)
            def _():
                self.down(d, self.dpi, False).wait_recv()
                self.add(d)
                self.down(d, self.dpi - 2, r == 1).start()

            @pl.when(z == chips - 1)
            def _():
                self.down(d, self.dpi - 2, r == 1, self.got).start()

    def finish(self, result):
        z, chips = self.chip, self.chips
        pl.when(z > 0)(lambda: self.up(z, self.dpi).wait_recv())
        pl.when(z < chips - 1)(lambda: self.down(z, self.dpi, True).wait_recv())

        def body(rows):
            total = self.got[z, rows, :].astype(F32)
            total += jnp.where(z > 0, self.held[z, rows, :].astype(F32), 0.0)
            result[rows, :] = total + jnp.where(z < chips - 1, self.held[chips, rows, :].astype(F32), 0.0)

        self.each(body)
        for r in range(1, chips):
            pl.when(z + r < chips)(lambda: self.up(z + r, self.dpi + 2).wait_send())
            pl.when(z - r >= 0)(lambda: self.down(z - r, self.dpi - 2, r == 1).wait_send())


def feed_kernel(
    second_ref, incoming_ref, first_hbm, own_ref,
    whole_out, out_hbm, grad_hbm, rest_hbm, mine_ref,
    second_turned_ref, incoming_turned_ref, w_ref, terms_ref, got_ref, held_ref, active_ref, both_ref, out_ref, grad_ref, stage_ref,
    load_sem, store_sem, stage_sem, own_sem, ahead_send, ahead_recv, sum_send, sum_recv,
    *, tiles, ready, summed,
):
    dps = lax.axis_size("dp")
    chips = dps // 2
    seq, dpi = lax.axis_index("seq"), lax.axis_index("dp")
    chip, core = dpi // 2, dpi % 2
    length, model = second_ref.shape
    width = 3 * TILE
    later = own_ref.shape[1] // width if ready < tiles else 0
    loose = ready >= chips + 2
    above, below = ((chip + 1) % chips) * 2 + core, ((chip + chips - 1) % chips) * 2 + core
    greet([(seq, above), (seq, below), (seq, chip * 2 + 1 - core)])

    def columns(t):
        return pl.ds(pl.multiple_of(t * width, width), width)

    def load(t, source=first_hbm):
        return pltpu.make_async_copy(source.at[:, :, columns(t)], w_ref.at[t % 2], load_sem.at[t % 2])

    def start_load(t):
        pl.when(t < ready)(lambda: load(t).start())
        if later > 0:
            first = columns(t - ready)
            ahead = pltpu.make_async_copy(whole_out.at[:, :, first], w_ref.at[t % 2], load_sem.at[t % 2])
            pl.when(within(t, ready, tiles))(ahead.start)

    def store(t):
        return pltpu.make_async_copy(
            terms_ref.at[t % 3], rest_hbm.at[:, :, :, columns(t - summed)], store_sem.at[t % 3]
        )

    def gather(q):
        return ChipGather(
            whole_out, columns(q), (ahead_send.at[q], ahead_recv.at[q]), seq, dpi, chips, own_ref
        )

    def scatter(t):
        return ChipScatter(
            terms_ref.at[t % 3], got_ref.at[t], held_ref.at[t], (sum_send.at[t], sum_recv.at[t]), seq, dpi, chips
        )

    def within(value, low, high):
        return (value >= low) & (value < high)

    load(0).start()
    own = pltpu.make_async_copy(own_ref, whole_out.at[dpi], own_sem)
    own.start()
    out_ref[...] = jnp.zeros_like(out_ref)
    grad_ref[...] = jnp.zeros_like(grad_ref)

    @pl.loop(0, length // TILE)
    def _(i):
        at = slot_rows(i, TILE)
        second_turned_ref[:, at] = second_ref[at, :].T
        incoming_turned_ref[:, at] = incoming_ref[at, :].T

    own.wait()
    far = list(range(chips - 1, 0, -1))
    thirds = [far[: -(-len(far) // 3)], far[-(-len(far) // 3) : -(-2 * len(far) // 3)], far[-(-2 * len(far) // 3) :]]

    @pl.loop(0, tiles)
    def _(t):
        def sent_at(tick):
            q = tick - tick // 3 if loose else tick
            return (tick >= 0) & (q < later) & ((tick % 3 != 2) if loose else True), q

        def pass_on(s):
            if later > 0:
                one, q = sent_at(t - s)

                @pl.when(one)
                def _():
                    gather(q).came(s)
                    gather(q).send(s)

        def sum_on(part):
            if part == 0:
                pl.when(within(t - 1, 0, summed))(lambda: scatter(t - 1).take())
            v = t - 1 - part
            j = v - v // 3

            @pl.when((v >= 0) & (v % 3 != 2) & (j < summed))
            def _():
                sums = scatter(j)
                if part == 3:
                    sums.finish(mine_ref.at[j])
                else:
                    for r in thirds[part]:
                        sums.step(r)

        if later > 0:
            one, q = sent_at(t)
            pl.when(one)(lambda: gather(q).send(0))
            arrived, q_last = sent_at(t - chips)

            @pl.when(arrived)
            def _():
                for s in range(chips):
                    gather(q_last).came_across(s)
                    gather(q_last).sent(s)

        start_load(t + 1)
        pltpu.make_async_copy(
            first_hbm.at[:, :, pl.ds(0, width)], w_ref.at[t % 2], load_sem.at[t % 2]
        ).wait()
        pl.when(t - 3 >= summed)(lambda: store(t - 3).wait())

        w = w_ref[t % 2].reshape(model, width)
        for i in range(2):
            at = slice(i * length // 2, (i + 1) * length // 2)
            both = nn(second_ref[at, :], w[:, : 2 * TILE])
            back = nn(incoming_ref[at, :], w[:, 2 * TILE :])
            gate, up = both[:, :TILE], both[:, TILE:]
            sigma = jax.nn.sigmoid(gate)
            silu = gate * sigma
            active_ref[at, :] = (silu * up).astype(BF)
            both_ref[at, :TILE] = (back * up * sigma * (1.0 + gate * (1.0 - sigma))).astype(BF)
            both_ref[at, TILE:] = (back * silu).astype(BF)
        pass_on(1)
        sum_on(0)
        rows = (chips, 2, model // dps)
        terms_ref[t % 3, :, :, :, : 2 * TILE] = nn(second_turned_ref[...], both_ref[...], BF).reshape(rows + (2 * TILE,))
        terms_ref[t % 3, :, :, :, 2 * TILE :] = nn(incoming_turned_ref[...], active_ref[...], BF).reshape(rows + (TILE,))
        pl.when(t < summed)(lambda: scatter(t).give().start())
        pl.when(t >= summed)(lambda: store(t).start())
        for s in range(2, chips - 1):
            pass_on(s)
        sum_on(1)
        for i in range(2):
            at = slice(i * length // 2, (i + 1) * length // 2)
            w = w_ref[t % 2].reshape(model, width)
            grad_ref[at, :] += nt(both_ref[at, :], w[:, : 2 * TILE])
            out_ref[at, :] += nt(active_ref[at, :], w[:, 2 * TILE :])
            if i == 0:
                sum_on(2)
        pass_on(chips - 1)
        sum_on(3)

    for j in range(summed):
        for part in range(4):
            if 1 + j + j // 2 + part >= tiles:
                if part == 3:
                    scatter(j).finish(mine_ref.at[j])
                else:
                    for r in thirds[part]:
                        scatter(j).step(r)
    for t in range(max(summed, tiles - 3), tiles):
        store(t).wait()
    quarter = length // 4
    stores = []
    for i in range(8):
        src, dst = (grad_ref, grad_hbm) if i < 4 else (out_ref, out_hbm)
        at = pl.ds((i % 4) * quarter, quarter)
        if i >= 2:
            stores[i - 2].wait()
        stage_ref[i % 2] = src[at, :].astype(BF)
        stores.append(pltpu.make_async_copy(stage_ref.at[i % 2], dst.at[at], stage_sem.at[i % 2]))
        stores[-1].start()
    for copy in stores[-2:]:
        copy.wait()


def feed_call(second, incoming, first, own, summed):
    dps, share, columns = first.shape
    chips = dps // 2
    length, model = second.shape
    width = 3 * TILE
    ready = columns // width
    tiles = ready + own.shape[1] // width
    if tiles == ready:
        own = jnp.zeros((share, 128), BF)
    vmem, hbm = pl.BlockSpec(memory_space=pltpu.VMEM), pl.BlockSpec(memory_space=pl.ANY)
    shape, dma = jax.ShapeDtypeStruct, pltpu.SemaphoreType.DMA
    return pl.pallas_call(
        functools.partial(feed_kernel, tiles=tiles, ready=ready, summed=summed),
        out_shape=(
            shape((dps,) + own.shape, BF),
            shape((length, model), BF),
            shape((length, model), BF),
            shape((chips, 2, share, (tiles - summed) * width), BF),
            shape((summed, share, width), F32),
        ),
        in_specs=[vmem, vmem, hbm, vmem],
        out_specs=(hbm, hbm, hbm, hbm, vmem),
        scratch_shapes=[
            pltpu.VMEM((model, length), BF),
            pltpu.VMEM((model, length), BF),
            pltpu.VMEM((2, dps, share, width), BF),
            pltpu.VMEM((3, chips, 2, share, width), BF),
            pltpu.VMEM((summed, chips, share, width), BF),
            pltpu.VMEM((summed, chips + 1, share, width), BF),
            pltpu.VMEM((length, TILE), BF),
            pltpu.VMEM((length, 2 * TILE), BF),
            pltpu.VMEM((length, model), F32),
            pltpu.VMEM((length, model), F32),
            pltpu.VMEM((2, length // 4, model), BF),
            dma((2,)), dma((3,)), dma((2,)), dma,
            dma((max(tiles - ready, 1), 4, chips)), dma((max(tiles - ready, 1), 4, chips)),
            dma((summed, 3, chips)), dma((summed, 3, chips)),
        ],
        cost_estimate=pl.CostEstimate(flops=65 * 10**9, bytes_accessed=60 * 10**6, transcendentals=3 * 10**6),
        compiler_params=pltpu.CompilerParams(
            collective_id=4, has_side_effects=True, vmem_limit_bytes=63 * 2**20
        ),
        name="feed_forward",
    )(second, incoming, first, own)


def pack_kernel(gate_ref, up_ref, down_ref, first_ref, rest_ref):
    units = gate_ref.shape[1]
    split = first_ref.shape[1] // (3 * TILE)
    for t in range(-(-units // TILE)):
        size = min(TILE, units - t * TILE)
        ref, at = (first_ref, t) if t < split else (rest_ref, t - split)
        lanes = slice(t * TILE, t * TILE + size)
        for i, part in enumerate((gate_ref[:, lanes], up_ref[:, lanes], down_ref[:, lanes])):
            low = (3 * at + i) * TILE
            ref[:, low : low + size] = part
            if size < TILE:
                ref[:, low + size : low + TILE] = jnp.zeros((part.shape[0], TILE - size), BF)


def pack_call(gate, up, down, ready):
    rows, units = gate.shape
    tiles = -(-units // TILE)
    vmem = pl.BlockSpec(memory_space=pltpu.VMEM)
    width = 3 * TILE
    return pl.pallas_call(
        pack_kernel,
        out_shape=[
            jax.ShapeDtypeStruct((rows, ready * width), BF),
            jax.ShapeDtypeStruct((rows, max(tiles - ready, 1) * width), BF),
        ],
        in_specs=[vmem] * 3,
        out_specs=[vmem] * 2,
        cost_estimate=pl.CostEstimate(flops=0, bytes_accessed=10**7, transcendentals=0),
        compiler_params=pltpu.CompilerParams(vmem_limit_bytes=32 * 2**20),
        name="pack_weights",
    )(gate, up, down)


def unpack_kernel(summed_ref, rest_ref, *refs):
    count = len(refs) // 2 - 1
    gate_ref, up_ref, down_ref = refs[count : count + 3]
    for src, dst in zip(refs[:count], refs[count + 3 :]):
        dst[...] = src[...]
    units = gate_ref.shape[1]
    split = summed_ref.shape[0]
    for t in range(-(-units // TILE)):
        size = min(TILE, units - t * TILE)
        lanes = slice(t * TILE, t * TILE + size)
        for i in range(3):
            if t < split:
                part = summed_ref[t, :, i * TILE : i * TILE + size]
            else:
                low = (3 * (t - split) + i) * TILE
                part = rest_ref[:, low : low + size].astype(F32)
            (gate_ref, up_ref, down_ref)[i][:, lanes] = part


def unpack_call(summed, rest, units, *given):
    rows = rest.shape[0]
    vmem = pl.BlockSpec(memory_space=pltpu.VMEM)
    return pl.pallas_call(
        unpack_kernel,
        out_shape=[jax.ShapeDtypeStruct((rows, units), F32)] * 3
        + [jax.ShapeDtypeStruct(field.shape, field.dtype) for field in given],
        in_specs=[vmem] * (2 + len(given)),
        out_specs=[vmem] * (3 + len(given)),
        cost_estimate=pl.CostEstimate(flops=0, bytes_accessed=10**7, transcendentals=0),
        compiler_params=pltpu.CompilerParams(vmem_limit_bytes=32 * 2**20),
        name="unpack_gradients",
    )(summed, rest, *given)


def end_kernel(
    normed_grad_ref, hidden_grad_ref, x_ref, gain_ref, qkv_ref, out_ref, small_ref, feed_ref, hidden_hbm,
    input_grad_ref, qkv_out_ref, out_out_ref, small_out_ref, layer_out_ref,
    qkv_got_ref, out_got_ref, small_got_ref,
    qkv_move_ref, out_move_ref, small_move_ref, qkv_came_ref, out_came_ref, small_came_ref,
    came_ref, sums_ref, one_ref, two_ref, came2_ref, sums2_ref, one2_ref, two2_ref, hidden_ref,
    sum_send, sum_recv, sum2_send, sum2_recv, load_sem, core_send, core_recv, ring_send, ring_recv, seq_send, seq_recv,
):
    seqs, dps = lax.axis_size("seq"), lax.axis_size("dp")
    chips = dps // 2
    seq, dpi = lax.axis_index("seq"), lax.axis_index("dp")
    chip, core = dpi // 2, dpi % 2
    ahead = ((chip + 1) % chips) * 2 + core
    behind = ((chip + chips - 1) % chips) * 2 + core
    sibling = chip * 2 + 1 - core
    greet([(seq ^ k, dpi) for k in range(1, seqs)] + [(seq, other) for other in (ahead, behind, sibling)])
    rows = x_ref.shape[0]
    piece = rows // PIECES

    cores = [
        remote(src.at[..., 1 - core, :, :], dst, core_send.at[i], core_recv.at[i], (seq, sibling))
        for i, (src, dst) in enumerate(
            ((qkv_ref, qkv_got_ref), (out_ref, out_got_ref), (small_ref, small_got_ref))
        )
    ]
    for copy in cores:
        copy.start()
    total = SeqSum(normed_grad_ref, rows, came_ref, sums_ref, one_ref, two_ref, (sum_send, sum_recv), dpi, seq)
    total.begin()
    feed = SeqSum(feed_ref, rows, came2_ref, sums2_ref, one2_ref, two2_ref, (sum2_send, sum2_recv), dpi, seq)
    load = pltpu.make_async_copy(hidden_hbm.at[slot_rows(seq, rows)], hidden_ref, load_sem)
    load.start()
    for copy in cores:
        copy.wait_recv()

    def term(which, step):
        parts = [
            qkv_ref[:, which, core].astype(F32) + qkv_got_ref[:, which].astype(F32),
            out_ref[which, core].astype(F32) + out_got_ref[which].astype(F32),
            small_ref[which, core].astype(F32) + small_got_ref[which].astype(F32),
        ]
        if step > 0:
            came = (qkv_came_ref, out_came_ref, small_came_ref)
            parts = [part + field[step - 1].astype(F32) for part, field in zip(parts, came)]
        return parts

    def ring(step):
        return [
            remote(src.at[step], dst.at[step], ring_send.at[i, step], ring_recv.at[i, step], (seq, ahead))
            for i, (src, dst) in enumerate(
                ((qkv_move_ref, qkv_came_ref), (out_move_ref, out_came_ref), (small_move_ref, small_came_ref))
            )
        ]

    def input_piece(c):
        at = pl.ds(c * piece, piece)
        x = x_ref[at, :].astype(F32)
        factor = lax.rsqrt(jnp.mean(x * x, axis=-1, keepdims=True) + EPS)
        unit = x * factor
        scaled = total.take(c) * gain_ref[...]
        grad = scaled - unit * jnp.mean(scaled * unit, axis=-1, keepdims=True)
        input_grad_ref[at, :] = (hidden_grad_ref[at, :] + factor * grad).astype(BF)

    for step in range(chips - 1):
        if step > 0:
            for copy in ring(step - 1):
                copy.wait_recv()
        for field, part in zip((qkv_move_ref, out_move_ref, small_move_ref), term((chip + chips - 1 - step) % chips, step)):
            field[step] = part.astype(BF)
        for copy in ring(step):
            copy.start()
        if step == 0:
            total.middle()
            feed.begin()
        if step == 1:
            for c in range(PIECES):
                input_piece(c)
            feed.middle()
    load.wait()
    for c in range(PIECES):
        at = pl.ds(c * piece, piece)
        layer_out_ref[at, :] = (hidden_ref[at, :] + feed.take(c)).astype(BF)
    for copy in ring(chips - 2):
        copy.wait_recv()
    qkv, out, small = term(chip, chips - 1)
    out_out_ref[...] = out
    qkv_move_ref[chips - 1] = qkv.astype(BF)
    small_move_ref[chips - 1] = small.astype(BF)
    last = [
        remote(
            src, dst.at[seq], seq_send.at[i, k], seq_recv.at[i, k], (seq ^ k, dpi)
        )
        for k in range(1, seqs)
        for i, (src, dst) in enumerate(
            ((qkv_move_ref.at[chips - 1, seq ^ k], qkv_out_ref), (small_move_ref.at[chips - 1], small_out_ref))
        )
    ]
    for copy in last:
        copy.start()
    qkv_out_ref[seq] = qkv_move_ref[chips - 1, seq]
    small_out_ref[seq] = small_move_ref[chips - 1]
    total.finish()
    feed.finish()
    for copy in cores + [copy for step in range(chips - 1) for copy in ring(step)]:
        copy.wait_send()
    for copy in last:
        copy.wait()


def end_call(normed_grad, hidden_grad, x, gain, qkv, out, small, feed, hidden):
    seqs, chips, _, share, wide = qkv.shape
    rows, model = x.shape
    vmem = pl.BlockSpec(memory_space=pltpu.VMEM)
    shape, dma = jax.ShapeDtypeStruct, pltpu.SemaphoreType.DMA
    held = pltpu.VMEM((PIECES, rows // PIECES, model), BF)
    blocks = ((seqs, share, wide), (share, model), small.shape[2:])
    return pl.pallas_call(
        end_kernel,
        out_shape=(
            shape((rows, model), BF),
            shape(blocks[0], BF),
            shape(blocks[1], F32),
            shape((seqs,) + blocks[2], BF),
            shape((rows, model), BF),
        ),
        in_specs=[vmem] * 8 + [pl.BlockSpec(memory_space=pl.ANY)],
        out_specs=(vmem,) * 5,
        scratch_shapes=[
            pltpu.VMEM((seqs, chips, share, wide), BF),
            pltpu.VMEM((chips, share, model), BF),
            pltpu.VMEM((chips,) + blocks[2], BF),
        ]
        + [pltpu.VMEM((chips,) + block, BF) for block in blocks]
        + [pltpu.VMEM((chips - 1,) + block, BF) for block in blocks]
        + [
            held, held, held, held, held, held, held, held, pltpu.VMEM((rows, model), F32),
            dma((3, PIECES)), dma((3, PIECES)), dma((3, PIECES)), dma((3, PIECES)), dma, dma((3,)), dma((3,)),
            dma((3, chips)), dma((3, chips)), dma((2, seqs)), dma((2, seqs)),
        ],
        cost_estimate=pl.CostEstimate(flops=10**8, bytes_accessed=2 * 10**7, transcendentals=0),
        compiler_params=pltpu.CompilerParams(
            collective_id=3, has_side_effects=True, vmem_limit_bytes=48 * 2**20
        ),
        name="end_sums",
    )(normed_grad, hidden_grad, x, gain[None], qkv, out, small, feed, hidden)


def pair_tiles(left, right):
    units = left.shape[1]
    cuts = list(range(0, units, TILE)) + [units]
    return jnp.concatenate(
        [field[:, low:high] for low, high in zip(cuts[:-1], cuts[1:]) for field in (left, right)], axis=1
    )


def split_tiles(both):
    units = both.shape[1] // 2
    cuts = list(range(0, units, TILE)) + [units]
    spans = list(zip(cuts[:-1], cuts[1:]))
    return (
        jnp.concatenate([both[:, 2 * low : low + high] for low, high in spans], axis=1),
        jnp.concatenate([both[:, low + high : 2 * high] for low, high in spans], axis=1),
    )


def shards(
    inputs,
    block_ids,
    cotangent,
    first_gain,
    query_weight,
    query_bias,
    key_weight,
    key_bias,
    value_weight,
    value_bias,
    output_weight,
    second_gain,
    gate_weight,
    up_weight,
    down_weight,
):
    seqs = lax.axis_size("seq")
    seq = lax.axis_index("seq")
    dps = lax.axis_size("dp")
    dpi = lax.axis_index("dp")
    chips, chip, core = dps // 2, dpi // 2, dpi % 2
    heads = H // seqs
    copies = seqs // KEY_VALUE_HEADS
    wq = heads * HEAD_SIZE
    wide = wq + 2 * HEAD_SIZE
    tokens_here, model = inputs.shape[1:]
    share = first_gain.shape[0]
    kv_share = key_bias.shape[0]
    hidden_units = gate_weight.shape[1]

    small = jnp.concatenate([first_gain, second_gain, query_bias, key_bias, value_bias])
    packed = jnp.concatenate(
        [
            query_weight.reshape(share, seqs, wq),
            jnp.repeat(key_weight.reshape(share, KEY_VALUE_HEADS, HEAD_SIZE), copies, axis=1),
            jnp.repeat(value_weight.reshape(share, KEY_VALUE_HEADS, HEAD_SIZE), copies, axis=1),
        ],
        axis=-1,
    ).transpose(1, 0, 2)
    one = small.shape[0]
    small = jnp.pad(small[None], ((0, 15), (0, -one % 128)))
    tiles = -(-hidden_units // TILE)
    ready = READY if chips <= 4 else tiles
    first, later = pack_call(gate_weight, up_weight, down_weight.T, ready)
    later = later if ready < tiles else later[:, :0]
    first = lax.all_gather(first, "dp", axis=0, tiled=True).reshape(dps, model // dps, -1)
    tokens, incoming, blocks, smalls, weight_qkv, weight_out = start_call(
        inputs[0], cotangent[0], block_ids.reshape(-1, 128), small, packed, output_weight
    )
    blocks = blocks.reshape(-1)
    weight_qkv = weight_qkv.reshape(model, wide)
    smalls = smalls[:, :, 0, :one].transpose(1, 0, 2).astype(F32)
    gain_first = smalls[:, :, :share].reshape(model)
    gain_second = smalls[:, :, share : 2 * share].reshape(model)
    bias_q = lax.dynamic_index_in_dim(smalls, seq, 0, keepdims=False)[:, 2 * share : 3 * share].reshape(wq)
    group = seq // copies
    bias_k = smalls[:, :, 3 * share : 3 * share + kv_share].reshape(KEY_VALUE_HEADS, HEAD_SIZE)
    bias_v = smalls[:, :, 3 * share + kv_share :].reshape(KEY_VALUE_HEADS, HEAD_SIZE)
    bias = jnp.concatenate(
        [
            bias_q,
            lax.dynamic_index_in_dim(bias_k, group, 0, keepdims=False),
            lax.dynamic_index_in_dim(bias_v, group, 0, keepdims=False),
        ]
    )
    length = tokens.shape[0]
    cosine, sine = rope_tables(length)

    normed, qkv, mixed, logsum, hidden, second = attend_call(
        tokens, weight_qkv, bias[None], cosine, sine, blocks, gain_first, gain_second, weight_out.reshape(model, model)
    )
    second, weight_out = lax.optimization_barrier((second, weight_out))
    out_head = weight_out[0].reshape(dps * share, model)
    second, out_head = lax.optimization_barrier((second, out_head))
    _, out_sum, second_sum, rest, summed = feed_call(second, incoming, first, later, SUMMED)
    rest = rest.reshape(model, -1)
    rest = lax.psum_scatter(rest, "dp", scatter_dimension=0, tiled=True)
    normed_grad, grad_hidden, qkv_grad, out_weight_grad, bias_grad, gain_one_grad, gain_two_grad = backward_call(
        second_sum, cotangent[0], gain_first, gain_second, logsum, cosine, sine, blocks,
        hidden, tokens, normed, weight_qkv, out_head, qkv, mixed,
    )
    bias_grad, gain_one_grad, gain_two_grad = bias_grad[0], gain_one_grad[0], gain_two_grad[0]

    place = lambda field, count, at: jnp.where(
        (jnp.arange(count) == at)[:, None], field[None], 0.0
    ).reshape(seqs, dps, -1)
    small_grad = jnp.concatenate(
        [
            gain_one_grad.reshape(seqs, dps, share),
            gain_two_grad.reshape(seqs, dps, share),
            place(bias_grad[:wq], seqs, seq),
            place(bias_grad[wq : wq + HEAD_SIZE], KEY_VALUE_HEADS, group),
            place(bias_grad[wq + HEAD_SIZE :], KEY_VALUE_HEADS, group),
        ],
        axis=-1,
    )
    small_rows = -(-seqs * one // wide)
    small_grad = small_grad.transpose(1, 0, 2).reshape(dps, seqs * one).astype(BF)
    small_grad = jnp.pad(small_grad, ((0, 0), (0, small_rows * wide - seqs * one)))
    small_grad = jnp.pad(small_grad.reshape(dps, -1, wide), ((0, 0), (0, 16 - small_rows), (0, 0)))
    input_grad, parts, out_weight_grad, smalls, layer_out = end_call(
        normed_grad, grad_hidden, inputs[0], gain_first,
        qkv_grad.reshape(seqs, chips, 2, share, wide),
        out_weight_grad.reshape(chips, 2, share, model),
        small_grad.reshape(chips, 2, 16, wide),
        out_sum, hidden,
    )
    smalls = smalls[:, :small_rows].reshape(seqs, -1)[:, : seqs * one].reshape(seqs, seqs, one)
    small_sum = jnp.sum(
        lax.dynamic_index_in_dim(smalls, seq, 1, keepdims=False).astype(F32), axis=0
    )
    query_weight_grad = jnp.concatenate([part[:share, :wq] for part in parts], axis=1).astype(F32)
    pairs = [
        sum(part[:share, wq:].astype(F32) for part in parts[g * copies : (g + 1) * copies])
        for g in range(KEY_VALUE_HEADS)
    ]
    key_weight_grad = jnp.concatenate([pair[:, :HEAD_SIZE] for pair in pairs], axis=1)
    value_weight_grad = jnp.concatenate([pair[:, HEAD_SIZE:] for pair in pairs], axis=1)
    gain_one_grad, gain_two_grad, query_bias_grad, key_bias_grad, value_bias_grad = jnp.split(
        small_sum, [share, 2 * share, 3 * share, 3 * share + kv_share]
    )

    gate_grad, up_grad, down_grad, layer_out, input_grad, out_weight_grad = unpack_call(
        summed, rest, hidden_units, layer_out, input_grad, out_weight_grad
    )
    return (
        layer_out[None],
        input_grad[None],
        gain_one_grad,
        query_weight_grad,
        query_bias_grad,
        key_weight_grad,
        key_bias_grad,
        value_weight_grad,
        value_bias_grad,
        out_weight_grad,
        gain_two_grad,
        gate_grad,
        up_grad,
        down_grad.T,
    )


def solution(mesh):
    tokens = P("dp", "seq", None)
    whole = P(("seq", "dp"))
    matrix = P(("seq", "dp"), None)
    feed = P("dp", "seq")
    in_specs = (
        tokens,
        P("dp", "seq"),
        tokens,
        whole,
        matrix,
        whole,
        matrix,
        whole,
        matrix,
        whole,
        matrix,
        whole,
        feed,
        feed,
        P("seq", "dp"),
    )
    out_specs = (
        tokens,
        tokens,
        whole,
        matrix,
        whole,
        matrix,
        whole,
        matrix,
        whole,
        matrix,
        whole,
        feed,
        feed,
        P("seq", "dp"),
    )
    return jax.shard_map(shards, mesh=mesh, in_specs=in_specs, out_specs=out_specs, check_vma=False)
```
